512 devices in a mesh: bins: 128 (over z, y_lo, x), lat: 4 (over y_hi, core).
Axes of the slice: x: 4, y: 4 (y_hi: 2, y_lo: 2; y = y_hi * 2 + y_lo), z: 16, core: 2. Of those that a mesh axis runs over, the one named last changes fastest.
Arguments:
- spectrum: float32 [1152, 64, 384], P('bins', 'lat'), may hold values from 0.05 to 2
- sea_mask: int32 [64, 384], P('lat'), may hold values 0 or 1
- current: float32 [768, 128], P('bins', 'lat'), may hold values from -0.6 to 0.6
- partner_plus: int32 [1152], replicated, may hold values from 0 to 1151
- partner_minus: int32 [1152], replicated, may hold values from 0 to 1151
- source_map: int32 [768, 128], P('bins', 'lat'), may hold values from 0 to 8
Outputs:
- spectrum_out: float32 [1152, 64, 384], P('bins', 'lat')
- stokes: float32 [2, 64, 768, 128], P(None, None, 'bins', 'lat')
The draws below stay inside these ranges and needn't reach their ends.
All inputs are finite; a program needn't handle non-finite values. No bound on the sum of `sea_mask` on one device may be relied on, other than what follows from the above.
Results may differ from the reference program's by a relative error of at most 0.000086.
Values sent between devices are 32-bit elements; how exact they have to be, the bound alone decides.
No kernel may reach another device: no remote copies, remote signals or barrier semaphores. Data moves between devices by JAX's collectives and lax.ppermute only.
A program may use at most 64 MiB of HBM per device.

```python
import math
import jax
import jax.numpy as jnp
from jax import lax

NDIR = 36
NFREQ = 32
LEV = 64
NLON = 384
BINS = 1152
NLAT = 64


def with_ends(values, key, low, top_value):
    extent = values.shape
    index_at = [jax.random.randint(jax.random.fold_in(key, axis), (), 0, extent[axis]) for axis in range(len(extent))]
    values = values.at[tuple(index_at)].set(low)
    longest = extent.index(max(extent))
    index_at[longest] = (index_at[longest] + 1) % extent[longest]
    return values.at[tuple(index_at)].set(top_value)


def block_levels(key, shape, split, low, high):
    gain = 1.0
    for axis_at, shards_of in split:
        heights = jax.random.uniform(jax.random.fold_in(jax.random.fold_in(key, 6), axis_at), (shards_of,), jnp.float32, low / len(split), high / len(split))
        gain = gain * jnp.repeat(jnp.exp(heights), shape[axis_at] // shards_of).reshape((-1,) + (1,) * (len(shape) - 1 - axis_at))
    return gain


def gaussian(key, dims, deviation, limit, cuts=(), held_as=jnp.bfloat16):
    values = deviation * jax.random.normal(key, dims, jnp.float32)
    if cuts:
        values = values * block_levels(key, dims, cuts, -0.22, 0.18)
    return jnp.clip(values, -limit, limit).astype(held_as)


def setup_inputs(seed: int = 0) -> dict:
    keys = jax.random.split(jax.random.key(seed), 7)
    return {
        "spectrum": jnp.clip(jnp.exp(math.log(2.0) - 3.6888794 * jax.random.uniform(keys[0], (BINS, NLAT, NLON), jnp.float32) ** block_levels(keys[0], (BINS, NLAT, NLON), ((0, 128), (1, 4)), -0.2, 0.2)), 0.05, 2.0),
        "sea_mask": with_ends((jax.random.randint(keys[1], (NLAT, NLON), 0, 5) < 4).astype(jnp.int32), jax.random.fold_in(keys[1], 1), 0, 1),
        "current": gaussian(keys[2], (2 * NLON, 2 * NLAT), 0.15, 0.6, ((0, 128), (1, 4)), jnp.float32),
        "partner_plus": with_ends(jax.random.randint(keys[3], (BINS,), 0, BINS), jax.random.fold_in(keys[3], 1), 0, BINS - 1).astype(jnp.int32),
        "partner_minus": with_ends(jax.random.randint(keys[4], (BINS,), 0, BINS), jax.random.fold_in(keys[4], 1), 0, BINS - 1).astype(jnp.int32),
        "source_map": with_ends(jax.random.randint(keys[5], (2 * NLON, 2 * NLAT), 0, 9), jax.random.fold_in(keys[5], 1), 0, 8).astype(jnp.int32),
    }


HIGHEST = lax.Precision.HIGHEST

def bin_tables():
    dir_index = jnp.arange(NDIR, dtype=jnp.float32)
    freq_index = jnp.arange(NFREQ, dtype=jnp.float32)
    angles = 2.0 * math.pi * (dir_index + 0.5) / NDIR
    speeds = 0.12 + 0.25 * (NFREQ - 1 - freq_index) / (NFREQ - 1)
    along_x = jnp.repeat(speeds, NDIR) * jnp.tile(jnp.cos(angles), NFREQ)
    along_y = jnp.repeat(speeds, NDIR) * jnp.tile(jnp.sin(angles), NFREQ)
    strength = jnp.repeat(0.06 * (1.0 + freq_index / (NFREQ - 1)), NDIR)
    levels = jnp.arange(LEV, dtype=jnp.float32) + 0.5
    wavenumber = 0.02 * jnp.power(1.15, freq_index)
    decay = jnp.repeat(jnp.exp(-levels[:, None] * wavenumber[None, :]), NDIR, axis=1)
    amplitude = 2.0 / math.sqrt(NDIR * NFREQ)
    cosines = jnp.tile(jnp.cos(angles), NFREQ)
    sines = jnp.tile(jnp.sin(angles), NFREQ)
    drift_table = amplitude * jnp.concatenate([decay * cosines[None, :], decay * sines[None, :]], axis=0)
    return (along_x, along_y, strength, drift_table)

def cell_means(current_cells):
    lon_count = current_cells.shape[0] // 2
    lat_count = current_cells.shape[1] // 2
    return current_cells.reshape(lon_count, 2, lat_count, 2).mean(axis=(1, 3))

def face_fluxes(padded, velocity, dimension):
    face_count = padded.shape[dimension] - 3

    def section(low_edge):
        return lax.slice_in_dim(padded, low_edge, low_edge + face_count, axis=dimension)
    left_value = (-section(0) + 5.0 * section(1) + 2.0 * section(2)) / 6.0
    right_value = (2.0 * section(1) + 5.0 * section(2) - section(3)) / 6.0
    return jnp.maximum(velocity, 0.0) * left_value + jnp.minimum(velocity, 0.0) * right_value

def transport(padded_rows, zonal_flow, along_x, along_y, sea_cells):
    row_count = padded_rows.shape[1] - 4
    spectra = padded_rows[:, 2:2 + row_count, :]
    padded_cols = jnp.pad(spectra, ((0, 0), (0, 0), (2, 2)))
    zonal_padded = jnp.pad(zonal_flow, ((0, 0), (1, 1)))
    face_zonal = 0.5 * (zonal_padded[:, :-1] + zonal_padded[:, 1:])
    speed_x = along_x[:, None, None] + face_zonal[None, :, :]
    flux_x = face_fluxes(padded_cols, speed_x, 2)
    flux_y = face_fluxes(padded_rows, along_y[:, None, None], 1)
    change = flux_x[:, :, 1:] - flux_x[:, :, :-1] + flux_y[:, 1:, :] - flux_y[:, :-1, :]
    return sea_cells[None, :, :] * (spectra - change)

def transport_all(spectra, zonal_flow, along_x, along_y, sea_cells):
    grouped = spectra.reshape(NFREQ, NDIR, NLAT, NLON)

    def one_bundle(entries):
        bundle, speed_x, speed_y = entries
        padded = jnp.pad(bundle, ((0, 0), (2, 2), (0, 0)))
        return transport(padded, zonal_flow, speed_x, speed_y, sea_cells)
    carried = lax.map(one_bundle, (grouped, along_x.reshape(NFREQ, NDIR), along_y.reshape(NFREQ, NDIR)))
    return carried.reshape(NDIR * NFREQ, NLAT, NLON)

def spread_to_ocean(rim, source_map):
    row_count = rim.shape[1] - 2
    col_count = rim.shape[2] - 2
    result = jnp.zeros((rim.shape[0], 2 * col_count, 2 * row_count), jnp.float32)
    for offset in range(9):
        row_shift = offset // 3 - 1
        col_shift = offset % 3 - 1
        shifted = rim[:, 1 + row_shift:1 + row_shift + row_count, 1 + col_shift:1 + col_shift + col_count]
        shifted = jnp.swapaxes(shifted, 1, 2)
        shifted = jnp.repeat(jnp.repeat(shifted, 2, axis=1), 2, axis=2)
        result = result + jnp.where(source_map[None, :, :] == offset, shifted, jnp.float32(0.0))
    return result

def reference(spectrum, sea_mask, current, partner_plus, partner_minus, source_map):
    along_x, along_y, strength, drift_table = bin_tables()
    sea_cells = sea_mask.astype(jnp.float32)
    zonal_flow = cell_means(current).T
    masked = spectrum * sea_cells[None, :, :]
    after_first = transport_all(masked, zonal_flow, along_x, along_y, sea_cells)
    bin_count = NDIR * NFREQ
    flat_rows = after_first.reshape(bin_count, NLAT * NLON)
    plus_part = jnp.take(flat_rows, partner_plus, axis=0)
    minus_part = jnp.take(flat_rows, partner_minus, axis=0)
    source = strength[:, None] * (flat_rows * flat_rows * (plus_part + minus_part) - 2.0 * flat_rows * plus_part * minus_part)
    back = jax.ops.segment_sum(source, partner_plus, num_segments=bin_count) + jax.ops.segment_sum(source, partner_minus, num_segments=bin_count)
    middle = flat_rows + (source - 0.5 * back)
    drift_rows = jnp.dot(drift_table, middle, precision=HIGHEST).reshape(2 * LEV, NLAT, NLON)
    rim = jnp.pad(drift_rows, ((0, 0), (1, 1), (1, 1)))
    stokes = spread_to_ocean(rim, source_map).reshape(2, LEV, 2 * NLON, 2 * NLAT)
    second = transport_all(middle.reshape(bin_count, NLAT, NLON), zonal_flow, along_x, along_y, sea_cells)
    return (second, stokes)
```

```python
import math

import jax
import jax.numpy as jnp
import numpy as np
from jax import lax
from jax.experimental import pallas as pl
from jax.experimental.pallas import tpu as pltpu
from jax.sharding import PartitionSpec as P

NDIR = 36
NFREQ = 32
LEV = 64
BINS = NDIR * NFREQ
OWN = 9
ROWS = 16
NLON = 384
OWNERS = 128
COLS = 3
F32 = jnp.float32
BF16 = jnp.bfloat16
HIGHEST = lax.Precision.HIGHEST

GROUP_COLUMNS = (0, 1, 2, -2, -1, 3, 4)


def bin_values():
    j = np.arange(NFREQ, dtype=np.float64)
    angles = 2.0 * math.pi * (np.arange(NDIR) + 0.5) / NDIR
    speeds = np.repeat(0.12 + 0.25 * (NFREQ - 1 - j) / (NFREQ - 1), NDIR)
    cosines, sines = np.tile(np.cos(angles), NFREQ), np.tile(np.sin(angles), NFREQ)
    strength = np.repeat(0.06 * (1.0 + j / (NFREQ - 1)), NDIR)
    levels = np.arange(LEV) + 0.5
    decay = np.repeat(np.exp(-levels[:, None] * (0.02 * 1.15**j)[None, :]), NDIR, axis=1)
    drift = 2.0 / math.sqrt(BINS) * np.concatenate([decay * cosines, decay * sines], axis=0)
    return speeds * cosines, speeds * sines, strength, drift


def stencils():
    lane = {}
    for group, column in enumerate(GROUP_COLUMNS):
        for r in range(ROWS):
            lane[column, r] = 16 * group + r
    for column in range(COLS):
        for k, r in enumerate((-2, -1, 16, 17)):
            lane[column, r] = 112 + 4 * column + k
    table = np.zeros((128, 256), np.float32)
    for r in range(ROWS):
        for face in range(COLS + 1):
            at = 16 * face + r
            for d, w in ((-2, -1), (-1, 5), (0, 2)):
                table[lane[face + d, r], at] += w
            for d, w in ((-1, 2), (0, 5), (1, -1)):
                table[lane[face + d, r], 128 + at] += w
        for column in range(COLS):
            at = 64 + 16 * column + r
            for d, w in ((-2, 1), (-1, -6), (0, 3), (1, 2)):
                table[lane[column, r + d], at] += w
            for d, w in ((-1, -2), (0, -3), (1, 6), (2, -1)):
                table[lane[column, r + d], 128 + at] += w
    return table


def lanes(rows=1):
    return lax.broadcasted_iota(jnp.int32, (rows, 128), 1)


def split_beside(x):
    upper = x.astype(BF16).astype(F32)
    return (upper + pltpu.roll(x - upper, 64, 1)).astype(BF16)


def pack_kernel(spec, mask, low, high, current, out, mask_out, zonal_out, stack, turned, turned2):
    sea = mask[...].astype(F32)
    masked = spec[...] * sea[None]
    stack[...] = jnp.zeros_like(stack)
    stack[0:16, :] = masked[8]
    stack[16:32, :] = sea
    for i in range(OWN):
        stack[32 + 4 * i : 34 + 4 * i, :] = low[2 * i : 2 * i + 2, :]
        stack[34 + 4 * i : 36 + 4 * i, :] = high[2 * i : 2 * i + 2, :]
    for ref in (turned, turned2):
        ref[0:8, :] = jnp.zeros((8, 128), F32)
        ref[392:400, :] = jnp.zeros((8, 128), F32)
    turned[8:392, :] = masked[0:8].reshape(128, NLON).T
    turned2[8:392, :] = stack[...].T

    pair = lax.broadcasted_iota(jnp.int32, (32, 128), 0) // 2
    means = jnp.where(pair == lax.broadcasted_iota(jnp.int32, (32, 128), 1) % 16, 0.25, 0.0)
    sums = jnp.dot(current[...], means, precision=HIGHEST, preferred_element_type=F32)
    zonal = [sums[2 * c : 2 * c + 1] + sums[2 * c + 1 : 2 * c + 2] for c in range(COLS)]
    zonal_out[...] = jnp.concatenate(zonal + [jnp.zeros((5, 128), F32)], axis=0)

    lane = lanes(OWNERS)
    group = lane // 16

    def column(ref, offset):
        return ref[pl.ds(8 + offset, OWNERS, stride=COLS), :]

    for i in range(OWN):
        source, at = (turned, 16 * i) if i < 8 else (turned2, 0)
        acc = jnp.zeros((OWNERS, 128), F32)
        for g, offset in enumerate(GROUP_COLUMNS):
            acc = jnp.where(group == g, pltpu.roll(column(source, offset), (16 * g - at) % 128, 1), acc)
        for c in range(COLS):
            beyond = pltpu.roll(column(turned2, c), (80 + 4 * c - 4 * i) % 128, 1)
            acc = jnp.where((lane >= 112 + 4 * c) & (lane < 116 + 4 * c), beyond, acc)
        if i < 8:
            flow = pltpu.roll(zonal[0] if i < 4 else zonal[2], (124 - 4 * (i % 4)) % 128, 1)
            acc = jnp.where(lane >= 124, jnp.broadcast_to(flow, acc.shape), acc)
        out[pl.ds(i, OWNERS, stride=OWN), :] = acc
    acc = jnp.zeros((OWNERS, 128), F32)
    for c in range(COLS):
        acc = jnp.where(group == c, pltpu.roll(column(turned2, c), (16 * c - 16) % 128, 1), acc)
    mask_out[...] = acc


def points_kernel(
    me, arrived, masks, zonal, plus, minus, speeds, stencil, table,
    out, drift_out, first, source, middle, halves, plus_col, minus_col,
):
    device = me[0]
    lane1 = lanes()
    below = jnp.zeros((1, 128), F32)
    above = jnp.zeros((1, 128), F32)
    left = jnp.maximum(device - 1, 0) * OWN + 4
    right = jnp.minimum(device + 1, OWNERS - 1) * OWN
    for k in range(4):
        here = (lane1 >= 4 * k) & (lane1 < 4 * k + 4)
        below = jnp.where(here, pltpu.roll(arrived[pl.ds(left + k, 1), :], 4 + 4 * k, 1), below)
        above = jnp.where(here, pltpu.roll(arrived[pl.ds(right + k, 1), :], 4 + 4 * k, 1), above)
    below = jnp.where(device > 0, below, 0.0)
    above = pltpu.roll(jnp.where(device < OWNERS - 1, above, 0.0), 48, 1)
    group1 = lane1 // 16
    columns = [zonal[c : c + 1, :] for c in range(COLS)]
    lower = below
    upper = above
    for c in range(COLS):
        lower = jnp.where(group1 == c + 1, columns[c], lower)
        upper = jnp.where(group1 == c, columns[c], upper)
    faces = jnp.where(lane1 < 64, 0.5 * (lower + upper), 0.0)
    sea = masks[pl.ds(device, 1), :]

    def chunk(t):
        return slice(128 * t, 128 * t + 128)

    for t in range(OWN):
        value = arrived[chunk(t), :]
        upper_half = value.astype(BF16)
        lower_half = (value - upper_half.astype(F32)).astype(BF16)
        sums = jnp.dot(upper_half, stencil[...], preferred_element_type=F32) + jnp.dot(
            lower_half, stencil[...], preferred_element_type=F32
        )
        speed = (speeds[chunk(t), :] + faces) * (1.0 / 6.0)
        flux = jnp.maximum(speed, 0.0) * sums[:, 0:128] + jnp.minimum(speed, 0.0) * sums[:, 128:256]
        change = (pltpu.roll(flux, 112, 1) - flux) + pltpu.roll(flux, 64, 1)
        moved = sea * (value - change)
        moved = jnp.where(lanes(128) < 48, moved, 0.0)
        first[chunk(t), :] = moved
        halves[chunk(t), :] = split_beside(moved)
        for row, col in ((plus, plus_col), (minus, minus_col)):
            part = jnp.broadcast_to(row[:, chunk(t)].astype(F32), (128, 128))
            col[chunk(t), :] = part.T

    numbers = lax.broadcasted_iota(jnp.int32, (128, BINS), 1).astype(F32)

    def gathered(col, t):
        wide = jnp.concatenate([col[chunk(t), :]] * OWN, axis=1)
        chosen = jnp.where(wide == numbers, 1.0, 0.0).astype(BF16)
        both = jnp.dot(chosen, halves[...], preferred_element_type=F32)
        return both + pltpu.roll(both, 64, 1)

    for t in range(OWN):
        ahead = gathered(plus_col, t)
        behind = gathered(minus_col, t)
        f = first[chunk(t), :]
        strength = jnp.broadcast_to(speeds[chunk(t), 127:128], (128, 128))
        source[chunk(t), :] = strength * (f * f * (ahead + behind) - 2.0 * f * ahead * behind)
    for t in range(OWN):
        halves[chunk(t), :] = split_beside(source[chunk(t), :])
    for t in range(OWN):
        names = lax.broadcasted_iota(jnp.int32, (128, BINS), 0) + 128 * t
        hits = jnp.where(plus[...] == names, 1.0, 0.0) + jnp.where(minus[...] == names, 1.0, 0.0)
        both = jnp.dot(hits.astype(BF16), halves[...], preferred_element_type=F32)
        back = both + pltpu.roll(both, 64, 1)
        m = first[chunk(t), :] + (source[chunk(t), :] - 0.5 * back)
        middle[chunk(t), :] = jnp.where(lanes(128) < 48, m, 0.0)
    for t in range(OWN):
        halves[chunk(t), :] = split_beside(middle[chunk(t), :])
    sums = jnp.dot(table[...], halves[...], preferred_element_type=F32)
    drift = sums[0:128] + pltpu.roll(sums[0:128], 64, 1) + sums[128:256]
    drift_out[...] = drift.T[0:48]

    group = lanes(OWNERS) // 16
    for c in range(COLS):
        acc = jnp.zeros((OWNERS, 128), F32)
        for i in range(8):
            part = pltpu.roll(middle[pl.ds(i, OWNERS, stride=OWN), :], (16 * (i - c)) % 128, 1)
            acc = jnp.where(group == i, part, acc)
        out[pl.ds(c, OWNERS, stride=4), :] = acc
    acc = jnp.zeros((OWNERS, 128), F32)
    last = middle[pl.ds(8, OWNERS, stride=OWN), :]
    for c in range(COLS):
        acc = jnp.where(group == 2 * c, pltpu.roll(last, 16 * c, 1), acc)
        acc = jnp.where(group == 2 * c + 1, jnp.broadcast_to(columns[c], acc.shape), acc)
    out[pl.ds(3, OWNERS, stride=4), :] = acc


def unpack_kernel(arrived, drift, drift_low, drift_high, middle, zonal, low, high, turned, turned2):
    for c in range(COLS):
        turned[pl.ds(c, OWNERS, stride=COLS), :] = arrived[pl.ds(c, OWNERS, stride=4), :]
        rest = arrived[pl.ds(3, OWNERS, stride=4), :]
        turned2[pl.ds(c, OWNERS, stride=COLS), :] = pltpu.roll(rest, (128 - 32 * c) % 128, 1)
    middle[0:128, :] = turned[...].T
    rest = turned2[...].T
    middle[128:144, :] = rest[0:16]
    zonal[...] = rest[16:32]
    for i in range(OWN):
        low[2 * i : 2 * i + 2, :] = middle[16 * i : 16 * i + 2, :]
        high[2 * i : 2 * i + 2, :] = middle[16 * i + 14 : 16 * i + 16, :]
    for ref, r in ((low, 0), (high, 15)):
        pieces = [drift_low[r : r + 1, :]] + [drift[16 * c + r : 16 * c + r + 1, :] for c in range(COLS)]
        pieces += [drift_high[r : r + 1, :], jnp.zeros((1, 128), F32)]
        ref[18:19, :] = jnp.concatenate(pieces[0:3], axis=1)
        ref[19:20, :] = jnp.concatenate(pieces[3:6], axis=1)
        ref[20:24, :] = jnp.zeros((4, NLON), F32)


def final_kernel(
    me, speeds, middle, zonal, low, high, mask, drift, drift_low, drift_high, place, out, stokes, rows, near
):
    first_bin = me[0] * OWN
    sea = mask[...].astype(F32)
    column = lax.broadcasted_iota(jnp.int32, (ROWS, NLON), 1)

    def beside(x, d):
        moved = pltpu.roll(x, (-d) % NLON, 1)
        return jnp.where((column + d >= 0) & (column + d < NLON), moved, 0.0)

    flow = zonal[...]
    lower_flow = 0.5 * (beside(flow, -1) + flow)
    upper_flow = 0.5 * (flow + beside(flow, 1))
    for i in range(OWN):
        f = middle[16 * i : 16 * i + 16, :]
        rows[8:24, :] = f
        rows[6:8, :] = low[2 * i : 2 * i + 2, :]
        rows[24:26, :] = high[2 * i : 2 * i + 2, :]
        along_x = speeds[first_bin + i]
        along_y = speeds[BINS + first_bin + i]
        r2, r1, u1, u2 = rows[6:22, :], rows[7:23, :], rows[9:25, :], rows[10:26, :]
        forward = jnp.maximum(along_y, 0.0) * (1.0 / 6.0)
        backward = jnp.minimum(along_y, 0.0) * (1.0 / 6.0)
        change = forward * ((r2 - 6.0 * r1) + (3.0 * f + 2.0 * u1)) + backward * (
            (6.0 * u1 - u2) - (2.0 * r1 + 3.0 * f)
        )
        a2, a1, b1, b2 = beside(f, -2), beside(f, -1), beside(f, 1), beside(f, 2)
        speed = (along_x + upper_flow) * (1.0 / 6.0)
        change = change + (
            jnp.maximum(speed, 0.0) * (5.0 * f + 2.0 * b1 - a1) + jnp.minimum(speed, 0.0) * (2.0 * f + 5.0 * b1 - b2)
        )
        speed = (along_x + lower_flow) * (1.0 / 6.0)
        change = change - (
            jnp.maximum(speed, 0.0) * (5.0 * a1 + 2.0 * f - a2) + jnp.minimum(speed, 0.0) * (2.0 * a1 + 5.0 * f - b1)
        )
        out[i] = sea * (f - change)

    near[...] = jnp.zeros_like(near)
    near[0:16, :] = drift_low[...]
    near[16:64, :] = drift[...]
    near[64:80, :] = drift_high[...]
    for ref, at in ((low, 80), (high, 88)):
        for k in range(5):
            near[at + k : at + k + 1, :] = ref[18 + k // 3 : 19 + k // 3, 128 * (k % 3) : 128 * (k % 3) + 128]
    wanted = jnp.broadcast_to(place[...], (128, 256)).T[0:192]
    chosen = jnp.where(wanted == lanes(192).astype(F32), 1.0, 0.0).astype(BF16)
    rest = near[...]
    total = jnp.zeros((192, 128), F32)
    for _ in range(3):
        part = rest.astype(BF16)
        rest = rest - part.astype(F32)
        total = total + jnp.dot(chosen, part, preferred_element_type=F32)
    stokes[0] = total[:, 0:64]
    stokes[1] = total[:, 64:128]


def shapes(*sizes):
    return [jax.ShapeDtypeStruct(size, F32) for size in sizes]


def on_device(spectrum, sea_mask, current, partner_plus, partner_minus, source_map):
    along_x, along_y, strength, drift_table = bin_values()
    speeds = np.zeros((BINS, 128), np.float32)
    speeds[:, 0:64] = along_x[:, None]
    speeds[:, 64:112] = along_y[:, None]
    speeds[:, 127] = strength
    speed_list = np.concatenate([along_x, along_y]).astype(np.float32)
    drift_upper = drift_table.astype(np.float32).astype(BF16)
    drift_lower = (drift_table.astype(np.float32) - drift_upper.astype(np.float32)).astype(BF16)
    table = np.concatenate([drift_upper, drift_lower], axis=0)
    stencil = stencils().astype(BF16)

    device = lax.axis_index("bins").reshape(1)
    bands = lax.axis_size("lat")
    up = [(i, i + 1) for i in range(bands - 1)]
    down = [(i + 1, i) for i in range(bands - 1)]
    east = [(i, i + 1) for i in range(OWNERS - 1)]
    west = [(i + 1, i) for i in range(OWNERS - 1)]

    def edge(start):
        rows = spectrum[:, start : start + 2] * sea_mask[None, start : start + 2].astype(F32)
        return rows.reshape(2 * OWN, NLON)

    from_below = lax.ppermute(edge(14), "lat", up)
    from_above = lax.ppermute(edge(0), "lat", down)

    smem = pl.BlockSpec(memory_space=pltpu.SMEM)
    vmem = pl.BlockSpec(memory_space=pltpu.VMEM)
    sent, masks, zonal = pl.pallas_call(
        pack_kernel,
        out_shape=shapes((BINS, 128), (OWNERS, 128), (8, 128)),
        scratch_shapes=[pltpu.VMEM((128, NLON), F32), pltpu.VMEM((400, 128), F32), pltpu.VMEM((400, 128), F32)],
    )(spectrum, sea_mask, from_below, from_above, current)

    arrived = lax.all_to_all(sent.reshape(OWNERS, 1, OWN * 128), "bins", 0, 0).reshape(BINS, 128)

    big = pltpu.VMEM((BINS, 128), F32)
    sent, drift = pl.pallas_call(
        points_kernel,
        out_shape=shapes((4 * OWNERS, 128), (48, 128)),
        in_specs=[smem] + [vmem] * 8,
        scratch_shapes=[big, big, big, pltpu.VMEM((BINS, 128), BF16), big, big],
        compiler_params=pltpu.CompilerParams(vmem_limit_bytes=40 * 1024 * 1024),
    )(
        device, arrived, masks, zonal, partner_plus.reshape(1, BINS), partner_minus.reshape(1, BINS),
        jnp.asarray(speeds), jnp.asarray(stencil), jnp.asarray(table),
    )

    arrived = lax.all_to_all(sent.reshape(OWNERS, 1, 512), "bins", 0, 0).reshape(4 * OWNERS, 128)
    drift_low = lax.ppermute(drift[32:48], "bins", east)
    drift_high = lax.ppermute(drift[0:16], "bins", west)

    middle, zonal_all, low, high = pl.pallas_call(
        unpack_kernel,
        out_shape=shapes((OWN * ROWS, NLON), (ROWS, NLON), (24, NLON), (24, NLON)),
        scratch_shapes=[pltpu.VMEM((NLON, 128), F32), pltpu.VMEM((NLON, 128), F32)],
    )(arrived, drift, drift_low, drift_high)
    from_below = lax.ppermute(high, "lat", up)
    from_above = lax.ppermute(low, "lat", down)

    row = jnp.arange(32, dtype=jnp.int32)[None, :] // 2 + source_map // 3 - 1
    col = jnp.arange(6, dtype=jnp.int32)[:, None] // 2 + source_map % 3
    place = jnp.where(row < 0, 80 + col, jnp.where(row > 15, 88 + col, 16 * col + row))
    place = jnp.pad(place.reshape(1, 192), ((0, 0), (0, 64))).astype(F32)
    second, stokes = pl.pallas_call(
        final_kernel,
        out_shape=shapes((OWN, ROWS, NLON), (2, 192, 64)),
        in_specs=[smem, smem] + [vmem] * 9,
        scratch_shapes=[pltpu.VMEM((32, NLON), F32), pltpu.VMEM((128, 128), F32)],
    )(
        device, jnp.asarray(speed_list), middle, zonal_all, from_below, from_above, sea_mask,
        drift, drift_low, drift_high, place,
    )
    return second, stokes.reshape(2, 6, 32, LEV).transpose(0, 3, 1, 2)


def solution(mesh):
    in_specs = (P("bins", "lat", None), P("lat", None), P("bins", "lat"), P(), P(), P("bins", "lat"))
    out_specs = (P("bins", "lat", None), P(None, None, "bins", "lat"))
    return jax.shard_map(on_device, mesh=mesh, in_specs=in_specs, out_specs=out_specs, check_vma=False)
```

```python
import math

import jax
import jax.numpy as jnp
import numpy as np
from jax import lax
from jax.experimental import pallas as pl
from jax.experimental.pallas import tpu as pltpu
from jax.sharding import PartitionSpec as P

NDIR = 36
NFREQ = 32
LEV = 64
BINS = NDIR * NFREQ
OWN = 9
ROWS = 16
NLON = 384
OWNERS = 128
COLS = 3
F32 = jnp.float32
BF16 = jnp.bfloat16
HIGHEST = lax.Precision.HIGHEST

GROUP_COLUMNS = (0, 1, 2, -2, -1, 3, 4)


def bin_values():
    j = np.arange(NFREQ, dtype=np.float64)
    angles = 2.0 * math.pi * (np.arange(NDIR) + 0.5) / NDIR
    speeds = np.repeat(0.12 + 0.25 * (NFREQ - 1 - j) / (NFREQ - 1), NDIR)
    cosines, sines = np.tile(np.cos(angles), NFREQ), np.tile(np.sin(angles), NFREQ)
    strength = np.repeat(0.06 * (1.0 + j / (NFREQ - 1)), NDIR)
    levels = np.arange(LEV) + 0.5
    decay = np.repeat(np.exp(-levels[:, None] * (0.02 * 1.15**j)[None, :]), NDIR, axis=1)
    drift = 2.0 / math.sqrt(BINS) * np.concatenate([decay * cosines, decay * sines], axis=0)
    return speeds * cosines, speeds * sines, strength, drift


def stencils():
    lane = {}
    for group, column in enumerate(GROUP_COLUMNS):
        for r in range(ROWS):
            lane[column, r] = 16 * group + r
    for column in range(COLS):
        for k in range(2):
            lane[column, k - 2] = 112 + 2 * column + k
            lane[column, 16 + k] = 118 + 2 * column + k
    table = np.zeros((128, 256), np.float32)
    for r in range(ROWS):
        for face in range(COLS + 1):
            at = 16 * face + r
            for d, w in ((-2, -1), (-1, 5), (0, 2)):
                table[lane[face + d, r], at] += w
            for d, w in ((-1, 2), (0, 5), (1, -1)):
                table[lane[face + d, r], 128 + at] += w
        for column in range(COLS):
            at = 64 + 16 * column + r
            for d, w in ((-2, 1), (-1, -6), (0, 3), (1, 2)):
                table[lane[column, r + d], at] += w
            for d, w in ((-1, -2), (0, -3), (1, 6), (2, -1)):
                table[lane[column, r + d], 128 + at] += w
    return table


def lanes(rows=1):
    return lax.broadcasted_iota(jnp.int32, (rows, 128), 1)


def split_beside(x):
    upper = x.astype(BF16).astype(F32)
    return (upper + pltpu.roll(x - upper, 64, 1)).astype(BF16)


def pack_kernel(spec, mask, current, out, mask_out, stack, turned, turned2):
    sea = mask[...].astype(F32)
    masked = spec[...] * sea[None]
    stack[0:16, :] = masked[8]
    stack[16:32, :] = sea
    stack[32:128, :] = jnp.zeros((96, NLON), F32)
    turned[...] = masked[0:8].reshape(128, NLON).T
    turned2[...] = stack[...].T

    pair = lax.broadcasted_iota(jnp.int32, (32, 128), 0) // 2
    means = jnp.where(pair == lax.broadcasted_iota(jnp.int32, (32, 128), 1) % 16, 0.25, 0.0)
    sums = jnp.dot(current[...], means, precision=HIGHEST, preferred_element_type=F32)
    group = lanes(OWNERS) // 16
    rest = jnp.zeros((OWNERS, 128), F32)
    sea_rows = jnp.zeros((OWNERS, 128), F32)
    for c in range(COLS):
        out[pl.ds(c, OWNERS, stride=4), :] = turned[pl.ds(c, OWNERS, stride=COLS), :]
        column = turned2[pl.ds(c, OWNERS, stride=COLS), :]
        zonal = sums[2 * c : 2 * c + 1] + sums[2 * c + 1 : 2 * c + 2]
        rest = jnp.where(group == 2 * c, pltpu.roll(column, 32 * c, 1), rest)
        rest = jnp.where(group == 2 * c + 1, jnp.broadcast_to(zonal, rest.shape), rest)
        sea_rows = jnp.where(group == c, pltpu.roll(column, (16 * c - 16) % 128, 1), sea_rows)
    out[pl.ds(3, OWNERS, stride=4), :] = rest
    mask_out[...] = sea_rows


def edges_kernel(arrived, to_east, to_west, to_above, to_below):
    def part(c):
        return arrived[pl.ds(c, OWNERS, stride=4), :]

    lane = lanes(OWNERS)
    group = lane // 16
    inside = lane % 16
    rest = part(3)
    for ref, c in ((to_east, 1), (to_west, 0)):
        ref[0:128, :] = part(c)
        ref[128:256, :] = part(c + 1)
        pair = jnp.where(
            group == 0, pltpu.roll(rest, (-32 * c) % 128, 1), pltpu.roll(rest, (16 - 32 * (c + 1)) % 128, 1)
        )
        last = jnp.zeros((32, 128), F32)
        for q in range(4):
            moved = pltpu.roll(pair[32 * q : 32 * q + 32], 32 * q, 1)
            last = jnp.where(group[0:32] // 2 == q, moved, last)
        ref[256:288, :] = last
    for ref, r in ((to_above, 14), (to_below, 0)):
        acc = jnp.zeros((OWNERS, 128), F32)
        for c in range(COLS):
            moved = pltpu.roll(part(c), (2 * c - r) % 128, 1)
            acc = jnp.where((inside >= 2 * c) & (inside < 2 * c + 2), moved, acc)
        for c in range(COLS):
            moved = pltpu.roll(rest, (6 + 2 * c - 32 * c - r) % 128, 1)
            acc = jnp.where((lane >= 6 + 2 * c) & (lane < 8 + 2 * c), moved, acc)
        ref[...] = acc


def points_kernel(
    me, arrived, from_west, from_east, from_below, from_above, masks, plus, minus, speeds, stencil, table,
    out, drift_out, first, source, middle, halves, plus_col, minus_col,
):
    device = me[0]
    lane = lanes(OWNERS)
    group = lane // 16

    flow = arrived[pl.ds(4 * device + 3, 1), :]
    below = arrived[pl.ds(4 * jnp.maximum(device - 1, 0) + 3, 1), :]
    above = arrived[pl.ds(4 * jnp.minimum(device + 1, OWNERS - 1) + 3, 1), :]
    lower = jnp.where(device > 0, pltpu.roll(below, 48, 1), 0.0)
    upper = jnp.where(device < OWNERS - 1, pltpu.roll(above, 32, 1), 0.0)
    lane1 = lanes()
    group1 = lane1 // 16
    for c in range(COLS):
        lower = jnp.where(group1 == c + 1, pltpu.roll(flow, (-16 * c) % 128, 1), lower)
        upper = jnp.where(group1 == c, pltpu.roll(flow, (-16 * (c + 1)) % 128, 1), upper)
    faces = jnp.where(lane1 < 64, 0.5 * (lower + upper), 0.0)
    sea = masks[pl.ds(device, 1), :]

    def chunk(t):
        return slice(128 * t, 128 * t + 128)

    for i in range(OWN):
        acc = jnp.zeros((OWNERS, 128), F32)
        for g in range(7):
            if i == 8:
                if g < 3:
                    part = pltpu.roll(arrived[pl.ds(3, OWNERS, stride=4), :], (-16 * g) % 128, 1)
                else:
                    ref, at = (from_west, 48) if g < 5 else (from_east, 80)
                    piece = ref[256:288, :]
                    part = jnp.concatenate([pltpu.roll(piece, (at - 32 * q) % 128, 1) for q in range(4)], axis=0)
            else:
                if g < 3:
                    part = arrived[pl.ds(g, OWNERS, stride=4), :]
                elif g < 5:
                    part = from_west[chunk(g - 3), :]
                else:
                    part = from_east[chunk(g - 5), :]
                part = pltpu.roll(part, (16 * g - 16 * i) % 128, 1)
            acc = jnp.where(group == g, part, acc)
        held = 16 * i if i < 8 else 6
        for ref, at in ((from_below, 112), (from_above, 118)):
            acc = jnp.where((lane >= at) & (lane < at + 6), pltpu.roll(ref[...], (at - held) % 128, 1), acc)
        middle[pl.ds(i, OWNERS, stride=OWN), :] = acc

    for t in range(OWN):
        value = middle[chunk(t), :]
        upper_half = value.astype(BF16)
        lower_half = (value - upper_half.astype(F32)).astype(BF16)
        sums = jnp.dot(upper_half, stencil[...], preferred_element_type=F32) + jnp.dot(
            lower_half, stencil[...], preferred_element_type=F32
        )
        speed = (speeds[chunk(t), :] + faces) * (1.0 / 6.0)
        flux = jnp.maximum(speed, 0.0) * sums[:, 0:128] + jnp.minimum(speed, 0.0) * sums[:, 128:256]
        change = (pltpu.roll(flux, 112, 1) - flux) + pltpu.roll(flux, 64, 1)
        moved = sea * (value - change)
        moved = jnp.where(lane < 48, moved, 0.0)
        first[chunk(t), :] = moved
        halves[chunk(t), :] = split_beside(moved)
        for row, col in ((plus, plus_col), (minus, minus_col)):
            part = jnp.broadcast_to(row[:, chunk(t)].astype(F32), (128, 128))
            col[chunk(t), :] = part.T

    numbers = lax.broadcasted_iota(jnp.int32, (128, BINS), 1).astype(F32)

    def gathered(col, t):
        wide = jnp.concatenate([col[chunk(t), :]] * OWN, axis=1)
        chosen = jnp.where(wide == numbers, 1.0, 0.0).astype(BF16)
        both = jnp.dot(chosen, halves[...], preferred_element_type=F32)
        return both + pltpu.roll(both, 64, 1)

    for t in range(OWN):
        ahead = gathered(plus_col, t)
        behind = gathered(minus_col, t)
        f = first[chunk(t), :]
        strength = jnp.broadcast_to(speeds[chunk(t), 127:128], (128, 128))
        source[chunk(t), :] = strength * (f * f * (ahead + behind) - 2.0 * f * ahead * behind)
    for t in range(OWN):
        halves[chunk(t), :] = split_beside(source[chunk(t), :])
    for t in range(OWN):
        names = lax.broadcasted_iota(jnp.int32, (128, BINS), 0) + 128 * t
        hits = jnp.where(plus[...] == names, 1.0, 0.0) + jnp.where(minus[...] == names, 1.0, 0.0)
        both = jnp.dot(hits.astype(BF16), halves[...], preferred_element_type=F32)
        back = both + pltpu.roll(both, 64, 1)
        m = first[chunk(t), :] + (source[chunk(t), :] - 0.5 * back)
        middle[chunk(t), :] = jnp.where(lane < 48, m, 0.0)
    for t in range(OWN):
        halves[chunk(t), :] = split_beside(middle[chunk(t), :])
    sums = jnp.dot(table[...], halves[...], preferred_element_type=F32)
    drift = sums[0:128] + pltpu.roll(sums[0:128], 64, 1) + sums[128:256]
    drift_out[...] = drift.T[0:48]

    for c in range(COLS):
        acc = jnp.zeros((OWNERS, 128), F32)
        for i in range(8):
            part = pltpu.roll(middle[pl.ds(i, OWNERS, stride=OWN), :], (16 * (i - c)) % 128, 1)
            acc = jnp.where(group == i, part, acc)
        out[pl.ds(c, OWNERS, stride=4), :] = acc
    acc = jnp.broadcast_to(flow, (OWNERS, 128))
    last = middle[pl.ds(8, OWNERS, stride=OWN), :]
    for c in range(COLS):
        acc = jnp.where(group == 2 * c, pltpu.roll(last, 16 * c, 1), acc)
    out[pl.ds(3, OWNERS, stride=4), :] = acc


def unpack_kernel(arrived, drift, drift_low, drift_high, middle, zonal, low, high, turned, turned2):
    for c in range(COLS):
        turned[pl.ds(c, OWNERS, stride=COLS), :] = arrived[pl.ds(c, OWNERS, stride=4), :]
        rest = arrived[pl.ds(3, OWNERS, stride=4), :]
        turned2[pl.ds(c, OWNERS, stride=COLS), :] = pltpu.roll(rest, (128 - 32 * c) % 128, 1)
    middle[0:128, :] = turned[...].T
    rest = turned2[...].T
    middle[128:144, :] = rest[0:16]
    zonal[...] = rest[16:32]
    for i in range(OWN):
        low[2 * i : 2 * i + 2, :] = middle[16 * i : 16 * i + 2, :]
        high[2 * i : 2 * i + 2, :] = middle[16 * i + 14 : 16 * i + 16, :]
    for ref, r in ((low, 0), (high, 15)):
        pieces = [drift_low[r : r + 1, :]] + [drift[16 * c + r : 16 * c + r + 1, :] for c in range(COLS)]
        pieces += [drift_high[r : r + 1, :], jnp.zeros((1, 128), F32)]
        ref[18:19, :] = jnp.concatenate(pieces[0:3], axis=1)
        ref[19:20, :] = jnp.concatenate(pieces[3:6], axis=1)
        ref[20:24, :] = jnp.zeros((4, NLON), F32)


def final_kernel(
    me, speeds, middle, zonal, low, high, mask, drift, drift_low, drift_high, place, out, stokes, rows, near
):
    first_bin = me[0] * OWN
    sea = mask[...].astype(F32)
    column = lax.broadcasted_iota(jnp.int32, (ROWS, NLON), 1)

    def beside(x, d):
        moved = pltpu.roll(x, (-d) % NLON, 1)
        return jnp.where((column + d >= 0) & (column + d < NLON), moved, 0.0)

    flow = zonal[...]
    lower_flow = 0.5 * (beside(flow, -1) + flow)
    upper_flow = 0.5 * (flow + beside(flow, 1))
    for i in range(OWN):
        f = middle[16 * i : 16 * i + 16, :]
        rows[8:24, :] = f
        rows[6:8, :] = low[2 * i : 2 * i + 2, :]
        rows[24:26, :] = high[2 * i : 2 * i + 2, :]
        along_x = speeds[first_bin + i]
        along_y = speeds[BINS + first_bin + i]
        r2, r1, u1, u2 = rows[6:22, :], rows[7:23, :], rows[9:25, :], rows[10:26, :]
        forward = jnp.maximum(along_y, 0.0) * (1.0 / 6.0)
        backward = jnp.minimum(along_y, 0.0) * (1.0 / 6.0)
        change = forward * ((r2 - 6.0 * r1) + (3.0 * f + 2.0 * u1)) + backward * (
            (6.0 * u1 - u2) - (2.0 * r1 + 3.0 * f)
        )
        a2, a1, b1, b2 = beside(f, -2), beside(f, -1), beside(f, 1), beside(f, 2)
        speed = (along_x + upper_flow) * (1.0 / 6.0)
        change = change + (
            jnp.maximum(speed, 0.0) * (5.0 * f + 2.0 * b1 - a1) + jnp.minimum(speed, 0.0) * (2.0 * f + 5.0 * b1 - b2)
        )
        speed = (along_x + lower_flow) * (1.0 / 6.0)
        change = change - (
            jnp.maximum(speed, 0.0) * (5.0 * a1 + 2.0 * f - a2) + jnp.minimum(speed, 0.0) * (2.0 * a1 + 5.0 * f - b1)
        )
        out[i] = sea * (f - change)

    near[...] = jnp.zeros_like(near)
    near[0:16, :] = drift_low[...]
    near[16:64, :] = drift[...]
    near[64:80, :] = drift_high[...]
    for ref, at in ((low, 80), (high, 88)):
        for k in range(5):
            near[at + k : at + k + 1, :] = ref[18 + k // 3 : 19 + k // 3, 128 * (k % 3) : 128 * (k % 3) + 128]
    wanted = jnp.broadcast_to(place[...], (128, 256)).T[0:192]
    chosen = jnp.where(wanted == lanes(192).astype(F32), 1.0, 0.0).astype(BF16)
    rest = near[...]
    total = jnp.zeros((192, 128), F32)
    for _ in range(3):
        part = rest.astype(BF16)
        rest = rest - part.astype(F32)
        total = total + jnp.dot(chosen, part, preferred_element_type=F32)
    stokes[0] = total[:, 0:64]
    stokes[1] = total[:, 64:128]


def shapes(*sizes):
    return [jax.ShapeDtypeStruct(size, F32) for size in sizes]


def on_device(spectrum, sea_mask, current, partner_plus, partner_minus, source_map):
    along_x, along_y, strength, drift_table = bin_values()
    speeds = np.zeros((BINS, 128), np.float32)
    speeds[:, 0:64] = along_x[:, None]
    speeds[:, 64:112] = along_y[:, None]
    speeds[:, 127] = strength
    speed_list = np.concatenate([along_x, along_y]).astype(np.float32)
    drift_upper = drift_table.astype(np.float32).astype(BF16)
    drift_lower = (drift_table.astype(np.float32) - drift_upper.astype(np.float32)).astype(BF16)
    table = np.concatenate([drift_upper, drift_lower], axis=0)
    stencil = stencils().astype(BF16)

    device = lax.axis_index("bins").reshape(1)
    bands = lax.axis_size("lat")
    up = [(i, i + 1) for i in range(bands - 1)]
    down = [(i + 1, i) for i in range(bands - 1)]
    east = [(i, i + 1) for i in range(OWNERS - 1)]
    west = [(i + 1, i) for i in range(OWNERS - 1)]

    smem = pl.BlockSpec(memory_space=pltpu.SMEM)
    vmem = pl.BlockSpec(memory_space=pltpu.VMEM)
    grant = pltpu.CompilerParams(vmem_limit_bytes=16 * 1024 * 1024)
    sent, masks = pl.pallas_call(
        pack_kernel,
        out_shape=shapes((4 * OWNERS, 128), (OWNERS, 128)),
        scratch_shapes=[pltpu.VMEM((128, NLON), F32), pltpu.VMEM((NLON, 128), F32), pltpu.VMEM((NLON, 128), F32)],
        compiler_params=grant,
    )(spectrum, sea_mask, current)

    arrived = lax.all_to_all(sent.reshape(OWNERS, 1, 512), "bins", 0, 0).reshape(4 * OWNERS, 128)
    to_east, to_west, to_above, to_below = pl.pallas_call(
        edges_kernel,
        out_shape=shapes((288, 128), (288, 128), (OWNERS, 128), (OWNERS, 128)),
        compiler_params=grant,
    )(arrived)
    from_west = lax.ppermute(to_east, "bins", east)
    from_east = lax.ppermute(to_west, "bins", west)
    from_below = lax.ppermute(to_above, "lat", up)
    from_above = lax.ppermute(to_below, "lat", down)

    big = pltpu.VMEM((BINS, 128), F32)
    sent, drift = pl.pallas_call(
        points_kernel,
        out_shape=shapes((4 * OWNERS, 128), (48, 128)),
        in_specs=[smem] + [vmem] * 11,
        scratch_shapes=[big, big, big, pltpu.VMEM((BINS, 128), BF16), big, big],
        compiler_params=pltpu.CompilerParams(vmem_limit_bytes=32 * 1024 * 1024),
    )(
        device, arrived, from_west, from_east, from_below, from_above, masks,
        partner_plus.reshape(1, BINS), partner_minus.reshape(1, BINS),
        jnp.asarray(speeds), jnp.asarray(stencil), jnp.asarray(table),
    )

    arrived = lax.all_to_all(sent.reshape(OWNERS, 1, 512), "bins", 0, 0).reshape(4 * OWNERS, 128)
    drift_low = lax.ppermute(drift[32:48], "bins", east)
    drift_high = lax.ppermute(drift[0:16], "bins", west)

    middle, zonal_all, low, high = pl.pallas_call(
        unpack_kernel,
        out_shape=shapes((OWN * ROWS, NLON), (ROWS, NLON), (24, NLON), (24, NLON)),
        scratch_shapes=[pltpu.VMEM((NLON, 128), F32), pltpu.VMEM((NLON, 128), F32)],
        compiler_params=grant,
    )(arrived, drift, drift_low, drift_high)
    from_below = lax.ppermute(high, "lat", up)
    from_above = lax.ppermute(low, "lat", down)

    row = jnp.arange(32, dtype=jnp.int32)[None, :] // 2 + source_map // 3 - 1
    col = jnp.arange(6, dtype=jnp.int32)[:, None] // 2 + source_map % 3
    place = jnp.where(row < 0, 80 + col, jnp.where(row > 15, 88 + col, 16 * col + row))
    place = jnp.pad(place.reshape(1, 192), ((0, 0), (0, 64))).astype(F32)
    second, stokes = pl.pallas_call(
        final_kernel,
        out_shape=shapes((OWN, ROWS, NLON), (2, 192, 64)),
        in_specs=[smem, smem] + [vmem] * 9,
        scratch_shapes=[pltpu.VMEM((32, NLON), F32), pltpu.VMEM((128, 128), F32)],
        compiler_params=grant,
    )(
        device, jnp.asarray(speed_list), middle, zonal_all, from_below, from_above, sea_mask,
        drift, drift_low, drift_high, place,
    )
    return second, stokes.reshape(2, 6, 32, LEV).transpose(0, 3, 1, 2)


def solution(mesh):
    in_specs = (P("bins", "lat", None), P("lat", None), P("bins", "lat"), P(), P(), P("bins", "lat"))
    out_specs = (P("bins", "lat", None), P(None, None, "bins", "lat"))
    return jax.shard_map(on_device, mesh=mesh, in_specs=in_specs, out_specs=out_specs, check_vma=False)
```

```python
import math

import jax
import jax.numpy as jnp
import numpy as np
from jax import lax
from jax.experimental import pallas as pl
from jax.experimental.pallas import tpu as pltpu
from jax.sharding import PartitionSpec as P

NDIR = 36
NFREQ = 32
LEV = 64
BINS = NDIR * NFREQ
OWN = 9
ROWS = 16
NLON = 384
OWNERS = 128
COLS = 3
F32 = jnp.float32
BF16 = jnp.bfloat16
HIGHEST = lax.Precision.HIGHEST

GROUP_COLUMNS = (0, 1, 2, -2, -1, 3, 4)


def bin_values():
    j = np.arange(NFREQ, dtype=np.float64)
    angles = 2.0 * math.pi * (np.arange(NDIR) + 0.5) / NDIR
    speeds = np.repeat(0.12 + 0.25 * (NFREQ - 1 - j) / (NFREQ - 1), NDIR)
    cosines, sines = np.tile(np.cos(angles), NFREQ), np.tile(np.sin(angles), NFREQ)
    strength = np.repeat(0.06 * (1.0 + j / (NFREQ - 1)), NDIR)
    levels = np.arange(LEV) + 0.5
    decay = np.repeat(np.exp(-levels[:, None] * (0.02 * 1.15**j)[None, :]), NDIR, axis=1)
    drift = 2.0 / math.sqrt(BINS) * np.concatenate([decay * cosines, decay * sines], axis=0)
    return speeds * cosines, speeds * sines, strength, drift


def stencils():
    lane = {}
    for group, column in enumerate(GROUP_COLUMNS):
        for r in range(ROWS):
            lane[column, r] = 16 * group + r
    for column in range(COLS):
        for k in range(2):
            lane[column, k - 2] = 112 + 2 * column + k
            lane[column, 16 + k] = 118 + 2 * column + k
    table = np.zeros((128, 256), np.float32)
    for r in range(ROWS):
        for face in range(COLS + 1):
            at = 16 * face + r
            for d, w in ((-2, -1), (-1, 5), (0, 2)):
                table[lane[face + d, r], at] += w
            for d, w in ((-1, 2), (0, 5), (1, -1)):
                table[lane[face + d, r], 128 + at] += w
        for column in range(COLS):
            at = 64 + 16 * column + r
            for d, w in ((-2, 1), (-1, -6), (0, 3), (1, 2)):
                table[lane[column, r + d], at] += w
            for d, w in ((-1, -2), (0, -3), (1, 6), (2, -1)):
                table[lane[column, r + d], 128 + at] += w
    return table


def lanes(rows=1):
    return lax.broadcasted_iota(jnp.int32, (rows, 128), 1)


def split_beside(x):
    upper = x.astype(BF16).astype(F32)
    return (upper + pltpu.roll(x - upper, 64, 1)).astype(BF16)


def pack_kernel(spec_at, mask_at, current_at, out, mask_out, spec, mask, current, stack, turned, turned2, done):
    copies = [
        pltpu.make_async_copy(source, held, done.at[k])
        for k, (source, held) in enumerate(((spec_at, spec), (mask_at, mask), (current_at, current)))
    ]
    for copy in copies:
        copy.start()
    for copy in copies:
        copy.wait()
    sea = mask[...].astype(F32)
    masked = spec[...] * sea[None]
    stack[0:16, :] = masked[8]
    stack[16:32, :] = sea
    stack[32:128, :] = jnp.zeros((96, NLON), F32)
    turned[...] = masked[0:8].reshape(128, NLON).T
    turned2[...] = stack[...].T

    pair = lax.broadcasted_iota(jnp.int32, (32, 128), 0) // 2
    means = jnp.where(pair == lax.broadcasted_iota(jnp.int32, (32, 128), 1) % 16, 0.25, 0.0)
    sums = jnp.dot(current[...], means, precision=HIGHEST, preferred_element_type=F32)
    group = lanes(OWNERS) // 16
    rest = jnp.zeros((OWNERS, 128), F32)
    sea_rows = jnp.zeros((OWNERS, 128), F32)
    for c in range(COLS):
        out[pl.ds(c, OWNERS, stride=4), :] = turned[pl.ds(c, OWNERS, stride=COLS), :]
        column = turned2[pl.ds(c, OWNERS, stride=COLS), :]
        zonal = sums[2 * c : 2 * c + 1] + sums[2 * c + 1 : 2 * c + 2]
        rest = jnp.where(group == 2 * c, pltpu.roll(column, 32 * c, 1), rest)
        rest = jnp.where(group == 2 * c + 1, jnp.broadcast_to(zonal, rest.shape), rest)
        sea_rows = jnp.where(group == c, pltpu.roll(column, (16 * c - 16) % 128, 1), sea_rows)
    out[pl.ds(3, OWNERS, stride=4), :] = rest
    mask_out[...] = sea_rows


def edges_kernel(arrived, to_east, to_west, to_above, to_below):
    def part(c):
        return arrived[pl.ds(c, OWNERS, stride=4), :]

    lane = lanes(OWNERS)
    group = lane // 16
    inside = lane % 16
    rest = part(3)
    for ref, c in ((to_east, 1), (to_west, 0)):
        ref[0:128, :] = part(c)
        ref[128:256, :] = part(c + 1)
        pair = jnp.where(
            group == 0, pltpu.roll(rest, (-32 * c) % 128, 1), pltpu.roll(rest, (16 - 32 * (c + 1)) % 128, 1)
        )
        last = jnp.zeros((32, 128), F32)
        for q in range(4):
            moved = pltpu.roll(pair[32 * q : 32 * q + 32], 32 * q, 1)
            last = jnp.where(group[0:32] // 2 == q, moved, last)
        ref[256:288, :] = last
    for ref, r in ((to_above, 14), (to_below, 0)):
        acc = jnp.zeros((OWNERS, 128), F32)
        for c in range(COLS):
            moved = pltpu.roll(part(c), (2 * c - r) % 128, 1)
            acc = jnp.where((inside >= 2 * c) & (inside < 2 * c + 2), moved, acc)
        for c in range(COLS):
            moved = pltpu.roll(rest, (6 + 2 * c - 32 * c - r) % 128, 1)
            acc = jnp.where((lane >= 6 + 2 * c) & (lane < 8 + 2 * c), moved, acc)
        ref[...] = acc


def partners_kernel(plus, minus, stencil_in, speeds_in, table_in, picks, hits, stencil, speeds, table):
    stencil[...] = stencil_in[...]
    speeds[...] = speeds_in[...]
    table[...] = table_in[...]
    numbers = lax.broadcasted_iota(jnp.int32, (128, BINS), 1).astype(F32)
    for t in range(OWN):
        rows = slice(128 * t, 128 * t + 128)
        for k, row in enumerate((plus, minus)):
            column = jnp.broadcast_to(row[:, rows].astype(F32), (128, 128)).T
            wide = jnp.concatenate([column] * OWN, axis=1)
            picks[BINS * k + 128 * t : BINS * k + 128 * t + 128, :] = jnp.where(wide == numbers, 1.0, 0.0).astype(BF16)
        names = lax.broadcasted_iota(jnp.int32, (128, BINS), 0) + 128 * t
        both = jnp.where(plus[...] == names, 1.0, 0.0) + jnp.where(minus[...] == names, 1.0, 0.0)
        hits[rows, :] = both.astype(BF16)


def points_kernel(
    me, arrived, from_west, from_east, from_below, from_above, masks, picks, hits, stencil, speeds, table,
    out, drift_out, first, source, middle, halves,
):
    device = me[0]
    lane = lanes(OWNERS)
    group = lane // 16

    flow = arrived[pl.ds(4 * device + 3, 1), :]
    below = arrived[pl.ds(4 * jnp.maximum(device - 1, 0) + 3, 1), :]
    above = arrived[pl.ds(4 * jnp.minimum(device + 1, OWNERS - 1) + 3, 1), :]
    lower = jnp.where(device > 0, pltpu.roll(below, 48, 1), 0.0)
    upper = jnp.where(device < OWNERS - 1, pltpu.roll(above, 32, 1), 0.0)
    lane1 = lanes()
    group1 = lane1 // 16
    for c in range(COLS):
        lower = jnp.where(group1 == c + 1, pltpu.roll(flow, (-16 * c) % 128, 1), lower)
        upper = jnp.where(group1 == c, pltpu.roll(flow, (-16 * (c + 1)) % 128, 1), upper)
    faces = jnp.where(lane1 < 64, 0.5 * (lower + upper), 0.0)
    sea = masks[pl.ds(device, 1), :]

    def chunk(t):
        return slice(128 * t, 128 * t + 128)

    for i in range(OWN):
        acc = jnp.zeros((OWNERS, 128), F32)
        for g in range(7):
            if i == 8:
                if g < 3:
                    part = pltpu.roll(arrived[pl.ds(3, OWNERS, stride=4), :], (-16 * g) % 128, 1)
                else:
                    ref, at = (from_west, 48) if g < 5 else (from_east, 80)
                    piece = ref[256:288, :]
                    part = jnp.concatenate([pltpu.roll(piece, (at - 32 * q) % 128, 1) for q in range(4)], axis=0)
            else:
                if g < 3:
                    part = arrived[pl.ds(g, OWNERS, stride=4), :]
                elif g < 5:
                    part = from_west[chunk(g - 3), :]
                else:
                    part = from_east[chunk(g - 5), :]
                part = pltpu.roll(part, (16 * g - 16 * i) % 128, 1)
            acc = jnp.where(group == g, part, acc)
        held = 16 * i if i < 8 else 6
        for ref, at in ((from_below, 112), (from_above, 118)):
            acc = jnp.where((lane >= at) & (lane < at + 6), pltpu.roll(ref[...], (at - held) % 128, 1), acc)
        middle[pl.ds(i, OWNERS, stride=OWN), :] = acc

    for t in range(OWN):
        value = middle[chunk(t), :]
        upper_half = value.astype(BF16)
        lower_half = (value - upper_half.astype(F32)).astype(BF16)
        sums = jnp.dot(upper_half, stencil[...], preferred_element_type=F32) + jnp.dot(
            lower_half, stencil[...], preferred_element_type=F32
        )
        speed = (speeds[chunk(t), :] + faces) * (1.0 / 6.0)
        flux = jnp.maximum(speed, 0.0) * sums[:, 0:128] + jnp.minimum(speed, 0.0) * sums[:, 128:256]
        change = (pltpu.roll(flux, 112, 1) - flux) + pltpu.roll(flux, 64, 1)
        moved = sea * (value - change)
        moved = jnp.where(lane < 48, moved, 0.0)
        first[chunk(t), :] = moved
        halves[chunk(t), :] = split_beside(moved)

    def gathered(at):
        both = jnp.dot(picks[at : at + 128, :], halves[...], preferred_element_type=F32)
        return both + pltpu.roll(both, 64, 1)

    for t in range(OWN):
        ahead = gathered(128 * t)
        behind = gathered(BINS + 128 * t)
        f = first[chunk(t), :]
        strength = jnp.broadcast_to(speeds[chunk(t), 127:128], (128, 128))
        source[chunk(t), :] = strength * (f * f * (ahead + behind) - 2.0 * f * ahead * behind)
    for t in range(OWN):
        halves[chunk(t), :] = split_beside(source[chunk(t), :])
    for t in range(OWN):
        both = jnp.dot(hits[chunk(t), :], halves[...], preferred_element_type=F32)
        back = both + pltpu.roll(both, 64, 1)
        m = first[chunk(t), :] + (source[chunk(t), :] - 0.5 * back)
        middle[chunk(t), :] = jnp.where(lane < 48, m, 0.0)
    for t in range(OWN):
        halves[chunk(t), :] = split_beside(middle[chunk(t), :])
    sums = jnp.dot(table[...], halves[...], preferred_element_type=F32)
    drift = sums[0:128] + pltpu.roll(sums[0:128], 64, 1) + sums[128:256]
    drift_out[...] = drift.T[0:48]

    for c in range(COLS):
        acc = jnp.zeros((OWNERS, 128), F32)
        for i in range(8):
            part = pltpu.roll(middle[pl.ds(i, OWNERS, stride=OWN), :], (16 * (i - c)) % 128, 1)
            acc = jnp.where(group == i, part, acc)
        out[pl.ds(c, OWNERS, stride=4), :] = acc
    acc = jnp.broadcast_to(flow, (OWNERS, 128))
    last = middle[pl.ds(8, OWNERS, stride=OWN), :]
    for c in range(COLS):
        acc = jnp.where(group == 2 * c, pltpu.roll(last, 16 * c, 1), acc)
    out[pl.ds(3, OWNERS, stride=4), :] = acc


def unpack_kernel(arrived, drift, drift_low, drift_high, middle, zonal, low, high, turned, turned2):
    for c in range(COLS):
        turned[pl.ds(c, OWNERS, stride=COLS), :] = arrived[pl.ds(c, OWNERS, stride=4), :]
        rest = arrived[pl.ds(3, OWNERS, stride=4), :]
        turned2[pl.ds(c, OWNERS, stride=COLS), :] = pltpu.roll(rest, (128 - 32 * c) % 128, 1)
    middle[0:128, :] = turned[...].T
    rest = turned2[...].T
    middle[128:144, :] = rest[0:16]
    zonal[...] = rest[16:32]
    for i in range(OWN):
        low[2 * i : 2 * i + 2, :] = middle[16 * i : 16 * i + 2, :]
        high[2 * i : 2 * i + 2, :] = middle[16 * i + 14 : 16 * i + 16, :]
    for ref, r in ((low, 0), (high, 15)):
        pieces = [drift_low[r : r + 1, :]] + [drift[16 * c + r : 16 * c + r + 1, :] for c in range(COLS)]
        pieces += [drift_high[r : r + 1, :], jnp.zeros((1, 128), F32)]
        ref[18:19, :] = jnp.concatenate(pieces[0:3], axis=1)
        ref[19:20, :] = jnp.concatenate(pieces[3:6], axis=1)
        ref[20:24, :] = jnp.zeros((4, NLON), F32)


def inside_kernel(me, speeds, middle, zonal, mask, out, rows):
    first_bin = me[0] * OWN
    sea = mask[...].astype(F32)
    column = lax.broadcasted_iota(jnp.int32, (ROWS, NLON), 1)

    def beside(x, d):
        moved = pltpu.roll(x, (-d) % NLON, 1)
        return jnp.where((column + d >= 0) & (column + d < NLON), moved, 0.0)

    flow = zonal[...]
    lower_flow = 0.5 * (beside(flow, -1) + flow)
    upper_flow = 0.5 * (flow + beside(flow, 1))
    rows[0:8, :] = jnp.zeros((8, NLON), F32)
    rows[24:32, :] = jnp.zeros((8, NLON), F32)
    for i in range(OWN):
        f = middle[16 * i : 16 * i + 16, :]
        rows[8:24, :] = f
        along_x = speeds[first_bin + i]
        along_y = speeds[BINS + first_bin + i]
        r2, r1, u1, u2 = rows[6:22, :], rows[7:23, :], rows[9:25, :], rows[10:26, :]
        forward = jnp.maximum(along_y, 0.0) * (1.0 / 6.0)
        backward = jnp.minimum(along_y, 0.0) * (1.0 / 6.0)
        change = forward * ((r2 - 6.0 * r1) + (3.0 * f + 2.0 * u1)) + backward * (
            (6.0 * u1 - u2) - (2.0 * r1 + 3.0 * f)
        )
        a2, a1, b1, b2 = beside(f, -2), beside(f, -1), beside(f, 1), beside(f, 2)
        speed = (along_x + upper_flow) * (1.0 / 6.0)
        change = change + (
            jnp.maximum(speed, 0.0) * (5.0 * f + 2.0 * b1 - a1) + jnp.minimum(speed, 0.0) * (2.0 * f + 5.0 * b1 - b2)
        )
        speed = (along_x + lower_flow) * (1.0 / 6.0)
        change = change - (
            jnp.maximum(speed, 0.0) * (5.0 * a1 + 2.0 * f - a2) + jnp.minimum(speed, 0.0) * (2.0 * a1 + 5.0 * f - b1)
        )
        out[i] = sea * (f - change)


def final_kernel(me, speeds, inside, low, high, mask, drift, drift_low, drift_high, place, out, stokes, near):
    first_bin = me[0] * OWN
    sea = mask[...].astype(F32)
    out[...] = inside[...]
    for i in range(OWN):
        along_y = speeds[BINS + first_bin + i]
        forward = jnp.maximum(along_y, 0.0) * (1.0 / 6.0)
        backward = jnp.minimum(along_y, 0.0) * (1.0 / 6.0)
        r2, r1 = low[2 * i : 2 * i + 1, :], low[2 * i + 1 : 2 * i + 2, :]
        u1, u2 = high[2 * i : 2 * i + 1, :], high[2 * i + 1 : 2 * i + 2, :]
        lower = jnp.concatenate([forward * (r2 - 6.0 * r1) - backward * (2.0 * r1), forward * r1], axis=0)
        upper = jnp.concatenate([-backward * u1, forward * (2.0 * u1) + backward * (6.0 * u1 - u2)], axis=0)
        out[i, 0:2, :] = inside[i, 0:2, :] - sea[0:2] * lower
        out[i, 14:16, :] = inside[i, 14:16, :] - sea[14:16] * upper

    near[...] = jnp.zeros_like(near)
    near[0:16, :] = drift_low[...]
    near[16:64, :] = drift[...]
    near[64:80, :] = drift_high[...]
    for ref, at in ((low, 80), (high, 88)):
        for k in range(5):
            near[at + k : at + k + 1, :] = ref[18 + k // 3 : 19 + k // 3, 128 * (k % 3) : 128 * (k % 3) + 128]
    wanted = jnp.broadcast_to(place[...], (128, 256)).T[0:192]
    chosen = jnp.where(wanted == lanes(192).astype(F32), 1.0, 0.0).astype(BF16)
    rest = near[...]
    total = jnp.zeros((192, 128), F32)
    for _ in range(3):
        part = rest.astype(BF16)
        rest = rest - part.astype(F32)
        total = total + jnp.dot(chosen, part, preferred_element_type=F32)
    stokes[0] = total[:, 0:64]
    stokes[1] = total[:, 64:128]


def shapes(*sizes):
    return [jax.ShapeDtypeStruct(size, F32) for size in sizes]


def on_device(spectrum, sea_mask, current, partner_plus, partner_minus, source_map):
    along_x, along_y, strength, drift_table = bin_values()
    speeds = np.zeros((BINS, 128), np.float32)
    speeds[:, 0:64] = along_x[:, None]
    speeds[:, 64:112] = along_y[:, None]
    speeds[:, 127] = strength
    speed_list = np.concatenate([along_x, along_y]).astype(np.float32)
    drift_upper = drift_table.astype(np.float32).astype(BF16)
    drift_lower = (drift_table.astype(np.float32) - drift_upper.astype(np.float32)).astype(BF16)
    table = np.concatenate([drift_upper, drift_lower], axis=0)
    stencil = stencils().astype(BF16)

    device = lax.axis_index("bins").reshape(1)
    bands = lax.axis_size("lat")
    up = [(i, i + 1) for i in range(bands - 1)]
    down = [(i + 1, i) for i in range(bands - 1)]
    east = [(i, i + 1) for i in range(OWNERS - 1)]
    west = [(i + 1, i) for i in range(OWNERS - 1)]

    smem = pl.BlockSpec(memory_space=pltpu.SMEM)
    vmem = pl.BlockSpec(memory_space=pltpu.VMEM)
    hbm = pl.BlockSpec(memory_space=pltpu.HBM)
    grant = pltpu.CompilerParams(vmem_limit_bytes=16 * 1024 * 1024)
    sent, masks = pl.pallas_call(
        pack_kernel,
        out_shape=shapes((4 * OWNERS, 128), (OWNERS, 128)),
        in_specs=[hbm] * 3,
        scratch_shapes=[
            pltpu.VMEM(spectrum.shape, F32),
            pltpu.VMEM(sea_mask.shape, jnp.int32),
            pltpu.VMEM(current.shape, F32),
            pltpu.VMEM((128, NLON), F32),
            pltpu.VMEM((NLON, 128), F32),
            pltpu.VMEM((NLON, 128), F32),
            pltpu.SemaphoreType.DMA((3,)),
        ],
        compiler_params=pltpu.CompilerParams(vmem_limit_bytes=60 * 1024 * 1024),
    )(spectrum, sea_mask, current)

    plus, minus, sent = lax.optimization_barrier((partner_plus, partner_minus, sent))
    arrived = lax.all_to_all(sent.reshape(OWNERS, 1, 512), "bins", 0, 0).reshape(4 * OWNERS, 128)
    tables = (jnp.asarray(stencil), jnp.asarray(speeds), jnp.asarray(table))
    tables = pl.pallas_call(
        partners_kernel,
        out_shape=[
            jax.ShapeDtypeStruct((2 * BINS, BINS), BF16),
            jax.ShapeDtypeStruct((BINS, BINS), BF16),
            *(jax.ShapeDtypeStruct(t.shape, t.dtype) for t in tables),
        ],
        compiler_params=grant,
        cost_estimate=pl.CostEstimate(flops=8 * BINS * BINS, bytes_accessed=6 * BINS * BINS, transcendentals=0),
    )(plus.reshape(1, BINS), minus.reshape(1, BINS), *tables)
    to_east, to_west, to_above, to_below = pl.pallas_call(
        edges_kernel,
        out_shape=shapes((288, 128), (288, 128), (OWNERS, 128), (OWNERS, 128)),
        compiler_params=grant,
    )(arrived)
    from_west = lax.ppermute(to_east, "bins", east)
    from_east = lax.ppermute(to_west, "bins", west)
    from_below = lax.ppermute(to_above, "lat", up)
    from_above = lax.ppermute(to_below, "lat", down)

    big = pltpu.VMEM((BINS, 128), F32)
    sent, drift = pl.pallas_call(
        points_kernel,
        out_shape=shapes((4 * OWNERS, 128), (48, 128)),
        in_specs=[smem] + [vmem] * 11,
        scratch_shapes=[big, big, big, pltpu.VMEM((BINS, 128), BF16)],
        compiler_params=pltpu.CompilerParams(vmem_limit_bytes=24 * 1024 * 1024),
    )(device, arrived, from_west, from_east, from_below, from_above, masks, *tables)

    arrived = lax.all_to_all(sent.reshape(OWNERS, 1, 512), "bins", 0, 0).reshape(4 * OWNERS, 128)
    drift_low = lax.ppermute(drift[32:48], "bins", east)
    drift_high = lax.ppermute(drift[0:16], "bins", west)

    middle, zonal_all, low, high = pl.pallas_call(
        unpack_kernel,
        out_shape=shapes((OWN * ROWS, NLON), (ROWS, NLON), (24, NLON), (24, NLON)),
        scratch_shapes=[pltpu.VMEM((NLON, 128), F32), pltpu.VMEM((NLON, 128), F32)],
        compiler_params=grant,
    )(arrived, drift, drift_low, drift_high)
    from_below = lax.ppermute(high, "lat", up)
    from_above = lax.ppermute(low, "lat", down)

    row = jnp.arange(32, dtype=jnp.int32)[None, :] // 2 + source_map // 3 - 1
    col = jnp.arange(6, dtype=jnp.int32)[:, None] // 2 + source_map % 3
    place = jnp.where(row < 0, 80 + col, jnp.where(row > 15, 88 + col, 16 * col + row))
    place = jnp.pad(place.reshape(1, 192), ((0, 0), (0, 64))).astype(F32)
    speed_refs = jnp.asarray(speed_list)
    inside = pl.pallas_call(
        inside_kernel,
        out_shape=jax.ShapeDtypeStruct((OWN, ROWS, NLON), F32),
        in_specs=[smem, smem] + [vmem] * 3,
        scratch_shapes=[pltpu.VMEM((32, NLON), F32)],
        compiler_params=grant,
        cost_estimate=pl.CostEstimate(flops=60 * OWN * ROWS * NLON, bytes_accessed=8 * OWN * ROWS * NLON, transcendentals=0),
    )(device, speed_refs, middle, zonal_all, sea_mask)
    second, stokes = pl.pallas_call(
        final_kernel,
        out_shape=shapes((OWN, ROWS, NLON), (2, 192, 64)),
        in_specs=[smem, smem] + [vmem] * 8,
        scratch_shapes=[pltpu.VMEM((128, 128), F32)],
        compiler_params=grant,
    )(device, speed_refs, inside, from_below, from_above, sea_mask, drift, drift_low, drift_high, place)
    return second, stokes.reshape(2, 6, 32, LEV).transpose(0, 3, 1, 2)


def solution(mesh):
    in_specs = (P("bins", "lat", None), P("lat", None), P("bins", "lat"), P(), P(), P("bins", "lat"))
    out_specs = (P("bins", "lat", None), P(None, None, "bins", "lat"))
    return jax.shard_map(on_device, mesh=mesh, in_specs=in_specs, out_specs=out_specs, check_vma=False)
```

```python
import math

import jax
import jax.numpy as jnp
import numpy as np
from jax import lax
from jax.experimental import pallas as pl
from jax.experimental.pallas import tpu as pltpu
from jax.sharding import Mesh
from jax.sharding import PartitionSpec as P

NDIR = 36
NFREQ = 32
LEV = 64
BINS = NDIR * NFREQ
OWN = 9
ROWS = 16
NLON = 384
OWNERS = 128
BANDS = 4
ALONG_BINS = ("z", "y", "x")
EXCHANGE = ("z", "x", "y")
COLS = 3
F32 = jnp.float32
BF16 = jnp.bfloat16
HIGHEST = lax.Precision.HIGHEST

GROUP_COLUMNS = (0, 1, 2, -2, -1, 3, 4)


def bin_values():
    j = np.arange(NFREQ, dtype=np.float64)
    angles = 2.0 * math.pi * (np.arange(NDIR) + 0.5) / NDIR
    speeds = np.repeat(0.12 + 0.25 * (NFREQ - 1 - j) / (NFREQ - 1), NDIR)
    cosines, sines = np.tile(np.cos(angles), NFREQ), np.tile(np.sin(angles), NFREQ)
    strength = np.repeat(0.06 * (1.0 + j / (NFREQ - 1)), NDIR)
    wavenumber = np.repeat(0.02 * 1.15**j, NDIR)
    amplitude = 2.0 / math.sqrt(BINS)
    rows = (speeds * cosines, speeds * sines, strength, -wavenumber, amplitude * cosines, amplitude * sines)
    return np.stack(rows).astype(np.float32)


def stencils():
    lane = {}
    for group, column in enumerate(GROUP_COLUMNS):
        for r in range(ROWS):
            lane[column, r] = 16 * group + r
    for column in range(COLS):
        for k in range(2):
            lane[column, k - 2] = 112 + 2 * column + k
            lane[column, 16 + k] = 118 + 2 * column + k
    table = np.zeros((128, 256), np.float32)
    for r in range(ROWS):
        for face in range(COLS + 1):
            at = 16 * face + r
            for d, w in ((-2, -1), (-1, 5), (0, 2)):
                table[lane[face + d, r], at] += w
            for d, w in ((-1, 2), (0, 5), (1, -1)):
                table[lane[face + d, r], 128 + at] += w
        for column in range(COLS):
            at = 64 + 16 * column + r
            for d, w in ((-2, 1), (-1, -6), (0, 3), (1, 2)):
                table[lane[column, r + d], at] += w
            for d, w in ((-1, -2), (0, -3), (1, 6), (2, -1)):
                table[lane[column, r + d], 128 + at] += w
    return table


def lanes(rows=1):
    return lax.broadcasted_iota(jnp.int32, (rows, 128), 1)


def exchange_place(device):
    return (device & -8) | ((device & 3) << 1) | ((device >> 2) & 1)


def device_at(place):
    return (place & -8) | ((place & 1) << 2) | ((place >> 1) & 3)


def bin_at(row):
    place = (row * 7282) >> 16
    return device_at(place) * OWN + row - place * OWN


def split_beside(x):
    upper = x.astype(BF16).astype(F32)
    return (upper + pltpu.roll(x - upper, 64, 1)).astype(BF16)


def pack_kernel(spec, mask, current, out, mask_out, stack, turned, turned2, held):
    sea = mask[...].astype(F32)
    masked = spec[...] * sea[None]
    stack[0:16, :] = masked[8]
    stack[16:32, :] = sea
    stack[32:128, :] = jnp.zeros((96, NLON), F32)
    turned[...] = masked[0:8].reshape(128, NLON).T
    turned2[...] = stack[...].T

    pair = lax.broadcasted_iota(jnp.int32, (32, 128), 0) // 2
    means = jnp.where(pair == lax.broadcasted_iota(jnp.int32, (32, 128), 1) % 16, 0.25, 0.0)
    sums = jnp.dot(current[...], means, precision=HIGHEST, preferred_element_type=F32)
    group = lanes(OWNERS) // 16
    rest = jnp.zeros((OWNERS, 128), F32)
    sea_rows = jnp.zeros((OWNERS, 128), F32)
    for c in range(COLS):
        for j in range(8):
            out[pl.ds(4 * exchange_place(j) + c, 16, stride=32), :] = turned[pl.ds(COLS * j + c, 16, stride=8 * COLS), :]
        column = turned2[pl.ds(c, OWNERS, stride=COLS), :]
        zonal = sums[2 * c : 2 * c + 1] + sums[2 * c + 1 : 2 * c + 2]
        rest = jnp.where(group == 2 * c, pltpu.roll(column, 32 * c, 1), rest)
        rest = jnp.where(group == 2 * c + 1, jnp.broadcast_to(zonal, rest.shape), rest)
        sea_rows = jnp.where(group == c, pltpu.roll(column, (16 * c - 16) % 128, 1), sea_rows)
    held[...] = rest
    for j in range(8):
        out[pl.ds(4 * exchange_place(j) + 3, 16, stride=32), :] = held[pl.ds(j, 16, stride=8), :]
    mask_out[...] = sea_rows


def edges_kernel(band, arrived, to_east, to_west, to_bands):
    def part(c):
        return arrived[pl.ds(c, OWNERS, stride=4), :]

    lane = lanes(OWNERS)
    group = lane // 16
    inside = lane % 16
    rest = part(3)
    for ref, c in ((to_east, 1), (to_west, 0)):
        ref[0:128, :] = part(c)
        ref[128:256, :] = part(c + 1)
        pair = jnp.where(
            group == 0, pltpu.roll(rest, (-32 * c) % 128, 1), pltpu.roll(rest, (16 - 32 * (c + 1)) % 128, 1)
        )
        last = jnp.zeros((32, 128), F32)
        for q in range(4):
            moved = pltpu.roll(pair[32 * q : 32 * q + 32], 32 * q, 1)
            last = jnp.where(group[0:32] // 2 == q, moved, last)
        ref[256:288, :] = last
    here = band[0]
    to_bands[...] = jnp.zeros_like(to_bands)
    for target, r in ((jnp.minimum(here + 1, BANDS - 1), 14), (jnp.maximum(here - 1, 0), 0)):
        acc = jnp.zeros((OWNERS, 128), F32)
        for c in range(COLS):
            moved = pltpu.roll(part(c), (2 * c - r) % 128, 1)
            acc = jnp.where((inside >= 2 * c) & (inside < 2 * c + 2), moved, acc)
        for c in range(COLS):
            moved = pltpu.roll(rest, (6 + 2 * c - 32 * c - r) % 128, 1)
            acc = jnp.where((lane >= 6 + 2 * c) & (lane < 8 + 2 * c), moved, acc)
        to_bands[pl.ds(pl.multiple_of(target * OWNERS, OWNERS), OWNERS), :] = acc
    to_bands[pl.ds(pl.multiple_of(here * OWNERS, OWNERS), OWNERS), :] = jnp.zeros((OWNERS, 128), F32)


def points_kernel(
    me, arrived, from_west, from_east, from_bands, masks, plus, minus, stencil, values,
    out, drift_out, first, source, middle, halves, speeds, plus_col, minus_col,
):
    device = me[0]
    lane = lanes(OWNERS)
    group = lane // 16

    flow = arrived[pl.ds(4 * exchange_place(device) + 3, 1), :]
    below = arrived[pl.ds(4 * exchange_place(jnp.maximum(device - 1, 0)) + 3, 1), :]
    above = arrived[pl.ds(4 * exchange_place(jnp.minimum(device + 1, OWNERS - 1)) + 3, 1), :]
    lower = jnp.where(device > 0, pltpu.roll(below, 48, 1), 0.0)
    upper = jnp.where(device < OWNERS - 1, pltpu.roll(above, 32, 1), 0.0)
    lane1 = lanes()
    group1 = lane1 // 16
    for c in range(COLS):
        lower = jnp.where(group1 == c + 1, pltpu.roll(flow, (-16 * c) % 128, 1), lower)
        upper = jnp.where(group1 == c, pltpu.roll(flow, (-16 * (c + 1)) % 128, 1), upper)
    faces = jnp.where(lane1 < 64, 0.5 * (lower + upper), 0.0)
    sea = masks[pl.ds(device, 1), :]

    def chunk(t):
        return slice(128 * t, 128 * t + 128)

    def band_rows(band):
        return from_bands[pl.ds(pl.multiple_of(band * OWNERS, OWNERS), OWNERS), :]

    for i in range(OWN):
        acc = jnp.zeros((OWNERS, 128), F32)
        for g in range(7):
            if i == 8:
                if g < 3:
                    part = pltpu.roll(arrived[pl.ds(3, OWNERS, stride=4), :], (-16 * g) % 128, 1)
                else:
                    ref, at = (from_west, 48) if g < 5 else (from_east, 80)
                    piece = ref[256:288, :]
                    part = jnp.concatenate([pltpu.roll(piece, (at - 32 * q) % 128, 1) for q in range(4)], axis=0)
            else:
                if g < 3:
                    part = arrived[pl.ds(g, OWNERS, stride=4), :]
                elif g < 5:
                    part = from_west[chunk(g - 3), :]
                else:
                    part = from_east[chunk(g - 5), :]
                part = pltpu.roll(part, (16 * g - 16 * i) % 128, 1)
            acc = jnp.where(group == g, part, acc)
        held = 16 * i if i < 8 else 6
        for band, at in ((jnp.maximum(me[1] - 1, 0), 112), (jnp.minimum(me[1] + 1, BANDS - 1), 118)):
            beyond = pltpu.roll(band_rows(band), (at - held) % 128, 1)
            acc = jnp.where((lane >= at) & (lane < at + 6), beyond, acc)
        middle[pl.ds(i, OWNERS, stride=OWN), :] = acc

    inner = lax.broadcasted_iota(jnp.int32, (128, 128), 0)
    for t in range(OWN):
        value = middle[chunk(t), :]
        upper_half = value.astype(BF16)
        lower_half = (value - upper_half.astype(F32)).astype(BF16)
        sums = jnp.dot(upper_half, stencil[...], preferred_element_type=F32) + jnp.dot(
            lower_half, stencil[...], preferred_element_type=F32
        )
        part = jnp.where(inner < 64, values[0:1, chunk(t)], values[1:2, chunk(t)])
        speeds[chunk(t), :] = jnp.where(inner == 127, values[2:3, chunk(t)], part).T
        for row, col in ((plus, plus_col), (minus, minus_col)):
            col[chunk(t), :] = jnp.broadcast_to(row[:, chunk(t)].astype(F32), (128, 128)).T
        speed = (speeds[chunk(t), :] + faces) * (1.0 / 6.0)
        flux = jnp.maximum(speed, 0.0) * sums[:, 0:128] + jnp.minimum(speed, 0.0) * sums[:, 128:256]
        change = (pltpu.roll(flux, 112, 1) - flux) + pltpu.roll(flux, 64, 1)
        moved = sea * (value - change)
        moved = jnp.where(lane < 48, moved, 0.0)
        first[chunk(t), :] = moved
        halves[chunk(t), :] = split_beside(moved)

    numbers = bin_at(lax.broadcasted_iota(jnp.int32, (128, BINS), 1)).astype(F32)

    def gathered(col, t):
        wide = jnp.concatenate([col[chunk(t), :]] * OWN, axis=1)
        chosen = jnp.where(wide == numbers, 1.0, 0.0).astype(BF16)
        both = jnp.dot(chosen, halves[...], preferred_element_type=F32)
        return both + pltpu.roll(both, 64, 1)

    for t in range(OWN):
        ahead = gathered(plus_col, t)
        behind = gathered(minus_col, t)
        f = first[chunk(t), :]
        strength = jnp.broadcast_to(speeds[chunk(t), 127:128], (128, 128))
        source[chunk(t), :] = strength * (f * f * (ahead + behind) - 2.0 * f * ahead * behind)
    for t in range(OWN):
        halves[chunk(t), :] = split_beside(source[chunk(t), :])
    for t in range(OWN):
        names = bin_at(inner + 128 * t)
        names = jnp.concatenate([names] * OWN, axis=1)
        hits = jnp.where(plus[...] == names, 1.0, 0.0) + jnp.where(minus[...] == names, 1.0, 0.0)
        both = jnp.dot(hits.astype(BF16), halves[...], preferred_element_type=F32)
        back = both + pltpu.roll(both, 64, 1)
        m = first[chunk(t), :] + (source[chunk(t), :] - 0.5 * back)
        middle[chunk(t), :] = jnp.where(lane < 48, m, 0.0)
    for t in range(OWN):
        halves[chunk(t), :] = split_beside(middle[chunk(t), :])
    level = lax.broadcasted_iota(jnp.int32, (LEV, BINS), 0).astype(F32) + 0.5
    decay = jnp.exp(level * values[3:4, :])
    table = jnp.concatenate([decay * values[4:5, :], decay * values[5:6, :]], axis=0)
    table_upper = table.astype(BF16)
    table_lower = (table - table_upper.astype(F32)).astype(BF16)
    sums = jnp.dot(table_upper, halves[...], preferred_element_type=F32)
    drift = sums + pltpu.roll(sums, 64, 1) + jnp.dot(table_lower, halves[...], preferred_element_type=F32)
    drift_out[...] = drift.T[0:48]

    for c in range(COLS):
        acc = jnp.zeros((OWNERS, 128), F32)
        for i in range(8):
            part = pltpu.roll(middle[pl.ds(i, OWNERS, stride=OWN), :], (16 * (i - c)) % 128, 1)
            acc = jnp.where(group == i, part, acc)
        out[pl.ds(c, OWNERS, stride=4), :] = acc
    acc = jnp.broadcast_to(flow, (OWNERS, 128))
    last = middle[pl.ds(8, OWNERS, stride=OWN), :]
    for c in range(COLS):
        acc = jnp.where(group == 2 * c, pltpu.roll(last, 16 * c, 1), acc)
    out[pl.ds(3, OWNERS, stride=4), :] = acc


def unpack_kernel(arrived, drift, drift_low, drift_high, middle, zonal, low, high, turned, turned2):
    for j in range(8):
        place = 4 * exchange_place(j)
        rest = arrived[pl.ds(place + 3, 16, stride=32), :]
        for c in range(COLS):
            turned[pl.ds(COLS * j + c, 16, stride=8 * COLS), :] = arrived[pl.ds(place + c, 16, stride=32), :]
            turned2[pl.ds(COLS * j + c, 16, stride=8 * COLS), :] = pltpu.roll(rest, (128 - 32 * c) % 128, 1)
    middle[0:128, :] = turned[...].T
    rest = turned2[...].T
    middle[128:144, :] = rest[0:16]
    zonal[...] = rest[16:32]
    for i in range(OWN):
        low[2 * i : 2 * i + 2, :] = middle[16 * i : 16 * i + 2, :]
        high[2 * i : 2 * i + 2, :] = middle[16 * i + 14 : 16 * i + 16, :]
    for ref, r in ((low, 0), (high, 15)):
        pieces = [drift_low[r : r + 1, :]] + [drift[16 * c + r : 16 * c + r + 1, :] for c in range(COLS)]
        pieces += [drift_high[r : r + 1, :], jnp.zeros((1, 128), F32)]
        ref[18:19, :] = jnp.concatenate(pieces[0:3], axis=1)
        ref[19:20, :] = jnp.concatenate(pieces[3:6], axis=1)
        ref[20:24, :] = jnp.zeros((4, NLON), F32)


def inside_kernel(me, speeds, middle, zonal, mask, out, rows):
    first_bin = me[0] * OWN
    sea = mask[...].astype(F32)
    column = lax.broadcasted_iota(jnp.int32, (ROWS, NLON), 1)

    def beside(x, d):
        moved = pltpu.roll(x, (-d) % NLON, 1)
        return jnp.where((column + d >= 0) & (column + d < NLON), moved, 0.0)

    flow = zonal[...]
    lower_flow = 0.5 * (beside(flow, -1) + flow)
    upper_flow = 0.5 * (flow + beside(flow, 1))
    rows[0:8, :] = jnp.zeros((8, NLON), F32)
    rows[24:32, :] = jnp.zeros((8, NLON), F32)
    for i in range(OWN):
        f = middle[16 * i : 16 * i + 16, :]
        rows[8:24, :] = f
        along_x = speeds[first_bin + i]
        along_y = speeds[BINS + first_bin + i]
        r2, r1, u1, u2 = rows[6:22, :], rows[7:23, :], rows[9:25, :], rows[10:26, :]
        forward = jnp.maximum(along_y, 0.0) * (1.0 / 6.0)
        backward = jnp.minimum(along_y, 0.0) * (1.0 / 6.0)
        change = forward * ((r2 - 6.0 * r1) + (3.0 * f + 2.0 * u1)) + backward * (
            (6.0 * u1 - u2) - (2.0 * r1 + 3.0 * f)
        )
        a2, a1, b1, b2 = beside(f, -2), beside(f, -1), beside(f, 1), beside(f, 2)
        speed = (along_x + upper_flow) * (1.0 / 6.0)
        change = change + (
            jnp.maximum(speed, 0.0) * (5.0 * f + 2.0 * b1 - a1) + jnp.minimum(speed, 0.0) * (2.0 * f + 5.0 * b1 - b2)
        )
        speed = (along_x + lower_flow) * (1.0 / 6.0)
        change = change - (
            jnp.maximum(speed, 0.0) * (5.0 * a1 + 2.0 * f - a2) + jnp.minimum(speed, 0.0) * (2.0 * a1 + 5.0 * f - b1)
        )
        out[i] = sea * (f - change)


def final_kernel(me, speeds, inside, low, high, mask, drift, drift_low, drift_high, place, out, stokes, near):
    first_bin = me[0] * OWN
    sea = mask[...].astype(F32)
    out[...] = inside[...]
    for i in range(OWN):
        along_y = speeds[BINS + first_bin + i]
        forward = jnp.maximum(along_y, 0.0) * (1.0 / 6.0)
        backward = jnp.minimum(along_y, 0.0) * (1.0 / 6.0)
        r2, r1 = low[2 * i : 2 * i + 1, :], low[2 * i + 1 : 2 * i + 2, :]
        u1, u2 = high[2 * i : 2 * i + 1, :], high[2 * i + 1 : 2 * i + 2, :]
        lower = jnp.concatenate([forward * (r2 - 6.0 * r1) - backward * (2.0 * r1), forward * r1], axis=0)
        upper = jnp.concatenate([-backward * u1, forward * (2.0 * u1) + backward * (6.0 * u1 - u2)], axis=0)
        out[i, 0:2, :] = inside[i, 0:2, :] - sea[0:2] * lower
        out[i, 14:16, :] = inside[i, 14:16, :] - sea[14:16] * upper

    near[...] = jnp.zeros_like(near)
    near[0:16, :] = drift_low[...]
    near[16:64, :] = drift[...]
    near[64:80, :] = drift_high[...]
    for ref, at in ((low, 80), (high, 88)):
        for k in range(5):
            near[at + k : at + k + 1, :] = ref[18 + k // 3 : 19 + k // 3, 128 * (k % 3) : 128 * (k % 3) + 128]
    wanted = jnp.broadcast_to(place[...], (128, 256)).T[0:192]
    chosen = jnp.where(wanted == lanes(192).astype(F32), 1.0, 0.0).astype(BF16)
    rest = near[...]
    total = jnp.zeros((192, 128), F32)
    for _ in range(3):
        part = rest.astype(BF16)
        rest = rest - part.astype(F32)
        total = total + jnp.dot(chosen, part, preferred_element_type=F32)
    stokes[0] = total[:, 0:64]
    stokes[1] = total[:, 64:128]


def in_exchange_order(partner):
    return partner.reshape(16, 2, 4, OWN).transpose(0, 2, 1, 3).reshape(1, BINS)


def shapes(*sizes):
    return [jax.ShapeDtypeStruct(size, F32) for size in sizes]


def on_device(spectrum, sea_mask, current, partner_plus, partner_minus, source_map):
    values = bin_values()
    speed_list = values[0:2].reshape(-1)
    held_values = np.concatenate([values[:, bin_at(np.arange(BINS))], np.zeros((2, BINS), np.float32)])
    stencil = stencils().astype(BF16)

    device = lax.axis_index(ALONG_BINS).reshape(1)
    band = lax.axis_index("lat").reshape(1)
    me = jnp.concatenate([device, band])
    up = [(i, i + 1) for i in range(BANDS - 1)]
    down = [(i + 1, i) for i in range(BANDS - 1)]
    east = [(i, i + 1) for i in range(OWNERS - 1)]
    west = [(i + 1, i) for i in range(OWNERS - 1)]

    smem = pl.BlockSpec(memory_space=pltpu.SMEM)
    vmem = pl.BlockSpec(memory_space=pltpu.VMEM)
    grant = pltpu.CompilerParams(vmem_limit_bytes=16 * 1024 * 1024)
    sent, masks = pl.pallas_call(
        pack_kernel,
        out_shape=shapes((4 * OWNERS, 128), (OWNERS, 128)),
        scratch_shapes=[
            pltpu.VMEM((128, NLON), F32),
            pltpu.VMEM((NLON, 128), F32),
            pltpu.VMEM((NLON, 128), F32),
            pltpu.VMEM((OWNERS, 128), F32),
        ],
        compiler_params=grant,
    )(spectrum, sea_mask, current)

    plus, minus, sent = lax.optimization_barrier((partner_plus, partner_minus, sent))
    arrived = lax.all_to_all(sent.reshape(OWNERS, 1, 512), EXCHANGE, 0, 0).reshape(4 * OWNERS, 128)
    plus, minus = in_exchange_order(plus), in_exchange_order(minus)
    arrived, plus, minus = lax.optimization_barrier((arrived, plus, minus))
    to_east, to_west, to_bands = pl.pallas_call(
        edges_kernel,
        out_shape=shapes((288, 128), (288, 128), (BANDS * OWNERS, 128)),
        in_specs=[smem, vmem],
        compiler_params=grant,
    )(band, arrived)
    from_west = lax.ppermute(to_east, ALONG_BINS, east)
    from_east = lax.ppermute(to_west, ALONG_BINS, west)
    from_bands = lax.all_to_all(to_bands.reshape(BANDS, OWNERS, 128), "lat", 0, 0).reshape(BANDS * OWNERS, 128)

    big = pltpu.VMEM((BINS, 128), F32)
    sent, drift = pl.pallas_call(
        points_kernel,
        out_shape=shapes((4 * OWNERS, 128), (48, 128)),
        in_specs=[smem] + [vmem] * 9,
        scratch_shapes=[big, big, big, pltpu.VMEM((BINS, 128), BF16), big, big, big],
        compiler_params=pltpu.CompilerParams(vmem_limit_bytes=24 * 1024 * 1024),
    )(me, arrived, from_west, from_east, from_bands, masks, plus, minus, jnp.asarray(stencil), jnp.asarray(held_values))

    arrived = lax.all_to_all(sent.reshape(OWNERS, 1, 512), EXCHANGE, 0, 0).reshape(4 * OWNERS, 128)
    drift_low = lax.ppermute(drift[32:48], ALONG_BINS, east)
    drift_high = lax.ppermute(drift[0:16], ALONG_BINS, west)

    middle, zonal_all, low, high = pl.pallas_call(
        unpack_kernel,
        out_shape=shapes((OWN * ROWS, NLON), (ROWS, NLON), (24, NLON), (24, NLON)),
        scratch_shapes=[pltpu.VMEM((NLON, 128), F32), pltpu.VMEM((NLON, 128), F32)],
        compiler_params=grant,
    )(arrived, drift, drift_low, drift_high)
    from_below = lax.ppermute(high, "lat", up)
    from_above = lax.ppermute(low, "lat", down)

    row = jnp.arange(32, dtype=jnp.int32)[None, :] // 2 + source_map // 3 - 1
    col = jnp.arange(6, dtype=jnp.int32)[:, None] // 2 + source_map % 3
    place = jnp.where(row < 0, 80 + col, jnp.where(row > 15, 88 + col, 16 * col + row))
    place = jnp.pad(place.reshape(1, 192), ((0, 0), (0, 64))).astype(F32)
    speed_refs = jnp.asarray(speed_list)
    inside = pl.pallas_call(
        inside_kernel,
        out_shape=jax.ShapeDtypeStruct((OWN, ROWS, NLON), F32),
        in_specs=[smem, smem] + [vmem] * 3,
        scratch_shapes=[pltpu.VMEM((32, NLON), F32)],
        compiler_params=grant,
        cost_estimate=pl.CostEstimate(flops=60 * OWN * ROWS * NLON, bytes_accessed=8 * OWN * ROWS * NLON, transcendentals=0),
    )(device, speed_refs, middle, zonal_all, sea_mask)
    second, stokes = pl.pallas_call(
        final_kernel,
        out_shape=shapes((OWN, ROWS, NLON), (2, 192, 64)),
        in_specs=[smem, smem] + [vmem] * 8,
        scratch_shapes=[pltpu.VMEM((128, 128), F32)],
        compiler_params=grant,
    )(device, speed_refs, inside, from_below, from_above, sea_mask, drift, drift_low, drift_high, place)
    return second, stokes.reshape(2, 6, 32, LEV).transpose(0, 3, 1, 2)


def solution(mesh):
    finer = Mesh(mesh.devices.reshape(16, 2, 4, BANDS), ALONG_BINS + ("lat",))
    bins = ALONG_BINS
    in_specs = (P(bins, "lat", None), P("lat", None), P(bins, "lat"), P(), P(), P(bins, "lat"))
    out_specs = (P(bins, "lat", None), P(None, None, bins, "lat"))
    return jax.shard_map(on_device, mesh=finer, in_specs=in_specs, out_specs=out_specs, check_vma=False)
```

```python
import math

import jax
import jax.numpy as jnp
import numpy as np
from jax import lax
from jax.experimental import pallas as pl
from jax.experimental.pallas import tpu as pltpu
from jax.sharding import PartitionSpec as P

NDIR = 36
NFREQ = 32
LEV = 64
BINS = NDIR * NFREQ
OWN = 9
ROWS = 16
NLON = 384
OWNERS = 128
BANDS = 4
COLS = 3
F32 = jnp.float32
BF16 = jnp.bfloat16
HIGHEST = lax.Precision.HIGHEST

GROUP_COLUMNS = (0, 1, 2, -2, -1, 3, 4)


def bin_values():
    j = np.arange(NFREQ, dtype=np.float64)
    angles = 2.0 * math.pi * (np.arange(NDIR) + 0.5) / NDIR
    speeds = np.repeat(0.12 + 0.25 * (NFREQ - 1 - j) / (NFREQ - 1), NDIR)
    cosines, sines = np.tile(np.cos(angles), NFREQ), np.tile(np.sin(angles), NFREQ)
    strength = np.repeat(0.06 * (1.0 + j / (NFREQ - 1)), NDIR)
    wavenumber = np.repeat(0.02 * 1.15**j, NDIR)
    amplitude = 2.0 / math.sqrt(BINS)
    rows = (speeds * cosines, speeds * sines, strength, -wavenumber, amplitude * cosines, amplitude * sines)
    return np.stack(rows).astype(np.float32)


def stencils():
    lane = {}
    for group, column in enumerate(GROUP_COLUMNS):
        for r in range(ROWS):
            lane[column, r] = 16 * group + r
    for column in range(COLS):
        for k in range(2):
            lane[column, k - 2] = 112 + 2 * column + k
            lane[column, 16 + k] = 118 + 2 * column + k
    table = np.zeros((128, 256), np.float32)
    for r in range(ROWS):
        for face in range(COLS + 1):
            at = 16 * face + r
            for d, w in ((-2, -1), (-1, 5), (0, 2)):
                table[lane[face + d, r], at] += w
            for d, w in ((-1, 2), (0, 5), (1, -1)):
                table[lane[face + d, r], 128 + at] += w
        for column in range(COLS):
            at = 64 + 16 * column + r
            for d, w in ((-2, 1), (-1, -6), (0, 3), (1, 2)):
                table[lane[column, r + d], at] += w
            for d, w in ((-1, -2), (0, -3), (1, 6), (2, -1)):
                table[lane[column, r + d], 128 + at] += w
    return table


def lanes(rows=1):
    return lax.broadcasted_iota(jnp.int32, (rows, 128), 1)


def split_beside(x):
    upper = x.astype(BF16).astype(F32)
    return (upper + pltpu.roll(x - upper, 64, 1)).astype(BF16)


def pack_kernel(me, spec, mask, current, out, mask_out, zonal_out, stack, turned, turned2):
    sea = mask[...].astype(F32)
    masked = spec[...] * sea[None]
    stack[0:16, :] = masked[8]
    stack[16:32, :] = sea
    stack[32:128, :] = jnp.zeros((96, NLON), F32)
    for ref in (turned, turned2):
        ref[0:8, :] = jnp.zeros((8, 128), F32)
        ref[392:400, :] = jnp.zeros((8, 128), F32)
    turned[8:392, :] = masked[0:8].reshape(128, NLON).T
    turned2[8:392, :] = stack[...].T

    pair = lax.broadcasted_iota(jnp.int32, (32, 128), 0) // 2
    means = jnp.where(pair == lax.broadcasted_iota(jnp.int32, (32, 128), 1) % 16, 0.25, 0.0)
    sums = jnp.dot(current[...], means, precision=HIGHEST, preferred_element_type=F32)
    zonal = [sums[2 * c : 2 * c + 1] + sums[2 * c + 1 : 2 * c + 2] for c in range(COLS)]
    zonal_out[...] = jnp.concatenate(zonal + [jnp.zeros((5, 128), F32)], axis=0)

    def column(ref, offset):
        return ref[pl.ds(8 + offset, OWNERS, stride=COLS), :]

    group = lanes(OWNERS) // 16
    east = lax.broadcasted_iota(jnp.int32, (OWNERS, 128), 0) == me[0] + 1
    rest = jnp.where(east, zonal[2], zonal[0])
    sea_rows = jnp.zeros((OWNERS, 128), F32)
    for g, offset in enumerate(GROUP_COLUMNS):
        out[pl.ds(g, OWNERS, stride=8), :] = column(turned, offset)
        last = column(turned2, offset)
        rest = jnp.where(group == g, pltpu.roll(last, 16 * g, 1), rest)
        if g < COLS:
            sea_rows = jnp.where(group == g, pltpu.roll(last, (16 * g - 16) % 128, 1), sea_rows)
    out[pl.ds(7, OWNERS, stride=8), :] = rest
    mask_out[...] = sea_rows


def edges_kernel(arrived, to_above, to_below):
    def part(g):
        return arrived[pl.ds(g, OWNERS, stride=8), :]

    lane = lanes(OWNERS)
    inside = lane % 16
    rest = part(7)
    for ref, r in ((to_above, 14), (to_below, 0)):
        acc = jnp.zeros((OWNERS, 128), F32)
        for c in range(COLS):
            moved = pltpu.roll(part(c), (2 * c - r) % 128, 1)
            acc = jnp.where((inside >= 2 * c) & (inside < 2 * c + 2), moved, acc)
        for c in range(COLS):
            moved = pltpu.roll(rest, (6 + 2 * c - 16 * c - r) % 128, 1)
            acc = jnp.where((lane >= 6 + 2 * c) & (lane < 8 + 2 * c), moved, acc)
        ref[...] = acc


def points_kernel(
    me, arrived, from_below, from_above, masks, zonal, plus, minus, stencil, values,
    out, drift_out, first, source, middle, halves, speeds, plus_col, minus_col,
):
    device = me[0]
    lane = lanes(OWNERS)
    group = lane // 16

    below = arrived[pl.ds(8 * jnp.maximum(device - 1, 0) + 7, 1), :]
    above = arrived[pl.ds(8 * jnp.minimum(device + 1, OWNERS - 1) + 7, 1), :]
    lower = jnp.where(device > 0, pltpu.roll(below, 16, 1), 0.0)
    upper = jnp.where(device < OWNERS - 1, pltpu.roll(above, 64, 1), 0.0)
    lane1 = lanes()
    group1 = lane1 // 16
    columns = [zonal[c : c + 1, :] for c in range(COLS)]
    for c in range(COLS):
        lower = jnp.where(group1 == c + 1, columns[c], lower)
        upper = jnp.where(group1 == c, columns[c], upper)
    faces = jnp.where(lane1 < 64, 0.5 * (lower + upper), 0.0)
    sea = masks[pl.ds(device, 1), :]

    def chunk(t):
        return slice(128 * t, 128 * t + 128)

    for i in range(OWN):
        if i < 8:
            acc = jnp.zeros((OWNERS, 128), F32)
            for g in range(7):
                part = pltpu.roll(arrived[pl.ds(g, OWNERS, stride=8), :], (16 * g - 16 * i) % 128, 1)
                acc = jnp.where(group == g, part, acc)
        else:
            acc = arrived[pl.ds(7, OWNERS, stride=8), :]
        held = 16 * i if i < 8 else 6
        for ref, at in ((from_below, 112), (from_above, 118)):
            acc = jnp.where((lane >= at) & (lane < at + 6), pltpu.roll(ref[...], (at - held) % 128, 1), acc)
        middle[pl.ds(i, OWNERS, stride=OWN), :] = acc

    inner = lax.broadcasted_iota(jnp.int32, (128, 128), 0)
    for t in range(OWN):
        value = middle[chunk(t), :]
        upper_half = value.astype(BF16)
        lower_half = (value - upper_half.astype(F32)).astype(BF16)
        sums = jnp.dot(upper_half, stencil[...], preferred_element_type=F32) + jnp.dot(
            lower_half, stencil[...], preferred_element_type=F32
        )
        part = jnp.where(inner < 64, values[0:1, chunk(t)], values[1:2, chunk(t)])
        speeds[chunk(t), :] = jnp.where(inner == 127, values[2:3, chunk(t)], part).T
        for row, col in ((plus, plus_col), (minus, minus_col)):
            col[chunk(t), :] = jnp.broadcast_to(row[:, chunk(t)].astype(F32), (128, 128)).T
        speed = (speeds[chunk(t), :] + faces) * (1.0 / 6.0)
        flux = jnp.maximum(speed, 0.0) * sums[:, 0:128] + jnp.minimum(speed, 0.0) * sums[:, 128:256]
        change = (pltpu.roll(flux, 112, 1) - flux) + pltpu.roll(flux, 64, 1)
        moved = sea * (value - change)
        moved = jnp.where(lane < 48, moved, 0.0)
        first[chunk(t), :] = moved
        halves[chunk(t), :] = split_beside(moved)

    numbers = lax.broadcasted_iota(jnp.int32, (128, BINS), 1).astype(F32)

    def gathered(col, t):
        wide = jnp.concatenate([col[chunk(t), :]] * OWN, axis=1)
        chosen = jnp.where(wide == numbers, 1.0, 0.0).astype(BF16)
        both = jnp.dot(chosen, halves[...], preferred_element_type=F32)
        return both + pltpu.roll(both, 64, 1)

    for t in range(OWN):
        ahead = gathered(plus_col, t)
        behind = gathered(minus_col, t)
        f = first[chunk(t), :]
        strength = jnp.broadcast_to(speeds[chunk(t), 127:128], (128, 128))
        source[chunk(t), :] = strength * (f * f * (ahead + behind) - 2.0 * f * ahead * behind)
    for t in range(OWN):
        halves[chunk(t), :] = split_beside(source[chunk(t), :])
    for t in range(OWN):
        names = lax.broadcasted_iota(jnp.int32, (128, BINS), 0) + 128 * t
        hits = jnp.where(plus[...] == names, 1.0, 0.0) + jnp.where(minus[...] == names, 1.0, 0.0)
        both = jnp.dot(hits.astype(BF16), halves[...], preferred_element_type=F32)
        back = both + pltpu.roll(both, 64, 1)
        m = first[chunk(t), :] + (source[chunk(t), :] - 0.5 * back)
        middle[chunk(t), :] = jnp.where(lane < 48, m, 0.0)
    for t in range(OWN):
        halves[chunk(t), :] = split_beside(middle[chunk(t), :])
    level = lax.broadcasted_iota(jnp.int32, (LEV, BINS), 0).astype(F32) + 0.5
    decay = jnp.exp(level * values[3:4, :])
    table = jnp.concatenate([decay * values[4:5, :], decay * values[5:6, :]], axis=0)
    table_upper = table.astype(BF16)
    table_lower = (table - table_upper.astype(F32)).astype(BF16)
    sums = jnp.dot(table_upper, halves[...], preferred_element_type=F32)
    drift = sums + pltpu.roll(sums, 64, 1) + jnp.dot(table_lower, halves[...], preferred_element_type=F32)
    drift_out[...] = drift.T[0:48]

    for c in range(COLS):
        acc = jnp.zeros((OWNERS, 128), F32)
        for i in range(8):
            part = pltpu.roll(middle[pl.ds(i, OWNERS, stride=OWN), :], (16 * (i - c)) % 128, 1)
            acc = jnp.where(group == i, part, acc)
        out[pl.ds(c, OWNERS, stride=4), :] = acc
    acc = jnp.zeros((OWNERS, 128), F32)
    last = middle[pl.ds(8, OWNERS, stride=OWN), :]
    for c in range(COLS):
        acc = jnp.where(group == 2 * c, pltpu.roll(last, 16 * c, 1), acc)
        acc = jnp.where(group == 2 * c + 1, jnp.broadcast_to(columns[c], acc.shape), acc)
    out[pl.ds(3, OWNERS, stride=4), :] = acc


def unpack_kernel(arrived, drift, drift_low, drift_high, middle, zonal, low, high, turned, turned2):
    rest = arrived[pl.ds(3, OWNERS, stride=4), :]
    for c in range(COLS):
        turned[pl.ds(c, OWNERS, stride=COLS), :] = arrived[pl.ds(c, OWNERS, stride=4), :]
        turned2[pl.ds(c, OWNERS, stride=COLS), :] = pltpu.roll(rest, (128 - 32 * c) % 128, 1)
    middle[0:128, :] = turned[...].T
    rest = turned2[...].T
    middle[128:144, :] = rest[0:16]
    zonal[...] = rest[16:32]
    for i in range(OWN):
        low[2 * i : 2 * i + 2, :] = middle[16 * i : 16 * i + 2, :]
        high[2 * i : 2 * i + 2, :] = middle[16 * i + 14 : 16 * i + 16, :]
    for ref, r in ((low, 0), (high, 15)):
        pieces = [drift_low[r : r + 1, :]] + [drift[16 * c + r : 16 * c + r + 1, :] for c in range(COLS)]
        pieces += [drift_high[r : r + 1, :], jnp.zeros((1, 128), F32)]
        ref[18:19, :] = jnp.concatenate(pieces[0:3], axis=1)
        ref[19:20, :] = jnp.concatenate(pieces[3:6], axis=1)
        ref[20:24, :] = jnp.zeros((4, NLON), F32)


def inside_kernel(me, speeds, middle, zonal, mask, out, rows):
    first_bin = me[0] * OWN
    sea = mask[...].astype(F32)
    column = lax.broadcasted_iota(jnp.int32, (ROWS, NLON), 1)

    def beside(x, d):
        moved = pltpu.roll(x, (-d) % NLON, 1)
        return jnp.where((column + d >= 0) & (column + d < NLON), moved, 0.0)

    flow = zonal[...]
    lower_flow = 0.5 * (beside(flow, -1) + flow)
    upper_flow = 0.5 * (flow + beside(flow, 1))
    rows[0:8, :] = jnp.zeros((8, NLON), F32)
    rows[24:32, :] = jnp.zeros((8, NLON), F32)
    for i in range(OWN):
        f = middle[16 * i : 16 * i + 16, :]
        rows[8:24, :] = f
        along_x = speeds[first_bin + i]
        along_y = speeds[BINS + first_bin + i]
        r2, r1, u1, u2 = rows[6:22, :], rows[7:23, :], rows[9:25, :], rows[10:26, :]
        forward = jnp.maximum(along_y, 0.0) * (1.0 / 6.0)
        backward = jnp.minimum(along_y, 0.0) * (1.0 / 6.0)
        change = forward * ((r2 - 6.0 * r1) + (3.0 * f + 2.0 * u1)) + backward * (
            (6.0 * u1 - u2) - (2.0 * r1 + 3.0 * f)
        )
        a2, a1, b1, b2 = beside(f, -2), beside(f, -1), beside(f, 1), beside(f, 2)
        speed = (along_x + upper_flow) * (1.0 / 6.0)
        change = change + (
            jnp.maximum(speed, 0.0) * (5.0 * f + 2.0 * b1 - a1) + jnp.minimum(speed, 0.0) * (2.0 * f + 5.0 * b1 - b2)
        )
        speed = (along_x + lower_flow) * (1.0 / 6.0)
        change = change - (
            jnp.maximum(speed, 0.0) * (5.0 * a1 + 2.0 * f - a2) + jnp.minimum(speed, 0.0) * (2.0 * a1 + 5.0 * f - b1)
        )
        out[i] = sea * (f - change)


def final_kernel(me, speeds, inside, low, high, mask, drift, drift_low, drift_high, place, out, stokes, near):
    first_bin = me[0] * OWN
    sea = mask[...].astype(F32)
    out[...] = inside[...]
    for i in range(OWN):
        along_y = speeds[BINS + first_bin + i]
        forward = jnp.maximum(along_y, 0.0) * (1.0 / 6.0)
        backward = jnp.minimum(along_y, 0.0) * (1.0 / 6.0)
        r2, r1 = low[2 * i : 2 * i + 1, :], low[2 * i + 1 : 2 * i + 2, :]
        u1, u2 = high[2 * i : 2 * i + 1, :], high[2 * i + 1 : 2 * i + 2, :]
        lower = jnp.concatenate([forward * (r2 - 6.0 * r1) - backward * (2.0 * r1), forward * r1], axis=0)
        upper = jnp.concatenate([-backward * u1, forward * (2.0 * u1) + backward * (6.0 * u1 - u2)], axis=0)
        out[i, 0:2, :] = inside[i, 0:2, :] - sea[0:2] * lower
        out[i, 14:16, :] = inside[i, 14:16, :] - sea[14:16] * upper

    near[...] = jnp.zeros_like(near)
    near[0:16, :] = drift_low[...]
    near[16:64, :] = drift[...]
    near[64:80, :] = drift_high[...]
    for ref, at in ((low, 80), (high, 88)):
        for k in range(5):
            near[at + k : at + k + 1, :] = ref[18 + k // 3 : 19 + k // 3, 128 * (k % 3) : 128 * (k % 3) + 128]
    wanted = jnp.broadcast_to(place[...], (128, 256)).T[0:192]
    chosen = jnp.where(wanted == lanes(192).astype(F32), 1.0, 0.0).astype(BF16)
    rest = near[...]
    total = jnp.zeros((192, 128), F32)
    for _ in range(3):
        part = rest.astype(BF16)
        rest = rest - part.astype(F32)
        total = total + jnp.dot(chosen, part, preferred_element_type=F32)
    stokes[0] = total[:, 0:64]
    stokes[1] = total[:, 64:128]


def shapes(*sizes):
    return [jax.ShapeDtypeStruct(size, F32) for size in sizes]


def on_device(spectrum, sea_mask, current, partner_plus, partner_minus, source_map):
    values = bin_values()
    speed_list = values[0:2].reshape(-1)
    held_values = np.concatenate([values, np.zeros((2, BINS), np.float32)])
    stencil = stencils().astype(BF16)

    device = lax.axis_index("bins").reshape(1)
    up = [(i, i + 1) for i in range(BANDS - 1)]
    down = [(i + 1, i) for i in range(BANDS - 1)]
    east = [(i, i + 1) for i in range(OWNERS - 1)]
    west = [(i + 1, i) for i in range(OWNERS - 1)]

    smem = pl.BlockSpec(memory_space=pltpu.SMEM)
    vmem = pl.BlockSpec(memory_space=pltpu.VMEM)
    grant = pltpu.CompilerParams(vmem_limit_bytes=16 * 1024 * 1024)
    sent, masks, zonal = pl.pallas_call(
        pack_kernel,
        out_shape=shapes((8 * OWNERS, 128), (OWNERS, 128), (8, 128)),
        in_specs=[smem] + [vmem] * 3,
        scratch_shapes=[pltpu.VMEM((128, NLON), F32), pltpu.VMEM((400, 128), F32), pltpu.VMEM((400, 128), F32)],
        compiler_params=grant,
    )(device, spectrum, sea_mask, current)

    plus, minus, sent = lax.optimization_barrier((partner_plus, partner_minus, sent))
    arrived = lax.all_to_all(sent.reshape(OWNERS, 1, 1024), "bins", 0, 0).reshape(8 * OWNERS, 128)
    plus, minus = plus.reshape(1, BINS), minus.reshape(1, BINS)
    arrived, plus, minus = lax.optimization_barrier((arrived, plus, minus))
    to_above, to_below = pl.pallas_call(
        edges_kernel,
        out_shape=shapes((OWNERS, 128), (OWNERS, 128)),
        compiler_params=grant,
    )(arrived)
    from_below = lax.ppermute(to_above, "lat", up)
    from_above = lax.ppermute(to_below, "lat", down)

    big = pltpu.VMEM((BINS, 128), F32)
    sent, drift = pl.pallas_call(
        points_kernel,
        out_shape=shapes((4 * OWNERS, 128), (48, 128)),
        in_specs=[smem] + [vmem] * 9,
        scratch_shapes=[big, big, big, pltpu.VMEM((BINS, 128), BF16), big, big, big],
        compiler_params=pltpu.CompilerParams(vmem_limit_bytes=24 * 1024 * 1024),
    )(device, arrived, from_below, from_above, masks, zonal, plus, minus, jnp.asarray(stencil), jnp.asarray(held_values))

    arrived = lax.all_to_all(sent.reshape(OWNERS, 1, 512), "bins", 0, 0).reshape(4 * OWNERS, 128)
    drift_low = lax.ppermute(drift[32:48], "bins", east)
    drift_high = lax.ppermute(drift[0:16], "bins", west)

    middle, zonal_all, low, high = pl.pallas_call(
        unpack_kernel,
        out_shape=shapes((OWN * ROWS, NLON), (ROWS, NLON), (24, NLON), (24, NLON)),
        scratch_shapes=[pltpu.VMEM((NLON, 128), F32), pltpu.VMEM((NLON, 128), F32)],
        compiler_params=grant,
    )(arrived, drift, drift_low, drift_high)
    from_below = lax.ppermute(high, "lat", up)
    from_above = lax.ppermute(low, "lat", down)

    row = jnp.arange(32, dtype=jnp.int32)[None, :] // 2 + source_map // 3 - 1
    col = jnp.arange(6, dtype=jnp.int32)[:, None] // 2 + source_map % 3
    place = jnp.where(row < 0, 80 + col, jnp.where(row > 15, 88 + col, 16 * col + row))
    place = jnp.pad(place.reshape(1, 192), ((0, 0), (0, 64))).astype(F32)
    speed_refs = jnp.asarray(speed_list)
    inside = pl.pallas_call(
        inside_kernel,
        out_shape=jax.ShapeDtypeStruct((OWN, ROWS, NLON), F32),
        in_specs=[smem, smem] + [vmem] * 3,
        scratch_shapes=[pltpu.VMEM((32, NLON), F32)],
        compiler_params=grant,
        cost_estimate=pl.CostEstimate(flops=60 * OWN * ROWS * NLON, bytes_accessed=8 * OWN * ROWS * NLON, transcendentals=0),
    )(device, speed_refs, middle, zonal_all, sea_mask)
    second, stokes = pl.pallas_call(
        final_kernel,
        out_shape=shapes((OWN, ROWS, NLON), (2, 192, 64)),
        in_specs=[smem, smem] + [vmem] * 8,
        scratch_shapes=[pltpu.VMEM((128, 128), F32)],
        compiler_params=grant,
    )(device, speed_refs, inside, from_below, from_above, sea_mask, drift, drift_low, drift_high, place)
    return second, stokes.reshape(2, 6, 32, LEV).transpose(0, 3, 1, 2)


def solution(mesh):
    in_specs = (P("bins", "lat", None), P("lat", None), P("bins", "lat"), P(), P(), P("bins", "lat"))
    out_specs = (P("bins", "lat", None), P(None, None, "bins", "lat"))
    return jax.shard_map(on_device, mesh=mesh, in_specs=in_specs, out_specs=out_specs, check_vma=False)
```

```python
import math

import jax
import jax.numpy as jnp
import numpy as np
from jax import lax
from jax.experimental import pallas as pl
from jax.experimental.pallas import tpu as pltpu
from jax.sharding import PartitionSpec as P

NDIR = 36
NFREQ = 32
LEV = 64
BINS = NDIR * NFREQ
OWN = 9
ROWS = 16
NLON = 384
OWNERS = 128
BANDS = 4
COLS = 3
F32 = jnp.float32
BF16 = jnp.bfloat16
HIGHEST = lax.Precision.HIGHEST

GROUP_COLUMNS = (0, 1, 2, -2, -1, 3, 4)


def bin_values():
    j = np.arange(NFREQ, dtype=np.float64)
    angles = 2.0 * math.pi * (np.arange(NDIR) + 0.5) / NDIR
    speeds = np.repeat(0.12 + 0.25 * (NFREQ - 1 - j) / (NFREQ - 1), NDIR)
    cosines, sines = np.tile(np.cos(angles), NFREQ), np.tile(np.sin(angles), NFREQ)
    strength = np.repeat(0.06 * (1.0 + j / (NFREQ - 1)), NDIR)
    wavenumber = np.repeat(0.02 * 1.15**j, NDIR)
    amplitude = 2.0 / math.sqrt(BINS)
    rows = (speeds * cosines, speeds * sines, strength, -wavenumber, amplitude * cosines, amplitude * sines)
    return np.stack(rows).astype(np.float32)


def stencils():
    lane = {}
    for group, column in enumerate(GROUP_COLUMNS):
        for r in range(ROWS):
            lane[column, r] = 16 * group + r
    for column in range(COLS):
        for k in range(2):
            lane[column, k - 2] = 112 + 2 * column + k
            lane[column, 16 + k] = 118 + 2 * column + k
    table = np.zeros((128, 256), np.float32)
    for r in range(ROWS):
        for face in range(COLS + 1):
            at = 16 * face + r
            for d, w in ((-2, -1), (-1, 5), (0, 2)):
                table[lane[face + d, r], at] += w
            for d, w in ((-1, 2), (0, 5), (1, -1)):
                table[lane[face + d, r], 128 + at] += w
        for column in range(COLS):
            at = 64 + 16 * column + r
            for d, w in ((-2, 1), (-1, -6), (0, 3), (1, 2)):
                table[lane[column, r + d], at] += w
            for d, w in ((-1, -2), (0, -3), (1, 6), (2, -1)):
                table[lane[column, r + d], 128 + at] += w
    return table


def lanes(rows=1):
    return lax.broadcasted_iota(jnp.int32, (rows, 128), 1)


def split_beside(x):
    upper = x.astype(BF16).astype(F32)
    return (upper + pltpu.roll(x - upper, 64, 1)).astype(BF16)


def pack_kernel(spec, mask, current, out, mask_out, stack, turned, turned2):
    sea = mask[...].astype(F32)
    masked = spec[...] * sea[None]
    stack[0:16, :] = masked[8]
    stack[16:32, :] = sea
    stack[32:128, :] = jnp.zeros((96, NLON), F32)
    turned[...] = masked[0:8].reshape(128, NLON).T
    turned2[...] = stack[...].T

    pair = lax.broadcasted_iota(jnp.int32, (32, 128), 0) // 2
    means = jnp.where(pair == lax.broadcasted_iota(jnp.int32, (32, 128), 1) % 16, 0.25, 0.0)
    sums = jnp.dot(current[...], means, precision=HIGHEST, preferred_element_type=F32)
    group = lanes(OWNERS) // 16
    rest = jnp.zeros((OWNERS, 128), F32)
    sea_rows = jnp.zeros((OWNERS, 128), F32)
    for c in range(COLS):
        out[pl.ds(c, OWNERS, stride=4), :] = turned[pl.ds(c, OWNERS, stride=COLS), :]
        column = turned2[pl.ds(c, OWNERS, stride=COLS), :]
        zonal = sums[2 * c : 2 * c + 1] + sums[2 * c + 1 : 2 * c + 2]
        rest = jnp.where(group == 2 * c, pltpu.roll(column, 32 * c, 1), rest)
        rest = jnp.where(group == 2 * c + 1, jnp.broadcast_to(zonal, rest.shape), rest)
        sea_rows = jnp.where(group == c, pltpu.roll(column, (16 * c - 16) % 128, 1), sea_rows)
    out[pl.ds(3, OWNERS, stride=4), :] = rest
    mask_out[...] = sea_rows


def swapped(odd, first, second):
    return jnp.where(odd, second, first), jnp.where(odd, first, second)


def edges_kernel(device, band, arrived, columns_a, columns_b, rows_a, rows_b):
    def part(c):
        return arrived[pl.ds(c, OWNERS, stride=4), :]

    lane = lanes(OWNERS)
    group = lane // 16
    inside = lane % 16
    rest = part(3)

    odd = (device[0] & 1) == 1
    columns_a[0:128, :], columns_b[0:128, :] = swapped(odd, part(1), part(0))
    columns_a[128:256, :], columns_b[128:256, :] = swapped(odd, part(2), part(1))
    lasts = []
    for c in (1, 0):
        pair = jnp.where(
            group == 0, pltpu.roll(rest, (-32 * c) % 128, 1), pltpu.roll(rest, (16 - 32 * (c + 1)) % 128, 1)
        )
        last = jnp.zeros((32, 128), F32)
        for q in range(4):
            moved = pltpu.roll(pair[32 * q : 32 * q + 32], 32 * q, 1)
            last = jnp.where(group[0:32] // 2 == q, moved, last)
        lasts.append(last)
    columns_a[256:288, :], columns_b[256:288, :] = swapped(odd, *lasts)

    edges = []
    for r in (14, 0):
        acc = jnp.zeros((OWNERS, 128), F32)
        for c in range(COLS):
            moved = pltpu.roll(part(c), (2 * c - r) % 128, 1)
            acc = jnp.where((inside >= 2 * c) & (inside < 2 * c + 2), moved, acc)
        for c in range(COLS):
            moved = pltpu.roll(rest, (6 + 2 * c - 32 * c - r) % 128, 1)
            acc = jnp.where((lane >= 6 + 2 * c) & (lane < 8 + 2 * c), moved, acc)
        edges.append(acc)
    rows_a[...], rows_b[...] = swapped((band[0] & 1) == 1, *edges)


def points_kernel(
    me, band, arrived, columns_a, columns_b, rows_a, rows_b, masks, plus, minus, stencil, values,
    out, drift_out, drift_a, drift_b, first, source, middle, halves, speeds, plus_col, minus_col,
):
    device = me[0]
    odd = (device & 1) == 1
    rows_below, rows_above = swapped((band[0] & 1) == 1, rows_b[...], rows_a[...])

    def from_west(rows):
        return jnp.where(odd, columns_a[rows, :], columns_b[rows, :])

    def from_east(rows):
        return jnp.where(odd, columns_b[rows, :], columns_a[rows, :])

    lane = lanes(OWNERS)
    group = lane // 16

    flow = arrived[pl.ds(4 * device + 3, 1), :]
    below = arrived[pl.ds(4 * jnp.maximum(device - 1, 0) + 3, 1), :]
    above = arrived[pl.ds(4 * jnp.minimum(device + 1, OWNERS - 1) + 3, 1), :]
    lower = jnp.where(device > 0, pltpu.roll(below, 48, 1), 0.0)
    upper = jnp.where(device < OWNERS - 1, pltpu.roll(above, 32, 1), 0.0)
    lane1 = lanes()
    group1 = lane1 // 16
    for c in range(COLS):
        lower = jnp.where(group1 == c + 1, pltpu.roll(flow, (-16 * c) % 128, 1), lower)
        upper = jnp.where(group1 == c, pltpu.roll(flow, (-16 * (c + 1)) % 128, 1), upper)
    faces = jnp.where(lane1 < 64, 0.5 * (lower + upper), 0.0)
    sea = masks[pl.ds(device, 1), :]

    def chunk(t):
        return slice(128 * t, 128 * t + 128)

    for i in range(OWN):
        acc = jnp.zeros((OWNERS, 128), F32)
        for g in range(7):
            if i == 8:
                if g < 3:
                    part = pltpu.roll(arrived[pl.ds(3, OWNERS, stride=4), :], (-16 * g) % 128, 1)
                else:
                    side, at = (from_west, 48) if g < 5 else (from_east, 80)
                    piece = side(slice(256, 288))
                    part = jnp.concatenate([pltpu.roll(piece, (at - 32 * q) % 128, 1) for q in range(4)], axis=0)
            else:
                if g < 3:
                    part = arrived[pl.ds(g, OWNERS, stride=4), :]
                elif g < 5:
                    part = from_west(chunk(g - 3))
                else:
                    part = from_east(chunk(g - 5))
                part = pltpu.roll(part, (16 * g - 16 * i) % 128, 1)
            acc = jnp.where(group == g, part, acc)
        held = 16 * i if i < 8 else 6
        for beyond, at in ((rows_below, 112), (rows_above, 118)):
            acc = jnp.where((lane >= at) & (lane < at + 6), pltpu.roll(beyond, (at - held) % 128, 1), acc)
        middle[pl.ds(i, OWNERS, stride=OWN), :] = acc

    inner = lax.broadcasted_iota(jnp.int32, (128, 128), 0)
    for t in range(OWN):
        value = middle[chunk(t), :]
        upper_half = value.astype(BF16)
        lower_half = (value - upper_half.astype(F32)).astype(BF16)
        sums = jnp.dot(upper_half, stencil[...], preferred_element_type=F32) + jnp.dot(
            lower_half, stencil[...], preferred_element_type=F32
        )
        part = jnp.where(inner < 64, values[0:1, chunk(t)], values[1:2, chunk(t)])
        speeds[chunk(t), :] = jnp.where(inner == 127, values[2:3, chunk(t)], part).T
        for row, col in ((plus, plus_col), (minus, minus_col)):
            col[chunk(t), :] = jnp.broadcast_to(row[:, chunk(t)].astype(F32), (128, 128)).T
        speed = (speeds[chunk(t), :] + faces) * (1.0 / 6.0)
        flux = jnp.maximum(speed, 0.0) * sums[:, 0:128] + jnp.minimum(speed, 0.0) * sums[:, 128:256]
        change = (pltpu.roll(flux, 112, 1) - flux) + pltpu.roll(flux, 64, 1)
        moved = sea * (value - change)
        moved = jnp.where(lane < 48, moved, 0.0)
        first[chunk(t), :] = moved
        halves[chunk(t), :] = split_beside(moved)

    numbers = lax.broadcasted_iota(jnp.int32, (128, BINS), 1).astype(F32)

    def gathered(col, t):
        wide = jnp.concatenate([col[chunk(t), :]] * OWN, axis=1)
        chosen = jnp.where(wide == numbers, 1.0, 0.0).astype(BF16)
        both = jnp.dot(chosen, halves[...], preferred_element_type=F32)
        return both + pltpu.roll(both, 64, 1)

    for t in range(OWN):
        ahead = gathered(plus_col, t)
        behind = gathered(minus_col, t)
        f = first[chunk(t), :]
        strength = jnp.broadcast_to(speeds[chunk(t), 127:128], (128, 128))
        source[chunk(t), :] = strength * (f * f * (ahead + behind) - 2.0 * f * ahead * behind)
    for t in range(OWN):
        halves[chunk(t), :] = split_beside(source[chunk(t), :])
    for t in range(OWN):
        names = lax.broadcasted_iota(jnp.int32, (128, BINS), 0) + 128 * t
        hits = jnp.where(plus[...] == names, 1.0, 0.0) + jnp.where(minus[...] == names, 1.0, 0.0)
        both = jnp.dot(hits.astype(BF16), halves[...], preferred_element_type=F32)
        back = both + pltpu.roll(both, 64, 1)
        m = first[chunk(t), :] + (source[chunk(t), :] - 0.5 * back)
        middle[chunk(t), :] = jnp.where(lane < 48, m, 0.0)
    for t in range(OWN):
        halves[chunk(t), :] = split_beside(middle[chunk(t), :])
    level = lax.broadcasted_iota(jnp.int32, (LEV, BINS), 0).astype(F32) + 0.5
    decay = jnp.exp(level * values[3:4, :])
    table = jnp.concatenate([decay * values[4:5, :], decay * values[5:6, :]], axis=0)
    table_upper = table.astype(BF16)
    table_lower = (table - table_upper.astype(F32)).astype(BF16)
    sums = jnp.dot(table_upper, halves[...], preferred_element_type=F32)
    drift = sums + pltpu.roll(sums, 64, 1) + jnp.dot(table_lower, halves[...], preferred_element_type=F32)
    turned = drift.T[0:48]
    drift_out[...] = turned
    drift_a[...], drift_b[...] = swapped(odd, turned[32:48], turned[0:16])

    for c in range(COLS):
        acc = jnp.zeros((OWNERS, 128), F32)
        for i in range(8):
            part = pltpu.roll(middle[pl.ds(i, OWNERS, stride=OWN), :], (16 * (i - c)) % 128, 1)
            acc = jnp.where(group == i, part, acc)
        out[pl.ds(c, OWNERS, stride=4), :] = acc
    acc = jnp.broadcast_to(flow, (OWNERS, 128))
    last = middle[pl.ds(8, OWNERS, stride=OWN), :]
    for c in range(COLS):
        acc = jnp.where(group == 2 * c, pltpu.roll(last, 16 * c, 1), acc)
    out[pl.ds(3, OWNERS, stride=4), :] = acc


def unpack_kernel(
    device, band, arrived, drift, drift_a, drift_b, middle, zonal, near, rows_a, rows_b, low, high, turned, turned2
):
    rest = arrived[pl.ds(3, OWNERS, stride=4), :]
    for c in range(COLS):
        turned[pl.ds(c, OWNERS, stride=COLS), :] = arrived[pl.ds(c, OWNERS, stride=4), :]
        turned2[pl.ds(c, OWNERS, stride=COLS), :] = pltpu.roll(rest, (128 - 32 * c) % 128, 1)
    middle[0:128, :] = turned[...].T
    rest = turned2[...].T
    middle[128:144, :] = rest[0:16]
    zonal[...] = rest[16:32]
    for i in range(OWN):
        low[2 * i : 2 * i + 2, :] = middle[16 * i : 16 * i + 2, :]
        high[2 * i : 2 * i + 2, :] = middle[16 * i + 14 : 16 * i + 16, :]
    near[0:16, :], near[64:80, :] = swapped((device[0] & 1) == 1, drift_b[...], drift_a[...])
    near[16:64, :] = drift[...]
    for ref, r in ((low, 0), (high, 15)):
        pieces = [near[16 * k + r : 16 * k + r + 1, :] for k in range(5)] + [jnp.zeros((1, 128), F32)]
        ref[18:19, :] = jnp.concatenate(pieces[0:3], axis=1)
        ref[19:20, :] = jnp.concatenate(pieces[3:6], axis=1)
        ref[20:24, :] = jnp.zeros((4, NLON), F32)
    rows_a[...], rows_b[...] = swapped((band[0] & 1) == 1, high[...], low[...])


def inside_kernel(me, speeds, middle, zonal, mask, out, rows):
    first_bin = me[0] * OWN
    sea = mask[...].astype(F32)
    column = lax.broadcasted_iota(jnp.int32, (ROWS, NLON), 1)

    def beside(x, d):
        moved = pltpu.roll(x, (-d) % NLON, 1)
        return jnp.where((column + d >= 0) & (column + d < NLON), moved, 0.0)

    flow = zonal[...]
    lower_flow = 0.5 * (beside(flow, -1) + flow)
    upper_flow = 0.5 * (flow + beside(flow, 1))
    rows[0:8, :] = jnp.zeros((8, NLON), F32)
    rows[24:32, :] = jnp.zeros((8, NLON), F32)
    for i in range(OWN):
        f = middle[16 * i : 16 * i + 16, :]
        rows[8:24, :] = f
        along_x = speeds[first_bin + i]
        along_y = speeds[BINS + first_bin + i]
        r2, r1, u1, u2 = rows[6:22, :], rows[7:23, :], rows[9:25, :], rows[10:26, :]
        forward = jnp.maximum(along_y, 0.0) * (1.0 / 6.0)
        backward = jnp.minimum(along_y, 0.0) * (1.0 / 6.0)
        change = forward * ((r2 - 6.0 * r1) + (3.0 * f + 2.0 * u1)) + backward * (
            (6.0 * u1 - u2) - (2.0 * r1 + 3.0 * f)
        )
        a2, a1, b1, b2 = beside(f, -2), beside(f, -1), beside(f, 1), beside(f, 2)
        speed = (along_x + upper_flow) * (1.0 / 6.0)
        change = change + (
            jnp.maximum(speed, 0.0) * (5.0 * f + 2.0 * b1 - a1) + jnp.minimum(speed, 0.0) * (2.0 * f + 5.0 * b1 - b2)
        )
        speed = (along_x + lower_flow) * (1.0 / 6.0)
        change = change - (
            jnp.maximum(speed, 0.0) * (5.0 * a1 + 2.0 * f - a2) + jnp.minimum(speed, 0.0) * (2.0 * a1 + 5.0 * f - b1)
        )
        out[i] = sea * (f - change)


def final_kernel(me, band, speeds, inside, rows_a, rows_b, mask, drift, place, out, stokes, near, low, high):
    first_bin = me[0] * OWN
    sea = mask[...].astype(F32)
    low[...], high[...] = swapped((band[0] & 1) == 1, rows_b[...], rows_a[...])
    out[...] = inside[...]
    for i in range(OWN):
        along_y = speeds[BINS + first_bin + i]
        forward = jnp.maximum(along_y, 0.0) * (1.0 / 6.0)
        backward = jnp.minimum(along_y, 0.0) * (1.0 / 6.0)
        r2, r1 = low[2 * i : 2 * i + 1, :], low[2 * i + 1 : 2 * i + 2, :]
        u1, u2 = high[2 * i : 2 * i + 1, :], high[2 * i + 1 : 2 * i + 2, :]
        lower = jnp.concatenate([forward * (r2 - 6.0 * r1) - backward * (2.0 * r1), forward * r1], axis=0)
        upper = jnp.concatenate([-backward * u1, forward * (2.0 * u1) + backward * (6.0 * u1 - u2)], axis=0)
        out[i, 0:2, :] = inside[i, 0:2, :] - sea[0:2] * lower
        out[i, 14:16, :] = inside[i, 14:16, :] - sea[14:16] * upper

    near[0:80, :] = drift[...]
    near[80:128, :] = jnp.zeros((48, 128), F32)
    for ref, at in ((low, 80), (high, 88)):
        for k in range(5):
            near[at + k : at + k + 1, :] = ref[18 + k // 3 : 19 + k // 3, 128 * (k % 3) : 128 * (k % 3) + 128]
    wanted = jnp.broadcast_to(place[...], (128, 256)).T[0:192]
    chosen = jnp.where(wanted == lanes(192).astype(F32), 1.0, 0.0).astype(BF16)
    rest = near[...]
    total = jnp.zeros((192, 128), F32)
    for _ in range(3):
        part = rest.astype(BF16)
        rest = rest - part.astype(F32)
        total = total + jnp.dot(chosen, part, preferred_element_type=F32)
    stokes[0] = total[:, 0:64]
    stokes[1] = total[:, 64:128]


def shapes(*sizes):
    return [jax.ShapeDtypeStruct(size, F32) for size in sizes]


def on_device(spectrum, sea_mask, current, partner_plus, partner_minus, source_map):
    values = bin_values()
    speed_list = values[0:2].reshape(-1)
    held_values = np.concatenate([values, np.zeros((2, BINS), np.float32)])
    stencil = stencils().astype(BF16)

    device = lax.axis_index("bins").reshape(1)
    band = lax.axis_index("lat").reshape(1)

    def swap(x, axis, second):
        pairs = [(k, k + 1) for k in range(second, lax.axis_size(axis) - 1, 2)]
        return lax.ppermute(x, axis, pairs + [(j, i) for i, j in pairs])

    smem = pl.BlockSpec(memory_space=pltpu.SMEM)
    vmem = pl.BlockSpec(memory_space=pltpu.VMEM)
    grant = pltpu.CompilerParams(vmem_limit_bytes=16 * 1024 * 1024)
    sent, masks = pl.pallas_call(
        pack_kernel,
        out_shape=shapes((4 * OWNERS, 128), (OWNERS, 128)),
        scratch_shapes=[pltpu.VMEM((128, NLON), F32), pltpu.VMEM((NLON, 128), F32), pltpu.VMEM((NLON, 128), F32)],
        compiler_params=grant,
    )(spectrum, sea_mask, current)

    plus, minus, sent = lax.optimization_barrier((partner_plus, partner_minus, sent))
    arrived = lax.all_to_all(sent.reshape(OWNERS, 1, 512), "bins", 0, 0).reshape(4 * OWNERS, 128)
    plus, minus = plus.reshape(1, BINS), minus.reshape(1, BINS)
    arrived, plus, minus = lax.optimization_barrier((arrived, plus, minus))
    columns_a, columns_b, rows_a, rows_b = pl.pallas_call(
        edges_kernel,
        out_shape=shapes((288, 128), (288, 128), (OWNERS, 128), (OWNERS, 128)),
        in_specs=[smem, smem, vmem],
        compiler_params=grant,
    )(device, band, arrived)
    rows_b = swap(rows_b, "lat", 1)
    columns_b = swap(columns_b, "bins", 1)
    columns_a = swap(columns_a, "bins", 0)
    rows_a = swap(rows_a, "lat", 0)

    big = pltpu.VMEM((BINS, 128), F32)
    sent, drift, drift_a, drift_b = pl.pallas_call(
        points_kernel,
        out_shape=shapes((4 * OWNERS, 128), (48, 128), (16, 128), (16, 128)),
        in_specs=[smem, smem] + [vmem] * 10,
        scratch_shapes=[big, big, big, pltpu.VMEM((BINS, 128), BF16), big, big, big],
        compiler_params=pltpu.CompilerParams(vmem_limit_bytes=24 * 1024 * 1024),
    )(
        device, band, arrived, columns_a, columns_b, rows_a, rows_b, masks, plus, minus,
        jnp.asarray(stencil), jnp.asarray(held_values),
    )

    arrived = lax.all_to_all(sent.reshape(OWNERS, 1, 512), "bins", 0, 0).reshape(4 * OWNERS, 128)
    drift_b = swap(drift_b, "bins", 1)
    drift_a = swap(drift_a, "bins", 0)

    middle, zonal_all, near, rows_a, rows_b = pl.pallas_call(
        unpack_kernel,
        out_shape=shapes((OWN * ROWS, NLON), (ROWS, NLON), (80, 128), (24, NLON), (24, NLON)),
        in_specs=[smem, smem] + [vmem] * 4,
        scratch_shapes=[
            pltpu.VMEM((24, NLON), F32),
            pltpu.VMEM((24, NLON), F32),
            pltpu.VMEM((NLON, 128), F32),
            pltpu.VMEM((NLON, 128), F32),
        ],
        compiler_params=grant,
    )(device, band, arrived, drift, drift_a, drift_b)
    rows_b = swap(rows_b, "lat", 1)
    rows_a = swap(rows_a, "lat", 0)

    row = jnp.arange(32, dtype=jnp.int32)[None, :] // 2 + source_map // 3 - 1
    col = jnp.arange(6, dtype=jnp.int32)[:, None] // 2 + source_map % 3
    place = jnp.where(row < 0, 80 + col, jnp.where(row > 15, 88 + col, 16 * col + row))
    place = jnp.pad(place.reshape(1, 192), ((0, 0), (0, 64))).astype(F32)
    speed_refs = jnp.asarray(speed_list)
    inside = pl.pallas_call(
        inside_kernel,
        out_shape=jax.ShapeDtypeStruct((OWN, ROWS, NLON), F32),
        in_specs=[smem, smem] + [vmem] * 3,
        scratch_shapes=[pltpu.VMEM((32, NLON), F32)],
        compiler_params=grant,
        cost_estimate=pl.CostEstimate(flops=60 * OWN * ROWS * NLON, bytes_accessed=8 * OWN * ROWS * NLON, transcendentals=0),
    )(device, speed_refs, middle, zonal_all, sea_mask)
    second, stokes = pl.pallas_call(
        final_kernel,
        out_shape=shapes((OWN, ROWS, NLON), (2, 192, 64)),
        in_specs=[smem, smem, smem] + [vmem] * 6,
        scratch_shapes=[pltpu.VMEM((128, 128), F32), pltpu.VMEM((24, NLON), F32), pltpu.VMEM((24, NLON), F32)],
        compiler_params=grant,
    )(device, band, speed_refs, inside, rows_a, rows_b, sea_mask, near, place)
    return second, stokes.reshape(2, 6, 32, LEV).transpose(0, 3, 1, 2)


def solution(mesh):
    in_specs = (P("bins", "lat", None), P("lat", None), P("bins", "lat"), P(), P(), P("bins", "lat"))
    out_specs = (P("bins", "lat", None), P(None, None, "bins", "lat"))
    return jax.shard_map(on_device, mesh=mesh, in_specs=in_specs, out_specs=out_specs, check_vma=False)
```

```python
import math

import jax
import jax.numpy as jnp
import numpy as np
from jax import lax
from jax.experimental import pallas as pl
from jax.experimental.pallas import tpu as pltpu
from jax.sharding import PartitionSpec as P

NDIR = 36
NFREQ = 32
LEV = 64
BINS = NDIR * NFREQ
OWN = 9
ROWS = 16
NLON = 384
OWNERS = 128
BANDS = 4
COLS = 3
F32 = jnp.float32
BF16 = jnp.bfloat16
HIGHEST = lax.Precision.HIGHEST

GROUP_COLUMNS = (0, 1, 2, -2, -1, 3, 4)


def bin_values():
    j = np.arange(NFREQ, dtype=np.float64)
    angles = 2.0 * math.pi * (np.arange(NDIR) + 0.5) / NDIR
    speeds = np.repeat(0.12 + 0.25 * (NFREQ - 1 - j) / (NFREQ - 1), NDIR)
    cosines, sines = np.tile(np.cos(angles), NFREQ), np.tile(np.sin(angles), NFREQ)
    strength = np.repeat(0.06 * (1.0 + j / (NFREQ - 1)), NDIR)
    wavenumber = np.repeat(0.02 * 1.15**j, NDIR)
    amplitude = 2.0 / math.sqrt(BINS)
    rows = (speeds * cosines, speeds * sines, strength, -wavenumber, amplitude * cosines, amplitude * sines)
    return np.stack(rows).astype(np.float32)


def stencils():
    lane = {}
    for group, column in enumerate(GROUP_COLUMNS):
        for r in range(ROWS):
            lane[column, r] = 16 * group + r
    for column in range(COLS):
        for k in range(2):
            lane[column, k - 2] = 112 + 2 * column + k
            lane[column, 16 + k] = 118 + 2 * column + k
    table = np.zeros((128, 256), np.float32)
    for r in range(ROWS):
        for face in range(COLS + 1):
            at = 16 * face + r
            for d, w in ((-2, -1), (-1, 5), (0, 2)):
                table[lane[face + d, r], at] += w
            for d, w in ((-1, 2), (0, 5), (1, -1)):
                table[lane[face + d, r], 128 + at] += w
        for column in range(COLS):
            at = 64 + 16 * column + r
            for d, w in ((-2, 1), (-1, -6), (0, 3), (1, 2)):
                table[lane[column, r + d], at] += w
            for d, w in ((-1, -2), (0, -3), (1, 6), (2, -1)):
                table[lane[column, r + d], 128 + at] += w
    return table


def lanes(rows=1):
    return lax.broadcasted_iota(jnp.int32, (rows, 128), 1)


def split_beside(x):
    upper = x.astype(BF16).astype(F32)
    return (upper + pltpu.roll(x - upper, 64, 1)).astype(BF16)


def pack_kernel(spec, mask, current, out, mask_out, stack, turned, turned2):
    sea = mask[...].astype(F32)
    masked = spec[...] * sea[None]
    stack[0:16, :] = masked[8]
    stack[16:32, :] = sea
    stack[32:128, :] = jnp.zeros((96, NLON), F32)
    turned[...] = masked[0:8].reshape(128, NLON).T
    turned2[...] = stack[...].T

    pair = lax.broadcasted_iota(jnp.int32, (32, 128), 0) // 2
    means = jnp.where(pair == lax.broadcasted_iota(jnp.int32, (32, 128), 1) % 16, 0.25, 0.0)
    sums = jnp.dot(current[...], means, precision=HIGHEST, preferred_element_type=F32)
    group = lanes(OWNERS) // 16
    rest = jnp.zeros((OWNERS, 128), F32)
    sea_rows = jnp.zeros((OWNERS, 128), F32)
    for c in range(COLS):
        out[pl.ds(c, OWNERS, stride=4), :] = turned[pl.ds(c, OWNERS, stride=COLS), :]
        column = turned2[pl.ds(c, OWNERS, stride=COLS), :]
        zonal = sums[2 * c : 2 * c + 1] + sums[2 * c + 1 : 2 * c + 2]
        rest = jnp.where(group == 2 * c, pltpu.roll(column, 32 * c, 1), rest)
        rest = jnp.where(group == 2 * c + 1, jnp.broadcast_to(zonal, rest.shape), rest)
        sea_rows = jnp.where(group == c, pltpu.roll(column, (16 * c - 16) % 128, 1), sea_rows)
    out[pl.ds(3, OWNERS, stride=4), :] = rest
    mask_out[...] = sea_rows


def swapped(odd, first, second):
    return jnp.where(odd, second, first), jnp.where(odd, first, second)


def edges_kernel(device, band, arrived, rows_b, columns_b, columns_a, rows_a):
    def part(c):
        return arrived[pl.ds(c, OWNERS, stride=4), :]

    lane = lanes(OWNERS)
    group = lane // 16
    inside = lane % 16
    rest = part(3)

    odd = (device[0] & 1) == 1
    columns_a[0:128, :], columns_b[0:128, :] = swapped(odd, part(1), part(0))
    columns_a[128:256, :], columns_b[128:256, :] = swapped(odd, part(2), part(1))
    lasts = []
    for c in (1, 0):
        pair = jnp.where(
            group == 0, pltpu.roll(rest, (-32 * c) % 128, 1), pltpu.roll(rest, (16 - 32 * (c + 1)) % 128, 1)
        )
        last = jnp.zeros((32, 128), F32)
        for q in range(4):
            moved = pltpu.roll(pair[32 * q : 32 * q + 32], 32 * q, 1)
            last = jnp.where(group[0:32] // 2 == q, moved, last)
        lasts.append(last)
    columns_a[256:288, :], columns_b[256:288, :] = swapped(odd, *lasts)

    edges = []
    for r in (14, 0):
        acc = jnp.zeros((OWNERS, 128), F32)
        for c in range(COLS):
            moved = pltpu.roll(part(c), (2 * c - r) % 128, 1)
            acc = jnp.where((inside >= 2 * c) & (inside < 2 * c + 2), moved, acc)
        for c in range(COLS):
            moved = pltpu.roll(rest, (6 + 2 * c - 32 * c - r) % 128, 1)
            acc = jnp.where((lane >= 6 + 2 * c) & (lane < 8 + 2 * c), moved, acc)
        edges.append(acc)
    rows_a[...], rows_b[...] = swapped((band[0] & 1) == 1, *edges)


def points_kernel(
    me, band, arrived, rows_b, columns_b, columns_a, rows_a, sea_row, plus, minus, stencil, values,
    out, drift_out, drift_b, drift_a, first, source, middle, halves, speeds, plus_col, minus_col,
):
    device = me[0]
    odd = (device & 1) == 1
    rows_below, rows_above = swapped((band[0] & 1) == 1, rows_b[...], rows_a[...])

    def from_west(rows):
        return jnp.where(odd, columns_a[rows, :], columns_b[rows, :])

    def from_east(rows):
        return jnp.where(odd, columns_b[rows, :], columns_a[rows, :])

    lane = lanes(OWNERS)
    group = lane // 16

    flow = arrived[pl.ds(4 * device + 3, 1), :]
    below = arrived[pl.ds(4 * jnp.maximum(device - 1, 0) + 3, 1), :]
    above = arrived[pl.ds(4 * jnp.minimum(device + 1, OWNERS - 1) + 3, 1), :]
    lower = jnp.where(device > 0, pltpu.roll(below, 48, 1), 0.0)
    upper = jnp.where(device < OWNERS - 1, pltpu.roll(above, 32, 1), 0.0)
    lane1 = lanes()
    group1 = lane1 // 16
    for c in range(COLS):
        lower = jnp.where(group1 == c + 1, pltpu.roll(flow, (-16 * c) % 128, 1), lower)
        upper = jnp.where(group1 == c, pltpu.roll(flow, (-16 * (c + 1)) % 128, 1), upper)
    faces = jnp.where(lane1 < 64, 0.5 * (lower + upper), 0.0)
    sea = sea_row[...]

    def chunk(t):
        return slice(128 * t, 128 * t + 128)

    for i in range(OWN):
        acc = jnp.zeros((OWNERS, 128), F32)
        for g in range(7):
            if i == 8:
                if g < 3:
                    part = pltpu.roll(arrived[pl.ds(3, OWNERS, stride=4), :], (-16 * g) % 128, 1)
                else:
                    side, at = (from_west, 48) if g < 5 else (from_east, 80)
                    piece = side(slice(256, 288))
                    part = jnp.concatenate([pltpu.roll(piece, (at - 32 * q) % 128, 1) for q in range(4)], axis=0)
            else:
                if g < 3:
                    part = arrived[pl.ds(g, OWNERS, stride=4), :]
                elif g < 5:
                    part = from_west(chunk(g - 3))
                else:
                    part = from_east(chunk(g - 5))
                part = pltpu.roll(part, (16 * g - 16 * i) % 128, 1)
            acc = jnp.where(group == g, part, acc)
        held = 16 * i if i < 8 else 6
        for beyond, at in ((rows_below, 112), (rows_above, 118)):
            acc = jnp.where((lane >= at) & (lane < at + 6), pltpu.roll(beyond, (at - held) % 128, 1), acc)
        middle[pl.ds(i, OWNERS, stride=OWN), :] = acc

    inner = lax.broadcasted_iota(jnp.int32, (128, 128), 0)
    for t in range(OWN):
        value = middle[chunk(t), :]
        upper_half = value.astype(BF16)
        lower_half = (value - upper_half.astype(F32)).astype(BF16)
        sums = jnp.dot(upper_half, stencil[...], preferred_element_type=F32) + jnp.dot(
            lower_half, stencil[...], preferred_element_type=F32
        )
        part = jnp.where(inner < 64, values[0:1, chunk(t)], values[1:2, chunk(t)])
        speeds[chunk(t), :] = jnp.where(inner == 127, values[2:3, chunk(t)], part).T
        for row, col in ((plus, plus_col), (minus, minus_col)):
            col[chunk(t), :] = jnp.broadcast_to(row[:, chunk(t)].astype(F32), (128, 128)).T
        speed = (speeds[chunk(t), :] + faces) * (1.0 / 6.0)
        flux = jnp.maximum(speed, 0.0) * sums[:, 0:128] + jnp.minimum(speed, 0.0) * sums[:, 128:256]
        change = (pltpu.roll(flux, 112, 1) - flux) + pltpu.roll(flux, 64, 1)
        moved = sea * (value - change)
        moved = jnp.where(lane < 48, moved, 0.0)
        first[chunk(t), :] = moved
        halves[chunk(t), :] = split_beside(moved)

    numbers = lax.broadcasted_iota(jnp.int32, (128, BINS), 1).astype(F32)

    def gathered(col, t):
        wide = jnp.concatenate([col[chunk(t), :]] * OWN, axis=1)
        chosen = jnp.where(wide == numbers, 1.0, 0.0).astype(BF16)
        both = jnp.dot(chosen, halves[...], preferred_element_type=F32)
        return both + pltpu.roll(both, 64, 1)

    for t in range(OWN):
        ahead = gathered(plus_col, t)
        behind = gathered(minus_col, t)
        f = first[chunk(t), :]
        strength = jnp.broadcast_to(speeds[chunk(t), 127:128], (128, 128))
        source[chunk(t), :] = strength * (f * f * (ahead + behind) - 2.0 * f * ahead * behind)
    for t in range(OWN):
        halves[chunk(t), :] = split_beside(source[chunk(t), :])
    for t in range(OWN):
        names = lax.broadcasted_iota(jnp.int32, (128, BINS), 0) + 128 * t
        hits = jnp.where(plus[...] == names, 1.0, 0.0) + jnp.where(minus[...] == names, 1.0, 0.0)
        both = jnp.dot(hits.astype(BF16), halves[...], preferred_element_type=F32)
        back = both + pltpu.roll(both, 64, 1)
        m = first[chunk(t), :] + (source[chunk(t), :] - 0.5 * back)
        middle[chunk(t), :] = jnp.where(lane < 48, m, 0.0)
    for t in range(OWN):
        halves[chunk(t), :] = split_beside(middle[chunk(t), :])
    level = lax.broadcasted_iota(jnp.int32, (LEV, BINS), 0).astype(F32) + 0.5
    decay = jnp.exp(level * values[3:4, :])
    table = jnp.concatenate([decay * values[4:5, :], decay * values[5:6, :]], axis=0)
    table_upper = table.astype(BF16)
    table_lower = (table - table_upper.astype(F32)).astype(BF16)
    sums = jnp.dot(table_upper, halves[...], preferred_element_type=F32)
    drift = sums + pltpu.roll(sums, 64, 1) + jnp.dot(table_lower, halves[...], preferred_element_type=F32)
    turned = drift.T[0:48]
    drift_out[...] = turned
    drift_a[...], drift_b[...] = swapped(odd, turned[32:48], turned[0:16])

    for c in range(COLS):
        acc = jnp.zeros((OWNERS, 128), F32)
        for i in range(8):
            part = pltpu.roll(middle[pl.ds(i, OWNERS, stride=OWN), :], (16 * (i - c)) % 128, 1)
            acc = jnp.where(group == i, part, acc)
        out[pl.ds(c, OWNERS, stride=4), :] = acc
    acc = jnp.broadcast_to(flow, (OWNERS, 128))
    last = middle[pl.ds(8, OWNERS, stride=OWN), :]
    for c in range(COLS):
        acc = jnp.where(group == 2 * c, pltpu.roll(last, 16 * c, 1), acc)
    out[pl.ds(3, OWNERS, stride=4), :] = acc


def unpack_kernel(
    device, band, arrived, drift, drift_b, drift_a, middle, zonal, near, rows_b, rows_a, low, high, turned, turned2
):
    rest = arrived[pl.ds(3, OWNERS, stride=4), :]
    for c in range(COLS):
        turned[pl.ds(c, OWNERS, stride=COLS), :] = arrived[pl.ds(c, OWNERS, stride=4), :]
        turned2[pl.ds(c, OWNERS, stride=COLS), :] = pltpu.roll(rest, (128 - 32 * c) % 128, 1)
    middle[0:128, :] = turned[...].T
    rest = turned2[...].T
    middle[128:144, :] = rest[0:16]
    zonal[...] = rest[16:32]
    for i in range(OWN):
        low[2 * i : 2 * i + 2, :] = middle[16 * i : 16 * i + 2, :]
        high[2 * i : 2 * i + 2, :] = middle[16 * i + 14 : 16 * i + 16, :]
    near[0:16, :], near[64:80, :] = swapped((device[0] & 1) == 1, drift_b[...], drift_a[...])
    near[16:64, :] = drift[...]
    for ref, r in ((low, 0), (high, 15)):
        pieces = [near[16 * k + r : 16 * k + r + 1, :] for k in range(5)] + [jnp.zeros((1, 128), F32)]
        ref[18:19, :] = jnp.concatenate(pieces[0:3], axis=1)
        ref[19:20, :] = jnp.concatenate(pieces[3:6], axis=1)
        ref[20:24, :] = jnp.zeros((4, NLON), F32)
    rows_a[...], rows_b[...] = swapped((band[0] & 1) == 1, high[...], low[...])


def inside_kernel(me, speeds, middle, zonal, mask, out, rows):
    first_bin = me[0] * OWN
    sea = mask[...].astype(F32)
    column = lax.broadcasted_iota(jnp.int32, (ROWS, NLON), 1)

    def beside(x, d):
        moved = pltpu.roll(x, (-d) % NLON, 1)
        return jnp.where((column + d >= 0) & (column + d < NLON), moved, 0.0)

    flow = zonal[...]
    lower_flow = 0.5 * (beside(flow, -1) + flow)
    upper_flow = 0.5 * (flow + beside(flow, 1))
    rows[0:8, :] = jnp.zeros((8, NLON), F32)
    rows[24:32, :] = jnp.zeros((8, NLON), F32)
    for i in range(OWN):
        f = middle[16 * i : 16 * i + 16, :]
        rows[8:24, :] = f
        along_x = speeds[first_bin + i]
        along_y = speeds[BINS + first_bin + i]
        r2, r1, u1, u2 = rows[6:22, :], rows[7:23, :], rows[9:25, :], rows[10:26, :]
        forward = jnp.maximum(along_y, 0.0) * (1.0 / 6.0)
        backward = jnp.minimum(along_y, 0.0) * (1.0 / 6.0)
        change = forward * ((r2 - 6.0 * r1) + (3.0 * f + 2.0 * u1)) + backward * (
            (6.0 * u1 - u2) - (2.0 * r1 + 3.0 * f)
        )
        a2, a1, b1, b2 = beside(f, -2), beside(f, -1), beside(f, 1), beside(f, 2)
        speed = (along_x + upper_flow) * (1.0 / 6.0)
        change = change + (
            jnp.maximum(speed, 0.0) * (5.0 * f + 2.0 * b1 - a1) + jnp.minimum(speed, 0.0) * (2.0 * f + 5.0 * b1 - b2)
        )
        speed = (along_x + lower_flow) * (1.0 / 6.0)
        change = change - (
            jnp.maximum(speed, 0.0) * (5.0 * a1 + 2.0 * f - a2) + jnp.minimum(speed, 0.0) * (2.0 * a1 + 5.0 * f - b1)
        )
        out[i] = sea * (f - change)


def final_kernel(me, band, speeds, inside, rows_b, rows_a, mask, drift, place, out, stokes, near, low, high):
    first_bin = me[0] * OWN
    sea = mask[...].astype(F32)
    low[...], high[...] = swapped((band[0] & 1) == 1, rows_b[...], rows_a[...])
    out[...] = inside[...]
    for i in range(OWN):
        along_y = speeds[BINS + first_bin + i]
        forward = jnp.maximum(along_y, 0.0) * (1.0 / 6.0)
        backward = jnp.minimum(along_y, 0.0) * (1.0 / 6.0)
        r2, r1 = low[2 * i : 2 * i + 1, :], low[2 * i + 1 : 2 * i + 2, :]
        u1, u2 = high[2 * i : 2 * i + 1, :], high[2 * i + 1 : 2 * i + 2, :]
        lower = jnp.concatenate([forward * (r2 - 6.0 * r1) - backward * (2.0 * r1), forward * r1], axis=0)
        upper = jnp.concatenate([-backward * u1, forward * (2.0 * u1) + backward * (6.0 * u1 - u2)], axis=0)
        out[i, 0:2, :] = inside[i, 0:2, :] - sea[0:2] * lower
        out[i, 14:16, :] = inside[i, 14:16, :] - sea[14:16] * upper

    near[0:80, :] = drift[...]
    near[80:128, :] = jnp.zeros((48, 128), F32)
    for ref, at in ((low, 80), (high, 88)):
        for k in range(5):
            near[at + k : at + k + 1, :] = ref[18 + k // 3 : 19 + k // 3, 128 * (k % 3) : 128 * (k % 3) + 128]
    wanted = jnp.broadcast_to(place[...], (128, 256)).T[0:192]
    chosen = jnp.where(wanted == lanes(192).astype(F32), 1.0, 0.0).astype(BF16)
    rest = near[...]
    total = jnp.zeros((192, 128), F32)
    for _ in range(3):
        part = rest.astype(BF16)
        rest = rest - part.astype(F32)
        total = total + jnp.dot(chosen, part, preferred_element_type=F32)
    stokes[0] = total[:, 0:64]
    stokes[1] = total[:, 64:128]


def shapes(*sizes):
    return [jax.ShapeDtypeStruct(size, F32) for size in sizes]


def on_device(spectrum, sea_mask, current, partner_plus, partner_minus, source_map):
    values = bin_values()
    speed_list = values[0:2].reshape(-1)
    held_values = np.concatenate([values, np.zeros((2, BINS), np.float32)])
    stencil = stencils().astype(BF16)

    device = lax.axis_index("bins").reshape(1)
    band = lax.axis_index("lat").reshape(1)

    def swap(x, axis, second):
        pairs = [(k, k + 1) for k in range(second, lax.axis_size(axis) - 1, 2)]
        return lax.ppermute(x, axis, pairs + [(j, i) for i, j in pairs])

    smem = pl.BlockSpec(memory_space=pltpu.SMEM)
    vmem = pl.BlockSpec(memory_space=pltpu.VMEM)
    grant = pltpu.CompilerParams(vmem_limit_bytes=16 * 1024 * 1024)
    sent, masks = pl.pallas_call(
        pack_kernel,
        out_shape=shapes((4 * OWNERS, 128), (OWNERS, 128)),
        scratch_shapes=[pltpu.VMEM((128, NLON), F32), pltpu.VMEM((NLON, 128), F32), pltpu.VMEM((NLON, 128), F32)],
        compiler_params=pltpu.CompilerParams(vmem_limit_bytes=60 * 1024 * 1024),
    )(spectrum, sea_mask, current)

    plus, minus, sent, masks = lax.optimization_barrier((partner_plus, partner_minus, sent, masks))
    arrived = lax.all_to_all(sent.reshape(OWNERS, 1, 512), "bins", 0, 0).reshape(4 * OWNERS, 128)
    plus, minus = plus.reshape(1, BINS), minus.reshape(1, BINS)
    sea = lax.dynamic_slice(masks, (device[0], 0), (1, 128))
    arrived, plus, minus, sea = lax.optimization_barrier((arrived, plus, minus, sea))
    rows_b, columns_b, columns_a, rows_a = pl.pallas_call(
        edges_kernel,
        out_shape=shapes((OWNERS, 128), (288, 128), (288, 128), (OWNERS, 128)),
        in_specs=[smem, smem, vmem],
        compiler_params=grant,
    )(device, band, arrived)
    rows_b = swap(rows_b, "lat", 1)
    columns_b = swap(columns_b, "bins", 1)
    columns_a = swap(columns_a, "bins", 0)
    rows_a = swap(rows_a, "lat", 0)

    big = pltpu.VMEM((BINS, 128), F32)
    sent, drift, drift_b, drift_a = pl.pallas_call(
        points_kernel,
        out_shape=shapes((4 * OWNERS, 128), (48, 128), (16, 128), (16, 128)),
        in_specs=[smem, smem] + [vmem] * 10,
        scratch_shapes=[big, big, big, pltpu.VMEM((BINS, 128), BF16), big, big, big],
        compiler_params=pltpu.CompilerParams(vmem_limit_bytes=24 * 1024 * 1024),
    )(
        device, band, arrived, rows_b, columns_b, columns_a, rows_a, sea, plus, minus,
        jnp.asarray(stencil), jnp.asarray(held_values),
    )

    arrived = lax.all_to_all(sent.reshape(OWNERS, 1, 512), "bins", 0, 0).reshape(4 * OWNERS, 128)
    drift_b = swap(drift_b, "bins", 1)
    drift_a = swap(drift_a, "bins", 0)

    middle, zonal_all, near, rows_b, rows_a = pl.pallas_call(
        unpack_kernel,
        out_shape=shapes((OWN * ROWS, NLON), (ROWS, NLON), (80, 128), (24, NLON), (24, NLON)),
        in_specs=[smem, smem] + [vmem] * 4,
        scratch_shapes=[
            pltpu.VMEM((24, NLON), F32),
            pltpu.VMEM((24, NLON), F32),
            pltpu.VMEM((NLON, 128), F32),
            pltpu.VMEM((NLON, 128), F32),
        ],
        compiler_params=grant,
    )(device, band, arrived, drift, drift_b, drift_a)
    rows_b = swap(rows_b, "lat", 1)
    rows_a = swap(rows_a, "lat", 0)

    row = jnp.arange(32, dtype=jnp.int32)[None, :] // 2 + source_map // 3 - 1
    col = jnp.arange(6, dtype=jnp.int32)[:, None] // 2 + source_map % 3
    place = jnp.where(row < 0, 80 + col, jnp.where(row > 15, 88 + col, 16 * col + row))
    place = jnp.pad(place.reshape(1, 192), ((0, 0), (0, 64))).astype(F32)
    speed_refs = jnp.asarray(speed_list)
    inside = pl.pallas_call(
        inside_kernel,
        out_shape=jax.ShapeDtypeStruct((OWN, ROWS, NLON), F32),
        in_specs=[smem, smem] + [vmem] * 3,
        scratch_shapes=[pltpu.VMEM((32, NLON), F32)],
        compiler_params=grant,
        cost_estimate=pl.CostEstimate(flops=60 * OWN * ROWS * NLON, bytes_accessed=8 * OWN * ROWS * NLON, transcendentals=0),
    )(device, speed_refs, middle, zonal_all, sea_mask)
    second, stokes = pl.pallas_call(
        final_kernel,
        out_shape=shapes((OWN, ROWS, NLON), (2, 192, 64)),
        in_specs=[smem, smem, smem] + [vmem] * 6,
        scratch_shapes=[pltpu.VMEM((128, 128), F32), pltpu.VMEM((24, NLON), F32), pltpu.VMEM((24, NLON), F32)],
        compiler_params=grant,
    )(device, band, speed_refs, inside, rows_b, rows_a, sea_mask, near, place)
    return second, stokes.reshape(2, 6, 32, LEV).transpose(0, 3, 1, 2)


def solution(mesh):
    in_specs = (P("bins", "lat", None), P("lat", None), P("bins", "lat"), P(), P(), P("bins", "lat"))
    out_specs = (P("bins", "lat", None), P(None, None, "bins", "lat"))
    return jax.shard_map(on_device, mesh=mesh, in_specs=in_specs, out_specs=out_specs, check_vma=False)
```

```python
import math

import jax
import jax.numpy as jnp
import numpy as np
from jax import lax
from jax.experimental import pallas as pl
from jax.experimental.pallas import tpu as pltpu
from jax.sharding import PartitionSpec as P

NDIR = 36
NFREQ = 32
LEV = 64
BINS = NDIR * NFREQ
OWN = 9
ROWS = 16
NLON = 384
OWNERS = 128
BANDS = 4
COLS = 3
F32 = jnp.float32
BF16 = jnp.bfloat16
HIGHEST = lax.Precision.HIGHEST

GROUP_COLUMNS = (0, 1, 2, -2, -1, 3, 4)


def bin_values():
    j = np.arange(NFREQ, dtype=np.float64)
    angles = 2.0 * math.pi * (np.arange(NDIR) + 0.5) / NDIR
    speeds = np.repeat(0.12 + 0.25 * (NFREQ - 1 - j) / (NFREQ - 1), NDIR)
    cosines, sines = np.tile(np.cos(angles), NFREQ), np.tile(np.sin(angles), NFREQ)
    strength = np.repeat(0.06 * (1.0 + j / (NFREQ - 1)), NDIR)
    wavenumber = np.repeat(0.02 * 1.15**j, NDIR)
    amplitude = 2.0 / math.sqrt(BINS)
    rows = (speeds * cosines, speeds * sines, strength, -wavenumber, amplitude * cosines, amplitude * sines)
    return np.stack(rows).astype(np.float32)


def stencils():
    lane = {}
    for group, column in enumerate(GROUP_COLUMNS):
        for r in range(ROWS):
            lane[column, r] = 16 * group + r
    for column in range(COLS):
        for k in range(2):
            lane[column, k - 2] = 112 + 2 * column + k
            lane[column, 16 + k] = 118 + 2 * column + k
    table = np.zeros((128, 256), np.float32)
    for r in range(ROWS):
        for face in range(COLS + 1):
            at = 16 * face + r
            for d, w in ((-2, -1), (-1, 5), (0, 2)):
                table[lane[face + d, r], at] += w
            for d, w in ((-1, 2), (0, 5), (1, -1)):
                table[lane[face + d, r], 128 + at] += w
        for column in range(COLS):
            at = 64 + 16 * column + r
            for d, w in ((-2, 1), (-1, -6), (0, 3), (1, 2)):
                table[lane[column, r + d], at] += w
            for d, w in ((-1, -2), (0, -3), (1, 6), (2, -1)):
                table[lane[column, r + d], 128 + at] += w
    return table


def lanes(rows=1):
    return lax.broadcasted_iota(jnp.int32, (rows, 128), 1)


def split_into(ref, rows, x):
    upper = x.astype(BF16)
    ref[rows, 0:128] = upper
    ref[rows, 128:256] = (x - upper.astype(F32)).astype(BF16)


def joined(both):
    return both[:, 0:128] + both[:, 128:256]


def pack_kernel(spec, mask, current, out, mask_out, stack, turned, turned2):
    sea = mask[...].astype(F32)
    masked = spec[...] * sea[None]
    stack[0:16, :] = masked[8]
    stack[16:32, :] = sea
    stack[32:128, :] = jnp.zeros((96, NLON), F32)
    turned[...] = masked[0:8].reshape(128, NLON).T
    turned2[...] = stack[...].T

    pair = lax.broadcasted_iota(jnp.int32, (32, 128), 0) // 2
    means = jnp.where(pair == lax.broadcasted_iota(jnp.int32, (32, 128), 1) % 16, 0.25, 0.0)
    sums = jnp.dot(current[...], means, precision=HIGHEST, preferred_element_type=F32)
    group = lanes(OWNERS) // 16
    rest = jnp.zeros((OWNERS, 128), F32)
    sea_rows = jnp.zeros((OWNERS, 128), F32)
    for c in range(COLS):
        out[pl.ds(c, OWNERS, stride=4), :] = turned[pl.ds(c, OWNERS, stride=COLS), :]
        column = turned2[pl.ds(c, OWNERS, stride=COLS), :]
        zonal = sums[2 * c : 2 * c + 1] + sums[2 * c + 1 : 2 * c + 2]
        rest = jnp.where(group == 2 * c, pltpu.roll(column, 32 * c, 1), rest)
        rest = jnp.where(group == 2 * c + 1, jnp.broadcast_to(zonal, rest.shape), rest)
        sea_rows = jnp.where(group == c, pltpu.roll(column, (16 * c - 16) % 128, 1), sea_rows)
    out[pl.ds(3, OWNERS, stride=4), :] = rest
    mask_out[...] = sea_rows


def swapped(odd, first, second):
    return jnp.where(odd, second, first), jnp.where(odd, first, second)


def edges_kernel(device, band, arrived, rows_b, columns_b, columns_a, rows_a):
    def part(c):
        return arrived[pl.ds(c, OWNERS, stride=4), :]

    lane = lanes(OWNERS)
    group = lane // 16
    inside = lane % 16
    rest = part(3)

    odd = (device[0] & 1) == 1
    columns_a[0:128, :], columns_b[0:128, :] = swapped(odd, part(1), part(0))
    columns_a[128:256, :], columns_b[128:256, :] = swapped(odd, part(2), part(1))
    lasts = []
    for c in (1, 0):
        pair = jnp.where(
            group == 0, pltpu.roll(rest, (-32 * c) % 128, 1), pltpu.roll(rest, (16 - 32 * (c + 1)) % 128, 1)
        )
        last = jnp.zeros((32, 128), F32)
        for q in range(4):
            moved = pltpu.roll(pair[32 * q : 32 * q + 32], 32 * q, 1)
            last = jnp.where(group[0:32] // 2 == q, moved, last)
        lasts.append(last)
    columns_a[256:288, :], columns_b[256:288, :] = swapped(odd, *lasts)

    edges = []
    for r in (14, 0):
        acc = jnp.zeros((OWNERS, 128), F32)
        for c in range(COLS):
            moved = pltpu.roll(part(c), (2 * c - r) % 128, 1)
            acc = jnp.where((inside >= 2 * c) & (inside < 2 * c + 2), moved, acc)
        for c in range(COLS):
            moved = pltpu.roll(rest, (6 + 2 * c - 32 * c - r) % 128, 1)
            acc = jnp.where((lane >= 6 + 2 * c) & (lane < 8 + 2 * c), moved, acc)
        edges.append(acc)
    rows_a[...], rows_b[...] = swapped((band[0] & 1) == 1, *edges)


def points_kernel(
    me, band, arrived, rows_b, columns_b, columns_a, rows_a, sea_row, plus, minus, stencil, values,
    out, drift_out, drift_b, drift_a, first, source, middle, halves, speeds, plus_col, minus_col,
):
    device = me[0]
    odd = (device & 1) == 1
    rows_below, rows_above = swapped((band[0] & 1) == 1, rows_b[...], rows_a[...])

    def from_west(rows):
        return jnp.where(odd, columns_a[rows, :], columns_b[rows, :])

    def from_east(rows):
        return jnp.where(odd, columns_b[rows, :], columns_a[rows, :])

    lane = lanes(OWNERS)
    group = lane // 16

    flow = arrived[pl.ds(4 * device + 3, 1), :]
    below = arrived[pl.ds(4 * jnp.maximum(device - 1, 0) + 3, 1), :]
    above = arrived[pl.ds(4 * jnp.minimum(device + 1, OWNERS - 1) + 3, 1), :]
    lower = jnp.where(device > 0, pltpu.roll(below, 48, 1), 0.0)
    upper = jnp.where(device < OWNERS - 1, pltpu.roll(above, 32, 1), 0.0)
    lane1 = lanes()
    group1 = lane1 // 16
    for c in range(COLS):
        lower = jnp.where(group1 == c + 1, pltpu.roll(flow, (-16 * c) % 128, 1), lower)
        upper = jnp.where(group1 == c, pltpu.roll(flow, (-16 * (c + 1)) % 128, 1), upper)
    faces = jnp.where(lane1 < 64, 0.5 * (lower + upper), 0.0)
    sea = sea_row[...]

    def chunk(t):
        return slice(128 * t, 128 * t + 128)

    for g in range(3):
        source[chunk(g), :] = arrived[pl.ds(g, OWNERS, stride=4), :]
    for g in range(3, 7):
        source[chunk(g), :] = from_west(chunk(g - 3)) if g < 5 else from_east(chunk(g - 5))
    source[chunk(7), :] = arrived[pl.ds(3, OWNERS, stride=4), :]
    for i in range(OWN):
        acc = jnp.zeros((OWNERS, 128), F32)
        for g in range(7):
            if i == 8:
                if g < 3:
                    part = pltpu.roll(source[chunk(7), :], (-16 * g) % 128, 1)
                else:
                    side, at = (from_west, 48) if g < 5 else (from_east, 80)
                    piece = side(slice(256, 288))
                    part = jnp.concatenate([pltpu.roll(piece, (at - 32 * q) % 128, 1) for q in range(4)], axis=0)
            else:
                part = pltpu.roll(source[chunk(g), :], (16 * g - 16 * i) % 128, 1)
            acc = jnp.where(group == g, part, acc)
        held = 16 * i if i < 8 else 6
        for beyond, at in ((rows_below, 112), (rows_above, 118)):
            acc = jnp.where((lane >= at) & (lane < at + 6), pltpu.roll(beyond, (at - held) % 128, 1), acc)
        middle[pl.ds(i, OWNERS, stride=OWN), :] = acc

    inner = lax.broadcasted_iota(jnp.int32, (128, 128), 0)
    for t in range(OWN):
        value = middle[chunk(t), :]
        upper_half = value.astype(BF16)
        lower_half = (value - upper_half.astype(F32)).astype(BF16)
        sums = jnp.dot(upper_half, stencil[...], preferred_element_type=F32) + jnp.dot(
            lower_half, stencil[...], preferred_element_type=F32
        )
        part = jnp.where(inner < 64, values[0:1, chunk(t)], values[1:2, chunk(t)])
        speeds[chunk(t), :] = jnp.where(inner == 127, values[2:3, chunk(t)], part).T
        for row, col in ((plus, plus_col), (minus, minus_col)):
            col[chunk(t), :] = jnp.broadcast_to(row[:, chunk(t)].astype(F32), (128, 128)).T
        speed = (speeds[chunk(t), :] + faces) * (1.0 / 6.0)
        flux = jnp.maximum(speed, 0.0) * sums[:, 0:128] + jnp.minimum(speed, 0.0) * sums[:, 128:256]
        change = (pltpu.roll(flux, 112, 1) - flux) + pltpu.roll(flux, 64, 1)
        moved = sea * (value - change)
        first[chunk(t), :] = moved
        split_into(halves, chunk(t), moved)

    numbers = lax.broadcasted_iota(jnp.int32, (128, BINS), 1).astype(jnp.int16)
    one, none = jnp.ones((128, BINS), BF16), jnp.zeros((128, BINS), BF16)

    def gathered(col, t):
        wide = jnp.concatenate([col[chunk(t), :].astype(jnp.int32).astype(jnp.int16)] * OWN, axis=1)
        chosen = jnp.where(wide == numbers, one, none)
        return joined(jnp.dot(chosen, halves[...], preferred_element_type=F32))

    for t in range(OWN):
        ahead = gathered(plus_col, t)
        behind = gathered(minus_col, t)
        f = first[chunk(t), :]
        strength = jnp.broadcast_to(speeds[chunk(t), 127:128], (128, 128))
        source[chunk(t), :] = strength * (f * f * (ahead + behind) - 2.0 * f * ahead * behind)
    for t in range(OWN):
        split_into(halves, chunk(t), source[chunk(t), :])
    plus_wide = jnp.broadcast_to(plus[...], (128, BINS)).astype(jnp.int16)
    minus_wide = jnp.broadcast_to(minus[...], (128, BINS)).astype(jnp.int16)
    for t in range(OWN):
        names = (lax.broadcasted_iota(jnp.int32, (128, BINS), 0) + 128 * t).astype(jnp.int16)
        hits = jnp.where(plus_wide == names, one, none) + jnp.where(minus_wide == names, one, none)
        back = joined(jnp.dot(hits, halves[...], preferred_element_type=F32))
        middle[chunk(t), :] = first[chunk(t), :] + (source[chunk(t), :] - 0.5 * back)
    for t in range(OWN):
        split_into(halves, chunk(t), middle[chunk(t), :])
    level = lax.broadcasted_iota(jnp.int32, (LEV, BINS), 0).astype(F32) + 0.5
    decay = jnp.exp(level * values[3:4, :])
    table = jnp.concatenate([decay * values[4:5, :], decay * values[5:6, :]], axis=0)
    table_upper = table.astype(BF16)
    table_lower = (table - table_upper.astype(F32)).astype(BF16)
    drift = joined(jnp.dot(table_upper, halves[...], preferred_element_type=F32))
    drift = drift + jnp.dot(table_lower, halves[:, 0:128], preferred_element_type=F32)
    turned = drift.T[0:48]
    drift_out[...] = turned
    drift_a[...], drift_b[...] = swapped(odd, turned[32:48], turned[0:16])

    accs = [jnp.zeros((OWNERS, 128), F32)] * COLS
    for i in range(8):
        value = middle[pl.ds(i, OWNERS, stride=OWN), :]
        for c in range(COLS):
            accs[c] = jnp.where(group == i, pltpu.roll(value, (16 * (i - c)) % 128, 1), accs[c])
    for c in range(COLS):
        out[pl.ds(c, OWNERS, stride=4), :] = accs[c]
    acc = jnp.broadcast_to(flow, (OWNERS, 128))
    last = middle[pl.ds(8, OWNERS, stride=OWN), :]
    for c in range(COLS):
        acc = jnp.where(group == 2 * c, pltpu.roll(last, 16 * c, 1), acc)
    out[pl.ds(3, OWNERS, stride=4), :] = acc


def unpack_kernel(
    device, band, arrived, drift, drift_b, drift_a, middle, zonal, near, rows_b, rows_a, low, high, turned, turned2
):
    rest = arrived[pl.ds(3, OWNERS, stride=4), :]
    for c in range(COLS):
        turned[pl.ds(c, OWNERS, stride=COLS), :] = arrived[pl.ds(c, OWNERS, stride=4), :]
        turned2[pl.ds(c, OWNERS, stride=COLS), :] = pltpu.roll(rest, (128 - 32 * c) % 128, 1)
    middle[0:128, :] = turned[...].T
    rest = turned2[...].T
    middle[128:144, :] = rest[0:16]
    zonal[...] = rest[16:32]
    for i in range(OWN):
        low[2 * i : 2 * i + 2, :] = middle[16 * i : 16 * i + 2, :]
        high[2 * i : 2 * i + 2, :] = middle[16 * i + 14 : 16 * i + 16, :]
    near[0:16, :], near[64:80, :] = swapped((device[0] & 1) == 1, drift_b[...], drift_a[...])
    near[16:64, :] = drift[...]
    for ref, r in ((low, 0), (high, 15)):
        pieces = [near[16 * k + r : 16 * k + r + 1, :] for k in range(5)] + [jnp.zeros((1, 128), F32)]
        ref[18:19, :] = jnp.concatenate(pieces[0:3], axis=1)
        ref[19:20, :] = jnp.concatenate(pieces[3:6], axis=1)
        ref[20:24, :] = jnp.zeros((4, NLON), F32)
    rows_a[...], rows_b[...] = swapped((band[0] & 1) == 1, high[...], low[...])


def inside_kernel(me, speeds, middle, zonal, mask, out, rows):
    first_bin = me[0] * OWN
    sea = mask[...].astype(F32)
    column = lax.broadcasted_iota(jnp.int32, (ROWS, NLON), 1)

    def beside(x, d):
        moved = pltpu.roll(x, (-d) % NLON, 1)
        return jnp.where((column + d >= 0) & (column + d < NLON), moved, 0.0)

    flow = zonal[...]
    lower_flow = 0.5 * (beside(flow, -1) + flow)
    upper_flow = 0.5 * (flow + beside(flow, 1))
    rows[0:8, :] = jnp.zeros((8, NLON), F32)
    rows[24:32, :] = jnp.zeros((8, NLON), F32)
    for i in range(OWN):
        f = middle[16 * i : 16 * i + 16, :]
        rows[8:24, :] = f
        along_x = speeds[first_bin + i]
        along_y = speeds[BINS + first_bin + i]
        r2, r1, u1, u2 = rows[6:22, :], rows[7:23, :], rows[9:25, :], rows[10:26, :]
        forward = jnp.maximum(along_y, 0.0) * (1.0 / 6.0)
        backward = jnp.minimum(along_y, 0.0) * (1.0 / 6.0)
        change = forward * ((r2 - 6.0 * r1) + (3.0 * f + 2.0 * u1)) + backward * (
            (6.0 * u1 - u2) - (2.0 * r1 + 3.0 * f)
        )
        a2, a1, b1, b2 = beside(f, -2), beside(f, -1), beside(f, 1), beside(f, 2)
        speed = (along_x + upper_flow) * (1.0 / 6.0)
        change = change + (
            jnp.maximum(speed, 0.0) * (5.0 * f + 2.0 * b1 - a1) + jnp.minimum(speed, 0.0) * (2.0 * f + 5.0 * b1 - b2)
        )
        speed = (along_x + lower_flow) * (1.0 / 6.0)
        change = change - (
            jnp.maximum(speed, 0.0) * (5.0 * a1 + 2.0 * f - a2) + jnp.minimum(speed, 0.0) * (2.0 * a1 + 5.0 * f - b1)
        )
        out[i] = sea * (f - change)


def final_kernel(me, band, speeds, inside, rows_b, rows_a, mask, drift, place, out, stokes, near, low, high):
    first_bin = me[0] * OWN
    sea = mask[...].astype(F32)
    low[...], high[...] = swapped((band[0] & 1) == 1, rows_b[...], rows_a[...])
    out[...] = inside[...]
    for i in range(OWN):
        along_y = speeds[BINS + first_bin + i]
        forward = jnp.maximum(along_y, 0.0) * (1.0 / 6.0)
        backward = jnp.minimum(along_y, 0.0) * (1.0 / 6.0)
        r2, r1 = low[2 * i : 2 * i + 1, :], low[2 * i + 1 : 2 * i + 2, :]
        u1, u2 = high[2 * i : 2 * i + 1, :], high[2 * i + 1 : 2 * i + 2, :]
        lower = jnp.concatenate([forward * (r2 - 6.0 * r1) - backward * (2.0 * r1), forward * r1], axis=0)
        upper = jnp.concatenate([-backward * u1, forward * (2.0 * u1) + backward * (6.0 * u1 - u2)], axis=0)
        out[i, 0:2, :] = inside[i, 0:2, :] - sea[0:2] * lower
        out[i, 14:16, :] = inside[i, 14:16, :] - sea[14:16] * upper

    near[0:80, :] = drift[...]
    near[80:128, :] = jnp.zeros((48, 128), F32)
    for ref, at in ((low, 80), (high, 88)):
        for k in range(5):
            near[at + k : at + k + 1, :] = ref[18 + k // 3 : 19 + k // 3, 128 * (k % 3) : 128 * (k % 3) + 128]
    wanted = jnp.broadcast_to(place[...], (128, 256)).T[0:192]
    chosen = jnp.where(wanted == lanes(192).astype(F32), 1.0, 0.0).astype(BF16)
    rest = near[...]
    total = jnp.zeros((192, 128), F32)
    for _ in range(3):
        part = rest.astype(BF16)
        rest = rest - part.astype(F32)
        total = total + jnp.dot(chosen, part, preferred_element_type=F32)
    stokes[0] = total[:, 0:64]
    stokes[1] = total[:, 64:128]


def shapes(*sizes):
    return [jax.ShapeDtypeStruct(size, F32) for size in sizes]


def on_device(spectrum, sea_mask, current, partner_plus, partner_minus, source_map):
    values = bin_values()
    speed_list = values[0:2].reshape(-1)
    held_values = np.concatenate([values, np.zeros((2, BINS), np.float32)])
    stencil = stencils().astype(BF16)

    device = lax.axis_index("bins").reshape(1)
    band = lax.axis_index("lat").reshape(1)

    def swap(x, axis, second):
        pairs = [(k, k + 1) for k in range(second, lax.axis_size(axis) - 1, 2)]
        return lax.ppermute(x, axis, pairs + [(j, i) for i, j in pairs])

    smem = pl.BlockSpec(memory_space=pltpu.SMEM)
    vmem = pl.BlockSpec(memory_space=pltpu.VMEM)
    grant = pltpu.CompilerParams(vmem_limit_bytes=16 * 1024 * 1024)
    sent, masks = pl.pallas_call(
        pack_kernel,
        out_shape=shapes((4 * OWNERS, 128), (OWNERS, 128)),
        scratch_shapes=[pltpu.VMEM((128, NLON), F32), pltpu.VMEM((NLON, 128), F32), pltpu.VMEM((NLON, 128), F32)],
        compiler_params=pltpu.CompilerParams(vmem_limit_bytes=60 * 1024 * 1024),
    )(spectrum, sea_mask, current)

    plus, minus, sent, masks = lax.optimization_barrier((partner_plus, partner_minus, sent, masks))
    arrived = lax.all_to_all(sent.reshape(OWNERS, 1, 512), "bins", 0, 0).reshape(4 * OWNERS, 128)
    plus, minus = plus.reshape(1, BINS), minus.reshape(1, BINS)
    sea = lax.dynamic_slice(masks, (device[0], 0), (1, 128))
    arrived, plus, minus, sea = lax.optimization_barrier((arrived, plus, minus, sea))
    rows_b, columns_b, columns_a, rows_a = pl.pallas_call(
        edges_kernel,
        out_shape=shapes((OWNERS, 128), (288, 128), (288, 128), (OWNERS, 128)),
        in_specs=[smem, smem, vmem],
        compiler_params=grant,
    )(device, band, arrived)
    rows_b = swap(rows_b, "lat", 1)
    columns_b = swap(columns_b, "bins", 1)
    columns_a = swap(columns_a, "bins", 0)
    rows_a = swap(rows_a, "lat", 0)

    big = pltpu.VMEM((BINS, 128), F32)
    sent, drift, drift_b, drift_a = pl.pallas_call(
        points_kernel,
        out_shape=shapes((4 * OWNERS, 128), (48, 128), (16, 128), (16, 128)),
        in_specs=[smem, smem] + [vmem] * 10,
        scratch_shapes=[big, big, big, pltpu.VMEM((BINS, 256), BF16), big, big, big],
        compiler_params=pltpu.CompilerParams(vmem_limit_bytes=24 * 1024 * 1024),
    )(
        device, band, arrived, rows_b, columns_b, columns_a, rows_a, sea, plus, minus,
        jnp.asarray(stencil), jnp.asarray(held_values),
    )

    arrived = lax.all_to_all(sent.reshape(OWNERS, 1, 512), "bins", 0, 0).reshape(4 * OWNERS, 128)
    drift_b = swap(drift_b, "bins", 1)
    drift_a = swap(drift_a, "bins", 0)

    middle, zonal_all, near, rows_b, rows_a = pl.pallas_call(
        unpack_kernel,
        out_shape=shapes((OWN * ROWS, NLON), (ROWS, NLON), (80, 128), (24, NLON), (24, NLON)),
        in_specs=[smem, smem] + [vmem] * 4,
        scratch_shapes=[
            pltpu.VMEM((24, NLON), F32),
            pltpu.VMEM((24, NLON), F32),
            pltpu.VMEM((NLON, 128), F32),
            pltpu.VMEM((NLON, 128), F32),
        ],
        compiler_params=grant,
    )(device, band, arrived, drift, drift_b, drift_a)
    rows_b = swap(rows_b, "lat", 1)
    rows_a = swap(rows_a, "lat", 0)

    row = jnp.arange(32, dtype=jnp.int32)[None, :] // 2 + source_map // 3 - 1
    col = jnp.arange(6, dtype=jnp.int32)[:, None] // 2 + source_map % 3
    place = jnp.where(row < 0, 80 + col, jnp.where(row > 15, 88 + col, 16 * col + row))
    place = jnp.pad(place.reshape(1, 192), ((0, 0), (0, 64))).astype(F32)
    speed_refs = jnp.asarray(speed_list)
    inside = pl.pallas_call(
        inside_kernel,
        out_shape=jax.ShapeDtypeStruct((OWN, ROWS, NLON), F32),
        in_specs=[smem, smem] + [vmem] * 3,
        scratch_shapes=[pltpu.VMEM((32, NLON), F32)],
        compiler_params=grant,
        cost_estimate=pl.CostEstimate(flops=60 * OWN * ROWS * NLON, bytes_accessed=8 * OWN * ROWS * NLON, transcendentals=0),
    )(device, speed_refs, middle, zonal_all, sea_mask)
    second, stokes = pl.pallas_call(
        final_kernel,
        out_shape=shapes((OWN, ROWS, NLON), (2, 192, 64)),
        in_specs=[smem, smem, smem] + [vmem] * 6,
        scratch_shapes=[pltpu.VMEM((128, 128), F32), pltpu.VMEM((24, NLON), F32), pltpu.VMEM((24, NLON), F32)],
        compiler_params=grant,
    )(device, band, speed_refs, inside, rows_b, rows_a, sea_mask, near, place)
    return second, stokes.reshape(2, 6, 32, LEV).transpose(0, 3, 1, 2)


def solution(mesh):
    in_specs = (P("bins", "lat", None), P("lat", None), P("bins", "lat"), P(), P(), P("bins", "lat"))
    out_specs = (P("bins", "lat", None), P(None, None, "bins", "lat"))
    return jax.shard_map(on_device, mesh=mesh, in_specs=in_specs, out_specs=out_specs, check_vma=False)
```

```python
import math

import jax
import jax.numpy as jnp
import numpy as np
from jax import lax
from jax.experimental import pallas as pl
from jax.experimental.pallas import tpu as pltpu
from jax.sharding import PartitionSpec as P

NDIR = 36
NFREQ = 32
LEV = 64
BINS = NDIR * NFREQ
OWN = 9
ROWS = 16
NLON = 384
OWNERS = 128
BANDS = 4
COLS = 3
F32 = jnp.float32
BF16 = jnp.bfloat16
HIGHEST = lax.Precision.HIGHEST

GROUP_COLUMNS = (0, 1, 2, -2, -1, 3, 4)


def bin_values():
    j = np.arange(NFREQ, dtype=np.float64)
    angles = 2.0 * math.pi * (np.arange(NDIR) + 0.5) / NDIR
    speeds = np.repeat(0.12 + 0.25 * (NFREQ - 1 - j) / (NFREQ - 1), NDIR)
    cosines, sines = np.tile(np.cos(angles), NFREQ), np.tile(np.sin(angles), NFREQ)
    strength = np.repeat(0.06 * (1.0 + j / (NFREQ - 1)), NDIR)
    wavenumber = np.repeat(0.02 * 1.15**j, NDIR)
    amplitude = 2.0 / math.sqrt(BINS)
    rows = (speeds * cosines, speeds * sines, strength, -wavenumber, amplitude * cosines, amplitude * sines)
    return np.stack(rows).astype(np.float32)


def stencils():
    lane = {}
    for group, column in enumerate(GROUP_COLUMNS):
        for r in range(ROWS):
            lane[column, r] = 16 * group + r
    for column in range(COLS):
        for k in range(2):
            lane[column, k - 2] = 112 + 2 * column + k
            lane[column, 16 + k] = 118 + 2 * column + k
    table = np.zeros((128, 256), np.float32)
    for r in range(ROWS):
        for face in range(COLS + 1):
            at = 16 * face + r
            for d, w in ((-2, -1), (-1, 5), (0, 2)):
                table[lane[face + d, r], at] += w
            for d, w in ((-1, 2), (0, 5), (1, -1)):
                table[lane[face + d, r], 128 + at] += w
        for column in range(COLS):
            at = 64 + 16 * column + r
            for d, w in ((-2, 1), (-1, -6), (0, 3), (1, 2)):
                table[lane[column, r + d], at] += w
            for d, w in ((-1, -2), (0, -3), (1, 6), (2, -1)):
                table[lane[column, r + d], 128 + at] += w
    return table


def lanes(rows=1):
    return lax.broadcasted_iota(jnp.int32, (rows, 128), 1)


def split_into(ref, rows, x):
    upper = x.astype(BF16)
    ref[rows, 0:128] = upper
    ref[rows, 128:256] = (x - upper.astype(F32)).astype(BF16)


def joined(both):
    return both[:, 0:128] + both[:, 128:256]


def pack_kernel(spec, mask, current, out, mask_out, stack, turned, turned2):
    sea = mask[...].astype(F32)
    masked = spec[...] * sea[None]
    stack[0:16, :] = masked[8]
    stack[16:32, :] = sea
    stack[32:128, :] = jnp.zeros((96, NLON), F32)
    turned[...] = masked[0:8].reshape(128, NLON).T
    turned2[...] = stack[...].T

    pair = lax.broadcasted_iota(jnp.int32, (32, 128), 0) // 2
    means = jnp.where(pair == lax.broadcasted_iota(jnp.int32, (32, 128), 1) % 16, 0.25, 0.0)
    sums = jnp.dot(current[...], means, precision=HIGHEST, preferred_element_type=F32)
    group = lanes(OWNERS) // 16
    rest = jnp.zeros((OWNERS, 128), F32)
    sea_rows = jnp.zeros((OWNERS, 128), F32)
    for c in range(COLS):
        out[pl.ds(c, OWNERS, stride=4), :] = turned[pl.ds(c, OWNERS, stride=COLS), :]
        column = turned2[pl.ds(c, OWNERS, stride=COLS), :]
        zonal = sums[2 * c : 2 * c + 1] + sums[2 * c + 1 : 2 * c + 2]
        rest = jnp.where(group == 2 * c, pltpu.roll(column, 32 * c, 1), rest)
        rest = jnp.where(group == 2 * c + 1, jnp.broadcast_to(zonal, rest.shape), rest)
        sea_rows = jnp.where(group == c, pltpu.roll(column, (16 * c - 16) % 128, 1), sea_rows)
    out[pl.ds(3, OWNERS, stride=4), :] = rest
    mask_out[...] = sea_rows


def swapped(odd, first, second):
    return jnp.where(odd, second, first), jnp.where(odd, first, second)


def edges_kernel(device, band, arrived, rows_b, columns_b, columns_a, rows_a):
    def part(c):
        return arrived[pl.ds(c, OWNERS, stride=4), :]

    lane = lanes(OWNERS)
    group = lane // 16
    inside = lane % 16
    rest = part(3)

    odd = (device[0] & 1) == 1
    columns_a[0:128, :], columns_b[0:128, :] = swapped(odd, part(1), part(0))
    columns_a[128:256, :], columns_b[128:256, :] = swapped(odd, part(2), part(1))
    lasts = []
    for c in (1, 0):
        pair = jnp.where(
            group == 0, pltpu.roll(rest, (-32 * c) % 128, 1), pltpu.roll(rest, (16 - 32 * (c + 1)) % 128, 1)
        )
        last = jnp.zeros((32, 128), F32)
        for q in range(4):
            moved = pltpu.roll(pair[32 * q : 32 * q + 32], 32 * q, 1)
            last = jnp.where(group[0:32] // 2 == q, moved, last)
        lasts.append(last)
    columns_a[256:288, :], columns_b[256:288, :] = swapped(odd, *lasts)

    edges = []
    for r in (14, 0):
        acc = jnp.zeros((OWNERS, 128), F32)
        for c in range(COLS):
            moved = pltpu.roll(part(c), (2 * c - r) % 128, 1)
            acc = jnp.where((inside >= 2 * c) & (inside < 2 * c + 2), moved, acc)
        for c in range(COLS):
            moved = pltpu.roll(rest, (6 + 2 * c - 32 * c - r) % 128, 1)
            acc = jnp.where((lane >= 6 + 2 * c) & (lane < 8 + 2 * c), moved, acc)
        edges.append(acc)
    rows_a[...], rows_b[...] = swapped((band[0] & 1) == 1, *edges)


def columns_kernel(plus, minus, values, speeds, plus_col, minus_col):
    inner = lax.broadcasted_iota(jnp.int32, (128, 128), 0)
    for t in range(OWN):
        rows = slice(128 * t, 128 * t + 128)
        part = jnp.where(inner < 64, values[0:1, rows], values[1:2, rows])
        speeds[rows, :] = jnp.where(inner == 127, values[2:3, rows], part).T
        for row, col in ((plus, plus_col), (minus, minus_col)):
            column = jnp.broadcast_to(row[:, rows].astype(F32), (128, 128)).T
            col[rows, :] = column.astype(jnp.int32).astype(jnp.int16)


def points_kernel(
    me, band, arrived, rows_b, columns_b, columns_a, rows_a, sea_row, plus, minus, stencil, speeds, plus_col, minus_col,
    out, halves, first, source, middle,
):
    device = me[0]
    odd = (device & 1) == 1
    rows_below, rows_above = swapped((band[0] & 1) == 1, rows_b[...], rows_a[...])

    def from_west(rows):
        return jnp.where(odd, columns_a[rows, :], columns_b[rows, :])

    def from_east(rows):
        return jnp.where(odd, columns_b[rows, :], columns_a[rows, :])

    lane = lanes(OWNERS)
    group = lane // 16

    flow = arrived[pl.ds(4 * device + 3, 1), :]
    below = arrived[pl.ds(4 * jnp.maximum(device - 1, 0) + 3, 1), :]
    above = arrived[pl.ds(4 * jnp.minimum(device + 1, OWNERS - 1) + 3, 1), :]
    lower = jnp.where(device > 0, pltpu.roll(below, 48, 1), 0.0)
    upper = jnp.where(device < OWNERS - 1, pltpu.roll(above, 32, 1), 0.0)
    lane1 = lanes()
    group1 = lane1 // 16
    for c in range(COLS):
        lower = jnp.where(group1 == c + 1, pltpu.roll(flow, (-16 * c) % 128, 1), lower)
        upper = jnp.where(group1 == c, pltpu.roll(flow, (-16 * (c + 1)) % 128, 1), upper)
    faces = jnp.where(lane1 < 64, 0.5 * (lower + upper), 0.0)
    sea = sea_row[...]

    def chunk(t):
        return slice(128 * t, 128 * t + 128)

    for g in range(3):
        source[chunk(g), :] = arrived[pl.ds(g, OWNERS, stride=4), :]
    for g in range(3, 7):
        source[chunk(g), :] = from_west(chunk(g - 3)) if g < 5 else from_east(chunk(g - 5))
    source[chunk(7), :] = arrived[pl.ds(3, OWNERS, stride=4), :]
    for i in range(OWN):
        acc = jnp.zeros((OWNERS, 128), F32)
        for g in range(7):
            if i == 8:
                if g < 3:
                    part = pltpu.roll(source[chunk(7), :], (-16 * g) % 128, 1)
                else:
                    side, at = (from_west, 48) if g < 5 else (from_east, 80)
                    piece = side(slice(256, 288))
                    part = jnp.concatenate([pltpu.roll(piece, (at - 32 * q) % 128, 1) for q in range(4)], axis=0)
            else:
                part = pltpu.roll(source[chunk(g), :], (16 * g - 16 * i) % 128, 1)
            acc = jnp.where(group == g, part, acc)
        held = 16 * i if i < 8 else 6
        for beyond, at in ((rows_below, 112), (rows_above, 118)):
            acc = jnp.where((lane >= at) & (lane < at + 6), pltpu.roll(beyond, (at - held) % 128, 1), acc)
        middle[pl.ds(i, OWNERS, stride=OWN), :] = acc

    for t in range(OWN):
        value = middle[chunk(t), :]
        upper_half = value.astype(BF16)
        lower_half = (value - upper_half.astype(F32)).astype(BF16)
        sums = jnp.dot(upper_half, stencil[...], preferred_element_type=F32) + jnp.dot(
            lower_half, stencil[...], preferred_element_type=F32
        )
        speed = (speeds[chunk(t), :] + faces) * (1.0 / 6.0)
        flux = jnp.maximum(speed, 0.0) * sums[:, 0:128] + jnp.minimum(speed, 0.0) * sums[:, 128:256]
        change = (pltpu.roll(flux, 112, 1) - flux) + pltpu.roll(flux, 64, 1)
        moved = sea * (value - change)
        first[chunk(t), :] = moved
        split_into(halves, chunk(t), moved)

    numbers = lax.broadcasted_iota(jnp.int32, (128, BINS), 1).astype(jnp.int16)
    one, none = jnp.ones((128, BINS), BF16), jnp.zeros((128, BINS), BF16)

    def gathered(col, t):
        wide = jnp.concatenate([col[chunk(t), :]] * OWN, axis=1)
        chosen = jnp.where(wide == numbers, one, none)
        return joined(jnp.dot(chosen, halves[...], preferred_element_type=F32))

    for t in range(OWN):
        ahead = gathered(plus_col, t)
        behind = gathered(minus_col, t)
        f = first[chunk(t), :]
        strength = jnp.broadcast_to(speeds[chunk(t), 127:128], (128, 128))
        source[chunk(t), :] = strength * (f * f * (ahead + behind) - 2.0 * f * ahead * behind)
    for t in range(OWN):
        split_into(halves, chunk(t), source[chunk(t), :])
    plus_wide = jnp.broadcast_to(plus[...], (128, BINS)).astype(jnp.int16)
    minus_wide = jnp.broadcast_to(minus[...], (128, BINS)).astype(jnp.int16)
    for t in range(OWN):
        names = (lax.broadcasted_iota(jnp.int32, (128, BINS), 0) + 128 * t).astype(jnp.int16)
        hits = jnp.where(plus_wide == names, one, none) + jnp.where(minus_wide == names, one, none)
        back = joined(jnp.dot(hits, halves[...], preferred_element_type=F32))
        middle[chunk(t), :] = first[chunk(t), :] + (source[chunk(t), :] - 0.5 * back)
    for t in range(OWN):
        split_into(halves, chunk(t), middle[chunk(t), :])
    accs = [jnp.zeros((OWNERS, 128), F32)] * COLS
    for i in range(8):
        value = middle[pl.ds(i, OWNERS, stride=OWN), :]
        for c in range(COLS):
            accs[c] = jnp.where(group == i, pltpu.roll(value, (16 * (i - c)) % 128, 1), accs[c])
    for c in range(COLS):
        out[pl.ds(c, OWNERS, stride=4), :] = accs[c]
    acc = jnp.broadcast_to(flow, (OWNERS, 128))
    last = middle[pl.ds(8, OWNERS, stride=OWN), :]
    for c in range(COLS):
        acc = jnp.where(group == 2 * c, pltpu.roll(last, 16 * c, 1), acc)
    out[pl.ds(3, OWNERS, stride=4), :] = acc


def drift_kernel(me, halves, values, drift_out, drift_b, drift_a):
    level = lax.broadcasted_iota(jnp.int32, (LEV, BINS), 0).astype(F32) + 0.5
    decay = jnp.exp(level * values[3:4, :])
    table = jnp.concatenate([decay * values[4:5, :], decay * values[5:6, :]], axis=0)
    table_upper = table.astype(BF16)
    table_lower = (table - table_upper.astype(F32)).astype(BF16)
    drift = joined(jnp.dot(table_upper, halves[...], preferred_element_type=F32))
    drift = drift + jnp.dot(table_lower, halves[:, 0:128], preferred_element_type=F32)
    turned = drift.T[0:48]
    drift_out[...] = turned
    drift_a[...], drift_b[...] = swapped((me[0] & 1) == 1, turned[32:48], turned[0:16])


def unpack_kernel(
    device, band, arrived, drift, drift_b, drift_a, middle, zonal, near, rows_b, rows_a, low, high, turned, turned2
):
    rest = arrived[pl.ds(3, OWNERS, stride=4), :]
    for c in range(COLS):
        turned[pl.ds(c, OWNERS, stride=COLS), :] = arrived[pl.ds(c, OWNERS, stride=4), :]
        turned2[pl.ds(c, OWNERS, stride=COLS), :] = pltpu.roll(rest, (128 - 32 * c) % 128, 1)
    middle[0:128, :] = turned[...].T
    rest = turned2[...].T
    middle[128:144, :] = rest[0:16]
    zonal[...] = rest[16:32]
    for i in range(OWN):
        low[2 * i : 2 * i + 2, :] = middle[16 * i : 16 * i + 2, :]
        high[2 * i : 2 * i + 2, :] = middle[16 * i + 14 : 16 * i + 16, :]
    near[0:16, :], near[64:80, :] = swapped((device[0] & 1) == 1, drift_b[...], drift_a[...])
    near[16:64, :] = drift[...]
    for ref, r in ((low, 0), (high, 15)):
        pieces = [near[16 * k + r : 16 * k + r + 1, :] for k in range(5)] + [jnp.zeros((1, 128), F32)]
        ref[18:19, :] = jnp.concatenate(pieces[0:3], axis=1)
        ref[19:20, :] = jnp.concatenate(pieces[3:6], axis=1)
        ref[20:24, :] = jnp.zeros((4, NLON), F32)
    rows_a[...], rows_b[...] = swapped((band[0] & 1) == 1, high[...], low[...])


def inside_kernel(me, speeds, middle, zonal, mask, out, rows):
    first_bin = me[0] * OWN
    sea = mask[...].astype(F32)
    column = lax.broadcasted_iota(jnp.int32, (ROWS, NLON), 1)

    def beside(x, d):
        moved = pltpu.roll(x, (-d) % NLON, 1)
        return jnp.where((column + d >= 0) & (column + d < NLON), moved, 0.0)

    flow = zonal[...]
    lower_flow = 0.5 * (beside(flow, -1) + flow)
    upper_flow = 0.5 * (flow + beside(flow, 1))
    rows[0:8, :] = jnp.zeros((8, NLON), F32)
    rows[24:32, :] = jnp.zeros((8, NLON), F32)
    for i in range(OWN):
        f = middle[16 * i : 16 * i + 16, :]
        rows[8:24, :] = f
        along_x = speeds[first_bin + i]
        along_y = speeds[BINS + first_bin + i]
        r2, r1, u1, u2 = rows[6:22, :], rows[7:23, :], rows[9:25, :], rows[10:26, :]
        forward = jnp.maximum(along_y, 0.0) * (1.0 / 6.0)
        backward = jnp.minimum(along_y, 0.0) * (1.0 / 6.0)
        change = forward * ((r2 - 6.0 * r1) + (3.0 * f + 2.0 * u1)) + backward * (
            (6.0 * u1 - u2) - (2.0 * r1 + 3.0 * f)
        )
        a2, a1, b1, b2 = beside(f, -2), beside(f, -1), beside(f, 1), beside(f, 2)
        speed = (along_x + upper_flow) * (1.0 / 6.0)
        change = change + (
            jnp.maximum(speed, 0.0) * (5.0 * f + 2.0 * b1 - a1) + jnp.minimum(speed, 0.0) * (2.0 * f + 5.0 * b1 - b2)
        )
        speed = (along_x + lower_flow) * (1.0 / 6.0)
        change = change - (
            jnp.maximum(speed, 0.0) * (5.0 * a1 + 2.0 * f - a2) + jnp.minimum(speed, 0.0) * (2.0 * a1 + 5.0 * f - b1)
        )
        out[i] = sea * (f - change)


def final_kernel(me, band, speeds, inside, rows_b, rows_a, mask, drift, place, out, stokes, near, low, high):
    first_bin = me[0] * OWN
    sea = mask[...].astype(F32)
    low[...], high[...] = swapped((band[0] & 1) == 1, rows_b[...], rows_a[...])
    out[...] = inside[...]
    for i in range(OWN):
        along_y = speeds[BINS + first_bin + i]
        forward = jnp.maximum(along_y, 0.0) * (1.0 / 6.0)
        backward = jnp.minimum(along_y, 0.0) * (1.0 / 6.0)
        r2, r1 = low[2 * i : 2 * i + 1, :], low[2 * i + 1 : 2 * i + 2, :]
        u1, u2 = high[2 * i : 2 * i + 1, :], high[2 * i + 1 : 2 * i + 2, :]
        lower = jnp.concatenate([forward * (r2 - 6.0 * r1) - backward * (2.0 * r1), forward * r1], axis=0)
        upper = jnp.concatenate([-backward * u1, forward * (2.0 * u1) + backward * (6.0 * u1 - u2)], axis=0)
        out[i, 0:2, :] = inside[i, 0:2, :] - sea[0:2] * lower
        out[i, 14:16, :] = inside[i, 14:16, :] - sea[14:16] * upper

    near[0:80, :] = drift[...]
    near[80:128, :] = jnp.zeros((48, 128), F32)
    for ref, at in ((low, 80), (high, 88)):
        for k in range(5):
            near[at + k : at + k + 1, :] = ref[18 + k // 3 : 19 + k // 3, 128 * (k % 3) : 128 * (k % 3) + 128]
    wanted = jnp.broadcast_to(place[...], (128, 256)).T[0:192]
    chosen = jnp.where(wanted == lanes(192).astype(F32), 1.0, 0.0).astype(BF16)
    rest = near[...]
    total = jnp.zeros((192, 128), F32)
    for _ in range(3):
        part = rest.astype(BF16)
        rest = rest - part.astype(F32)
        total = total + jnp.dot(chosen, part, preferred_element_type=F32)
    stokes[0] = total[:, 0:64]
    stokes[1] = total[:, 64:128]


def shapes(*sizes):
    return [jax.ShapeDtypeStruct(size, F32) for size in sizes]


def on_device(spectrum, sea_mask, current, partner_plus, partner_minus, source_map):
    values = bin_values()
    speed_list = values[0:2].reshape(-1)
    held_values = np.concatenate([values, np.zeros((2, BINS), np.float32)])
    stencil = stencils().astype(BF16)

    device = lax.axis_index("bins").reshape(1)
    band = lax.axis_index("lat").reshape(1)

    def swap(x, axis, second):
        pairs = [(k, k + 1) for k in range(second, lax.axis_size(axis) - 1, 2)]
        return lax.ppermute(x, axis, pairs + [(j, i) for i, j in pairs])

    smem = pl.BlockSpec(memory_space=pltpu.SMEM)
    vmem = pl.BlockSpec(memory_space=pltpu.VMEM)
    grant = pltpu.CompilerParams(vmem_limit_bytes=16 * 1024 * 1024)
    sent, masks = pl.pallas_call(
        pack_kernel,
        out_shape=shapes((4 * OWNERS, 128), (OWNERS, 128)),
        scratch_shapes=[pltpu.VMEM((128, NLON), F32), pltpu.VMEM((NLON, 128), F32), pltpu.VMEM((NLON, 128), F32)],
        compiler_params=pltpu.CompilerParams(vmem_limit_bytes=60 * 1024 * 1024),
    )(spectrum, sea_mask, current)

    plus, minus, sent, masks = lax.optimization_barrier((partner_plus, partner_minus, sent, masks))
    arrived = lax.all_to_all(sent.reshape(OWNERS, 1, 512), "bins", 0, 0).reshape(4 * OWNERS, 128)
    plus, minus = plus.reshape(1, BINS), minus.reshape(1, BINS)
    sea = lax.dynamic_slice(masks, (device[0], 0), (1, 128))
    number = jax.ShapeDtypeStruct((BINS, 128), jnp.int16)
    columns = pl.pallas_call(
        columns_kernel,
        out_shape=shapes((BINS, 128)) + [number, number],
        compiler_params=grant,
    )(plus, minus, jnp.asarray(held_values))
    arrived, plus, minus, sea, *columns = lax.optimization_barrier((arrived, plus, minus, sea, *columns))
    rows_b, columns_b, columns_a, rows_a = pl.pallas_call(
        edges_kernel,
        out_shape=shapes((OWNERS, 128), (288, 128), (288, 128), (OWNERS, 128)),
        in_specs=[smem, smem, vmem],
        compiler_params=grant,
    )(device, band, arrived)
    rows_b = swap(rows_b, "lat", 1)
    columns_b = swap(columns_b, "bins", 1)
    columns_a = swap(columns_a, "bins", 0)
    rows_a = swap(rows_a, "lat", 0)

    big = pltpu.VMEM((BINS, 128), F32)
    sent, halves = pl.pallas_call(
        points_kernel,
        out_shape=[jax.ShapeDtypeStruct((4 * OWNERS, 128), F32), jax.ShapeDtypeStruct((BINS, 256), BF16)],
        in_specs=[smem, smem] + [vmem] * 12,
        scratch_shapes=[big, big, big],
        compiler_params=pltpu.CompilerParams(vmem_limit_bytes=24 * 1024 * 1024),
    )(
        device, band, arrived, rows_b, columns_b, columns_a, rows_a, sea, plus, minus,
        jnp.asarray(stencil), *columns,
    )

    arrived = lax.all_to_all(sent.reshape(OWNERS, 1, 512), "bins", 0, 0).reshape(4 * OWNERS, 128)
    drift, drift_b, drift_a = pl.pallas_call(
        drift_kernel,
        out_shape=shapes((48, 128), (16, 128), (16, 128)),
        in_specs=[smem, vmem, vmem],
        compiler_params=grant,
    )(device, halves, jnp.asarray(held_values))
    drift_b = swap(drift_b, "bins", 1)
    drift_a = swap(drift_a, "bins", 0)

    middle, zonal_all, near, rows_b, rows_a = pl.pallas_call(
        unpack_kernel,
        out_shape=shapes((OWN * ROWS, NLON), (ROWS, NLON), (80, 128), (24, NLON), (24, NLON)),
        in_specs=[smem, smem] + [vmem] * 4,
        scratch_shapes=[
            pltpu.VMEM((24, NLON), F32),
            pltpu.VMEM((24, NLON), F32),
            pltpu.VMEM((NLON, 128), F32),
            pltpu.VMEM((NLON, 128), F32),
        ],
        compiler_params=grant,
    )(device, band, arrived, drift, drift_b, drift_a)
    rows_b = swap(rows_b, "lat", 1)
    rows_a = swap(rows_a, "lat", 0)

    row = jnp.arange(32, dtype=jnp.int32)[None, :] // 2 + source_map // 3 - 1
    col = jnp.arange(6, dtype=jnp.int32)[:, None] // 2 + source_map % 3
    place = jnp.where(row < 0, 80 + col, jnp.where(row > 15, 88 + col, 16 * col + row))
    place = jnp.pad(place.reshape(1, 192), ((0, 0), (0, 64))).astype(F32)
    speed_refs = jnp.asarray(speed_list)
    inside = pl.pallas_call(
        inside_kernel,
        out_shape=jax.ShapeDtypeStruct((OWN, ROWS, NLON), F32),
        in_specs=[smem, smem] + [vmem] * 3,
        scratch_shapes=[pltpu.VMEM((32, NLON), F32)],
        compiler_params=grant,
        cost_estimate=pl.CostEstimate(flops=60 * OWN * ROWS * NLON, bytes_accessed=8 * OWN * ROWS * NLON, transcendentals=0),
    )(device, speed_refs, middle, zonal_all, sea_mask)
    second, stokes = pl.pallas_call(
        final_kernel,
        out_shape=shapes((OWN, ROWS, NLON), (2, 192, 64)),
        in_specs=[smem, smem, smem] + [vmem] * 6,
        scratch_shapes=[pltpu.VMEM((128, 128), F32), pltpu.VMEM((24, NLON), F32), pltpu.VMEM((24, NLON), F32)],
        compiler_params=grant,
    )(device, band, speed_refs, inside, rows_b, rows_a, sea_mask, near, place)
    return second, stokes.reshape(2, 6, 32, LEV).transpose(0, 3, 1, 2)


def solution(mesh):
    in_specs = (P("bins", "lat", None), P("lat", None), P("bins", "lat"), P(), P(), P("bins", "lat"))
    out_specs = (P("bins", "lat", None), P(None, None, "bins", "lat"))
    return jax.shard_map(on_device, mesh=mesh, in_specs=in_specs, out_specs=out_specs, check_vma=False)
```

```python
import math

import jax
import jax.numpy as jnp
import numpy as np
from jax import lax
from jax.experimental import pallas as pl
from jax.experimental.pallas import tpu as pltpu
from jax.sharding import PartitionSpec as P

NDIR = 36
NFREQ = 32
LEV = 64
BINS = NDIR * NFREQ
OWN = 9
ROWS = 16
NLON = 384
OWNERS = 128
BANDS = 4
COLS = 3
F32 = jnp.float32
BF16 = jnp.bfloat16
HIGHEST = lax.Precision.HIGHEST

GROUP_COLUMNS = (0, 1, 2, -2, -1, 3, 4)


def bin_values():
    j = np.arange(NFREQ, dtype=np.float64)
    angles = 2.0 * math.pi * (np.arange(NDIR) + 0.5) / NDIR
    speeds = np.repeat(0.12 + 0.25 * (NFREQ - 1 - j) / (NFREQ - 1), NDIR)
    cosines, sines = np.tile(np.cos(angles), NFREQ), np.tile(np.sin(angles), NFREQ)
    strength = np.repeat(0.06 * (1.0 + j / (NFREQ - 1)), NDIR)
    wavenumber = np.repeat(0.02 * 1.15**j, NDIR)
    amplitude = 2.0 / math.sqrt(BINS)
    rows = (speeds * cosines, speeds * sines, strength, -wavenumber, amplitude * cosines, amplitude * sines)
    return np.stack(rows).astype(np.float32)


def stencils():
    lane = {}
    for group, column in enumerate(GROUP_COLUMNS):
        for r in range(ROWS):
            lane[column, r] = 16 * group + r
    for column in range(COLS):
        for k in range(2):
            lane[column, k - 2] = 112 + 2 * column + k
            lane[column, 16 + k] = 118 + 2 * column + k
    table = np.zeros((128, 256), np.float32)
    for r in range(ROWS):
        for face in range(COLS + 1):
            at = 16 * face + r
            for d, w in ((-2, -1), (-1, 5), (0, 2)):
                table[lane[face + d, r], at] += w
            for d, w in ((-1, 2), (0, 5), (1, -1)):
                table[lane[face + d, r], 128 + at] += w
        for column in range(COLS):
            at = 64 + 16 * column + r
            for d, w in ((-2, 1), (-1, -6), (0, 3), (1, 2)):
                table[lane[column, r + d], at] += w
            for d, w in ((-1, -2), (0, -3), (1, 6), (2, -1)):
                table[lane[column, r + d], 128 + at] += w
    return table


def lanes(rows=1):
    return lax.broadcasted_iota(jnp.int32, (rows, 128), 1)


def split_into(ref, rows, x):
    upper = x.astype(BF16)
    ref[rows, 0:128] = upper
    ref[rows, 128:256] = (x - upper.astype(F32)).astype(BF16)


def joined(both):
    return both[:, 0:128] + both[:, 128:256]


def pack_kernel(spec, mask, current, out, mask_out, stack, turned, turned2):
    sea = mask[...].astype(F32)
    masked = spec[...] * sea[None]
    stack[0:16, :] = masked[8]
    stack[16:32, :] = sea
    stack[32:128, :] = jnp.zeros((96, NLON), F32)
    turned[...] = masked[0:8].reshape(128, NLON).T
    turned2[...] = stack[...].T

    pair = lax.broadcasted_iota(jnp.int32, (32, 128), 0) // 2
    means = jnp.where(pair == lax.broadcasted_iota(jnp.int32, (32, 128), 1) % 16, 0.25, 0.0)
    sums = jnp.dot(current[...], means, precision=HIGHEST, preferred_element_type=F32)
    group = lanes(OWNERS) // 16
    rest = jnp.zeros((OWNERS, 128), F32)
    sea_rows = jnp.zeros((OWNERS, 128), F32)
    for c in range(COLS):
        out[pl.ds(c, OWNERS, stride=4), :] = turned[pl.ds(c, OWNERS, stride=COLS), :]
        column = turned2[pl.ds(c, OWNERS, stride=COLS), :]
        zonal = sums[2 * c : 2 * c + 1] + sums[2 * c + 1 : 2 * c + 2]
        rest = jnp.where(group == 2 * c, pltpu.roll(column, 32 * c, 1), rest)
        rest = jnp.where(group == 2 * c + 1, jnp.broadcast_to(zonal, rest.shape), rest)
        sea_rows = jnp.where(group == c, pltpu.roll(column, (16 * c - 16) % 128, 1), sea_rows)
    out[pl.ds(3, OWNERS, stride=4), :] = rest
    mask_out[...] = sea_rows


def swapped(odd, first, second):
    return jnp.where(odd, second, first), jnp.where(odd, first, second)


def edges_kernel(device, band, arrived, rows_b, columns_b, columns_a, rows_a):
    def part(c):
        return arrived[pl.ds(c, OWNERS, stride=4), :]

    lane = lanes(OWNERS)
    group = lane // 16
    inside = lane % 16
    rest = part(3)

    odd = (device[0] & 1) == 1
    columns_a[0:128, :], columns_b[0:128, :] = swapped(odd, part(1), part(0))
    columns_a[128:256, :], columns_b[128:256, :] = swapped(odd, part(2), part(1))
    lasts = []
    for c in (1, 0):
        pair = jnp.where(
            group == 0, pltpu.roll(rest, (-32 * c) % 128, 1), pltpu.roll(rest, (16 - 32 * (c + 1)) % 128, 1)
        )
        last = jnp.zeros((32, 128), F32)
        for q in range(4):
            moved = pltpu.roll(pair[32 * q : 32 * q + 32], 32 * q, 1)
            last = jnp.where(group[0:32] // 2 == q, moved, last)
        lasts.append(last)
    columns_a[256:288, :], columns_b[256:288, :] = swapped(odd, *lasts)

    edges = []
    for r in (14, 0):
        acc = jnp.zeros((OWNERS, 128), F32)
        for c in range(COLS):
            moved = pltpu.roll(part(c), (2 * c - r) % 128, 1)
            acc = jnp.where((inside >= 2 * c) & (inside < 2 * c + 2), moved, acc)
        for c in range(COLS):
            moved = pltpu.roll(rest, (6 + 2 * c - 32 * c - r) % 128, 1)
            acc = jnp.where((lane >= 6 + 2 * c) & (lane < 8 + 2 * c), moved, acc)
        edges.append(acc)
    rows_a[...], rows_b[...] = swapped((band[0] & 1) == 1, *edges)


def columns_kernel(plus, minus, values, speeds, plus_col, minus_col):
    inner = lax.broadcasted_iota(jnp.int32, (128, 128), 0)
    for t in range(OWN):
        rows = slice(128 * t, 128 * t + 128)
        part = jnp.where(inner < 64, values[0:1, rows], values[1:2, rows])
        speeds[rows, :] = jnp.where(inner == 127, values[2:3, rows], part).T
        for row, col in ((plus, plus_col), (minus, minus_col)):
            column = jnp.broadcast_to(row[:, rows].astype(F32), (128, 128)).T
            col[rows, :] = column.astype(jnp.int32).astype(jnp.int16)


def points_kernel(
    me, band, arrived, rows_b, columns_b, columns_a, rows_a, sea_row, plus, minus, stencil, speeds, plus_col, minus_col,
    out, halves, first, source, middle,
):
    device = me[0]
    odd = (device & 1) == 1
    rows_below, rows_above = swapped((band[0] & 1) == 1, rows_b[...], rows_a[...])

    def from_west(rows):
        return jnp.where(odd, columns_a[rows, :], columns_b[rows, :])

    def from_east(rows):
        return jnp.where(odd, columns_b[rows, :], columns_a[rows, :])

    lane = lanes(OWNERS)
    group = lane // 16

    flow = arrived[pl.ds(4 * device + 3, 1), :]
    below = arrived[pl.ds(4 * jnp.maximum(device - 1, 0) + 3, 1), :]
    above = arrived[pl.ds(4 * jnp.minimum(device + 1, OWNERS - 1) + 3, 1), :]
    lower = jnp.where(device > 0, pltpu.roll(below, 48, 1), 0.0)
    upper = jnp.where(device < OWNERS - 1, pltpu.roll(above, 32, 1), 0.0)
    lane1 = lanes()
    group1 = lane1 // 16
    for c in range(COLS):
        lower = jnp.where(group1 == c + 1, pltpu.roll(flow, (-16 * c) % 128, 1), lower)
        upper = jnp.where(group1 == c, pltpu.roll(flow, (-16 * (c + 1)) % 128, 1), upper)
    faces = jnp.where(lane1 < 64, 0.5 * (lower + upper), 0.0)
    sea = sea_row[...]

    def chunk(t):
        return slice(128 * t, 128 * t + 128)

    for g in range(3):
        source[chunk(g), :] = arrived[pl.ds(g, OWNERS, stride=4), :]
    for g in range(3, 7):
        source[chunk(g), :] = from_west(chunk(g - 3)) if g < 5 else from_east(chunk(g - 5))
    source[chunk(7), :] = arrived[pl.ds(3, OWNERS, stride=4), :]
    for i in range(OWN):
        acc = jnp.zeros((OWNERS, 128), F32)
        for g in range(7):
            if i == 8:
                if g < 3:
                    part = pltpu.roll(source[chunk(7), :], (-16 * g) % 128, 1)
                else:
                    side, at = (from_west, 48) if g < 5 else (from_east, 80)
                    piece = side(slice(256, 288))
                    part = jnp.concatenate([pltpu.roll(piece, (at - 32 * q) % 128, 1) for q in range(4)], axis=0)
            else:
                part = pltpu.roll(source[chunk(g), :], (16 * g - 16 * i) % 128, 1)
            acc = jnp.where(group == g, part, acc)
        held = 16 * i if i < 8 else 6
        for beyond, at in ((rows_below, 112), (rows_above, 118)):
            acc = jnp.where((lane >= at) & (lane < at + 6), pltpu.roll(beyond, (at - held) % 128, 1), acc)
        middle[pl.ds(i, OWNERS, stride=OWN), :] = acc

    for t in range(OWN):
        value = middle[chunk(t), :]
        upper_half = value.astype(BF16)
        lower_half = (value - upper_half.astype(F32)).astype(BF16)
        sums = jnp.dot(upper_half, stencil[...], preferred_element_type=F32) + jnp.dot(
            lower_half, stencil[...], preferred_element_type=F32
        )
        speed = (speeds[chunk(t), :] + faces) * (1.0 / 6.0)
        flux = jnp.maximum(speed, 0.0) * sums[:, 0:128] + jnp.minimum(speed, 0.0) * sums[:, 128:256]
        change = (pltpu.roll(flux, 112, 1) - flux) + pltpu.roll(flux, 64, 1)
        moved = sea * (value - change)
        first[chunk(t), :] = moved
        split_into(halves, chunk(t), moved)

    numbers = lax.broadcasted_iota(jnp.int32, (128, BINS), 1).astype(jnp.int16)
    one, none = jnp.ones((128, BINS), BF16), jnp.zeros((128, BINS), BF16)

    def gathered(col, t):
        wide = jnp.concatenate([col[chunk(t), :]] * OWN, axis=1)
        chosen = jnp.where(wide == numbers, one, none)
        return joined(jnp.dot(chosen, halves[...], preferred_element_type=F32))

    for t in range(OWN):
        ahead = gathered(plus_col, t)
        behind = gathered(minus_col, t)
        f = first[chunk(t), :]
        strength = jnp.broadcast_to(speeds[chunk(t), 127:128], (128, 128))
        source[chunk(t), :] = strength * (f * f * (ahead + behind) - 2.0 * f * ahead * behind)
    for t in range(OWN):
        split_into(halves, chunk(t), source[chunk(t), :])
    plus_wide = jnp.broadcast_to(plus[...], (128, BINS)).astype(jnp.int16)
    minus_wide = jnp.broadcast_to(minus[...], (128, BINS)).astype(jnp.int16)
    for t in range(OWN):
        names = (lax.broadcasted_iota(jnp.int32, (128, BINS), 0) + 128 * t).astype(jnp.int16)
        hits = jnp.where(plus_wide == names, one, none) + jnp.where(minus_wide == names, one, none)
        back = joined(jnp.dot(hits, halves[...], preferred_element_type=F32))
        middle[chunk(t), :] = first[chunk(t), :] + (source[chunk(t), :] - 0.5 * back)
    for t in range(OWN):
        split_into(halves, chunk(t), middle[chunk(t), :])
    accs = [jnp.zeros((OWNERS, 128), F32)] * COLS
    for i in range(8):
        value = middle[pl.ds(i, OWNERS, stride=OWN), :]
        for c in range(COLS):
            accs[c] = jnp.where(group == i, pltpu.roll(value, (16 * (i - c)) % 128, 1), accs[c])
    for c in range(COLS):
        out[pl.ds(c, OWNERS, stride=4), :] = accs[c]
    acc = jnp.broadcast_to(flow, (OWNERS, 128))
    last = middle[pl.ds(8, OWNERS, stride=OWN), :]
    for c in range(COLS):
        acc = jnp.where(group == 2 * c, pltpu.roll(last, 16 * c, 1), acc)
    out[pl.ds(3, OWNERS, stride=4), :] = acc


def drift_kernel(me, halves, values, drift_out, drift_b, drift_a):
    level = lax.broadcasted_iota(jnp.int32, (LEV, BINS), 0).astype(F32) + 0.5
    decay = jnp.exp(level * values[3:4, :])
    table = jnp.concatenate([decay * values[4:5, :], decay * values[5:6, :]], axis=0)
    table_upper = table.astype(BF16)
    table_lower = (table - table_upper.astype(F32)).astype(BF16)
    drift = joined(jnp.dot(table_upper, halves[...], preferred_element_type=F32))
    drift = drift + jnp.dot(table_lower, halves[:, 0:128], preferred_element_type=F32)
    turned = drift.T[0:48]
    drift_out[...] = turned
    drift_a[...], drift_b[...] = swapped((me[0] & 1) == 1, turned[32:48], turned[0:16])


def unpack_kernel(
    device, band, arrived, drift, drift_b, drift_a, middle, zonal, near, rows_b, rows_a, low, high, turned, turned2
):
    rest = arrived[pl.ds(3, OWNERS, stride=4), :]
    for c in range(COLS):
        turned[pl.ds(c, OWNERS, stride=COLS), :] = arrived[pl.ds(c, OWNERS, stride=4), :]
        turned2[pl.ds(c, OWNERS, stride=COLS), :] = pltpu.roll(rest, (128 - 32 * c) % 128, 1)
    middle[0:128, :] = turned[...].T
    rest = turned2[...].T
    middle[128:144, :] = rest[0:16]
    zonal[...] = rest[16:32]
    for i in range(OWN):
        low[2 * i : 2 * i + 2, :] = middle[16 * i : 16 * i + 2, :]
        high[2 * i : 2 * i + 2, :] = middle[16 * i + 14 : 16 * i + 16, :]
    near[0:16, :], near[64:80, :] = swapped((device[0] & 1) == 1, drift_b[...], drift_a[...])
    near[16:64, :] = drift[...]
    for ref, r in ((low, 0), (high, 15)):
        pieces = [near[16 * k + r : 16 * k + r + 1, :] for k in range(5)] + [jnp.zeros((1, 128), F32)]
        ref[18:19, :] = jnp.concatenate(pieces[0:3], axis=1)
        ref[19:20, :] = jnp.concatenate(pieces[3:6], axis=1)
        ref[20:24, :] = jnp.zeros((4, NLON), F32)
    rows_a[...], rows_b[...] = swapped((band[0] & 1) == 1, high[...], low[...])


def final_kernel(
    me, band, speeds, middle, zonal, rows_b, rows_a, mask, drift, place, out, stokes, near, low, high, rows
):
    first_bin = me[0] * OWN
    sea = mask[...].astype(F32)
    column = lax.broadcasted_iota(jnp.int32, (ROWS, NLON), 1)

    def beside(x, d):
        moved = pltpu.roll(x, (-d) % NLON, 1)
        return jnp.where((column + d >= 0) & (column + d < NLON), moved, 0.0)

    flow = zonal[...]
    lower_flow = 0.5 * (beside(flow, -1) + flow)
    upper_flow = 0.5 * (flow + beside(flow, 1))
    low[...], high[...] = swapped((band[0] & 1) == 1, rows_b[...], rows_a[...])
    for i in range(OWN):
        f = middle[16 * i : 16 * i + 16, :]
        rows[8:24, :] = f
        rows[6:8, :] = low[2 * i : 2 * i + 2, :]
        rows[24:26, :] = high[2 * i : 2 * i + 2, :]
        along_x = speeds[first_bin + i]
        along_y = speeds[BINS + first_bin + i]
        r2, r1, u1, u2 = rows[6:22, :], rows[7:23, :], rows[9:25, :], rows[10:26, :]
        forward = jnp.maximum(along_y, 0.0) * (1.0 / 6.0)
        backward = jnp.minimum(along_y, 0.0) * (1.0 / 6.0)
        change = forward * ((r2 - 6.0 * r1) + (3.0 * f + 2.0 * u1)) + backward * (
            (6.0 * u1 - u2) - (2.0 * r1 + 3.0 * f)
        )
        a2, a1, b1, b2 = beside(f, -2), beside(f, -1), beside(f, 1), beside(f, 2)
        speed = (along_x + upper_flow) * (1.0 / 6.0)
        change = change + (
            jnp.maximum(speed, 0.0) * (5.0 * f + 2.0 * b1 - a1) + jnp.minimum(speed, 0.0) * (2.0 * f + 5.0 * b1 - b2)
        )
        speed = (along_x + lower_flow) * (1.0 / 6.0)
        change = change - (
            jnp.maximum(speed, 0.0) * (5.0 * a1 + 2.0 * f - a2) + jnp.minimum(speed, 0.0) * (2.0 * a1 + 5.0 * f - b1)
        )
        out[i] = sea * (f - change)

    near[0:80, :] = drift[...]
    near[80:128, :] = jnp.zeros((48, 128), F32)
    for ref, at in ((low, 80), (high, 88)):
        for k in range(5):
            near[at + k : at + k + 1, :] = ref[18 + k // 3 : 19 + k // 3, 128 * (k % 3) : 128 * (k % 3) + 128]
    wanted = jnp.broadcast_to(place[...], (128, 256)).T[0:192]
    chosen = jnp.where(wanted == lanes(192).astype(F32), 1.0, 0.0).astype(BF16)
    rest = near[...]
    total = jnp.zeros((192, 128), F32)
    for _ in range(3):
        part = rest.astype(BF16)
        rest = rest - part.astype(F32)
        total = total + jnp.dot(chosen, part, preferred_element_type=F32)
    stokes[0] = total[:, 0:64]
    stokes[1] = total[:, 64:128]


def shapes(*sizes):
    return [jax.ShapeDtypeStruct(size, F32) for size in sizes]


def on_device(spectrum, sea_mask, current, partner_plus, partner_minus, source_map):
    values = bin_values()
    speed_list = values[0:2].reshape(-1)
    held_values = np.concatenate([values, np.zeros((2, BINS), np.float32)])
    stencil = stencils().astype(BF16)

    device = lax.axis_index("bins").reshape(1)
    band = lax.axis_index("lat").reshape(1)

    def swap(x, axis, second):
        pairs = [(k, k + 1) for k in range(second, lax.axis_size(axis) - 1, 2)]
        return lax.ppermute(x, axis, pairs + [(j, i) for i, j in pairs])

    smem = pl.BlockSpec(memory_space=pltpu.SMEM)
    vmem = pl.BlockSpec(memory_space=pltpu.VMEM)
    grant = pltpu.CompilerParams(vmem_limit_bytes=16 * 1024 * 1024)
    sent, masks = pl.pallas_call(
        pack_kernel,
        out_shape=shapes((4 * OWNERS, 128), (OWNERS, 128)),
        scratch_shapes=[pltpu.VMEM((128, NLON), F32), pltpu.VMEM((NLON, 128), F32), pltpu.VMEM((NLON, 128), F32)],
        compiler_params=pltpu.CompilerParams(vmem_limit_bytes=60 * 1024 * 1024),
    )(spectrum, sea_mask, current)

    plus, minus, sent, masks = lax.optimization_barrier((partner_plus, partner_minus, sent, masks))
    arrived = lax.all_to_all(sent.reshape(OWNERS, 1, 512), "bins", 0, 0).reshape(4 * OWNERS, 128)
    plus, minus = plus.reshape(1, BINS), minus.reshape(1, BINS)
    sea = lax.dynamic_slice(masks, (device[0], 0), (1, 128))
    number = jax.ShapeDtypeStruct((BINS, 128), jnp.int16)
    columns = pl.pallas_call(
        columns_kernel,
        out_shape=shapes((BINS, 128)) + [number, number],
        compiler_params=grant,
    )(plus, minus, jnp.asarray(held_values))
    arrived, plus, minus, sea, *columns = lax.optimization_barrier((arrived, plus, minus, sea, *columns))
    rows_b, columns_b, columns_a, rows_a = pl.pallas_call(
        edges_kernel,
        out_shape=shapes((OWNERS, 128), (288, 128), (288, 128), (OWNERS, 128)),
        in_specs=[smem, smem, vmem],
        compiler_params=grant,
    )(device, band, arrived)
    rows_b = swap(rows_b, "lat", 1)
    columns_b = swap(columns_b, "bins", 1)
    columns_a = swap(columns_a, "bins", 0)
    rows_a = swap(rows_a, "lat", 0)

    big = pltpu.VMEM((BINS, 128), F32)
    sent, halves = pl.pallas_call(
        points_kernel,
        out_shape=[jax.ShapeDtypeStruct((4 * OWNERS, 128), F32), jax.ShapeDtypeStruct((BINS, 256), BF16)],
        in_specs=[smem, smem] + [vmem] * 12,
        scratch_shapes=[big, big, big],
        compiler_params=pltpu.CompilerParams(vmem_limit_bytes=24 * 1024 * 1024),
    )(
        device, band, arrived, rows_b, columns_b, columns_a, rows_a, sea, plus, minus,
        jnp.asarray(stencil), *columns,
    )

    arrived = lax.all_to_all(sent.reshape(OWNERS, 1, 512), "bins", 0, 0).reshape(4 * OWNERS, 128)
    drift, drift_b, drift_a = pl.pallas_call(
        drift_kernel,
        out_shape=shapes((48, 128), (16, 128), (16, 128)),
        in_specs=[smem, vmem, vmem],
        compiler_params=grant,
    )(device, halves, jnp.asarray(held_values))
    drift_b = swap(drift_b, "bins", 1)
    drift_a = swap(drift_a, "bins", 0)

    middle, zonal_all, near, rows_b, rows_a = pl.pallas_call(
        unpack_kernel,
        out_shape=shapes((OWN * ROWS, NLON), (ROWS, NLON), (80, 128), (24, NLON), (24, NLON)),
        in_specs=[smem, smem] + [vmem] * 4,
        scratch_shapes=[
            pltpu.VMEM((24, NLON), F32),
            pltpu.VMEM((24, NLON), F32),
            pltpu.VMEM((NLON, 128), F32),
            pltpu.VMEM((NLON, 128), F32),
        ],
        compiler_params=grant,
    )(device, band, arrived, drift, drift_b, drift_a)
    rows_b = swap(rows_b, "lat", 1)
    rows_a = swap(rows_a, "lat", 0)

    row = jnp.arange(32, dtype=jnp.int32)[None, :] // 2 + source_map // 3 - 1
    col = jnp.arange(6, dtype=jnp.int32)[:, None] // 2 + source_map % 3
    place = jnp.where(row < 0, 80 + col, jnp.where(row > 15, 88 + col, 16 * col + row))
    place = jnp.pad(place.reshape(1, 192), ((0, 0), (0, 64))).astype(F32)
    speed_refs = jnp.asarray(speed_list)
    second, stokes = pl.pallas_call(
        final_kernel,
        out_shape=shapes((OWN, ROWS, NLON), (2, 192, 64)),
        in_specs=[smem, smem, smem] + [vmem] * 7,
        scratch_shapes=[pltpu.VMEM((128, 128), F32)] + [pltpu.VMEM((24, NLON), F32)] * 2 + [pltpu.VMEM((32, NLON), F32)],
        compiler_params=grant,
    )(device, band, speed_refs, middle, zonal_all, rows_b, rows_a, sea_mask, near, place)
    return second, stokes.reshape(2, 6, 32, LEV).transpose(0, 3, 1, 2)


def solution(mesh):
    in_specs = (P("bins", "lat", None), P("lat", None), P("bins", "lat"), P(), P(), P("bins", "lat"))
    out_specs = (P("bins", "lat", None), P(None, None, "bins", "lat"))
    return jax.shard_map(on_device, mesh=mesh, in_specs=in_specs, out_specs=out_specs, check_vma=False)
```
